256 devices in a mesh: gs: 64 (over z, y, core), view: 4 (over x).
Axes of the slice: x: 4, y: 4, z: 8, core: 2. Of those that a mesh axis runs over, the one named last changes fastest.
Arguments:
- gaussians: float32 [59, 262144], P(None, 'gs'), may hold values from -6 to 1.5, as said below
- send_index: int32 [4, 4096, 128], P('view', 'gs'), may hold values from 0 to 4095
- tile_list: int32 [4, 512, 256], P('view', 'gs'), may hold values from 0 to 8191
- tile_length: int32 [4, 512], P('view', 'gs'), may hold values from 32 to 256, as said below
- camera: float32 [4, 5], P('view'), may hold values from -3.140625 to 3.140625
- exposure: float32 [4, 5], P('view'), may hold values from 0.25 to 4
- target: float32 [4, 15, 1024, 128], P('view', None, 'gs'), may hold values from 0 to 1
Outputs:
- param_grad: float32 [59, 262144], P(None, 'gs')
- radiance: float32 [4, 3, 1024, 128], P('view', None, 'gs')
The draws below stay inside these ranges and needn't reach their ends.
Inputs may be any that keep to these rules, and one draw needn't show every extreme that they name: `gaussians`: Rows: position within [-1, 1], log scales within [-1, 0.5], quaternion w within [0.5, 1.5] and x, y, z within [-0.5, 0.5], opacity logit within [-6, -2], degree-0 harmonic coefficients within [-1, 1], the others within [-0.2, 0.2]. `tile_length`: every renderer's first tile uses all 256 entries.
All inputs are finite; a program needn't handle non-finite values.
Results may differ from the reference program's by a relative error of at most 0.0003.
Values sent between devices are 32-bit elements; how exact they have to be, the bound alone decides.
A program may use at most 128 MiB of HBM per device.

```python
import math
import jax
import jax.numpy as jnp
import numpy as np
from jax import lax

FEAT = 59
BRACKETS = 5
TILE_SIDE = 16
K = 256
G_DEV = 4096
CAP = 128
TY = 1
TX = 8
TILES_DEV = 8
TILES = 512
SLOTS = 8192
GAUSS = 262144
IMG_ROWS = 1024
COLS = 128
N_GS = 64
N_VIEW = 4


def draw_gaussians(key, part):
    key = jax.random.fold_in(key, 11)
    lows = jnp.array([-1.0, -1.0, -1.0, -1.0, -1.0, -1.0, 0.5, -0.5, -0.5, -0.5, -6.0, -1.0, -1.0, -1.0] + [-0.2] * 45, dtype=jnp.float32)
    highs = jnp.array([1.0, 1.0, 1.0, 0.5, 0.5, 0.5, 1.5, 0.5, 0.5, 0.5, -2.0, 1.0, 1.0, 1.0] + [0.2] * 45, dtype=jnp.float32)
    unit = jax.random.uniform(key, (FEAT, GAUSS), jnp.float32)
    return lows[:, None] + (highs - lows)[:, None] * unit


def draw_tile_length(key, part):
    key = jax.random.fold_in(key, 23)
    lengths = jax.random.randint(key, (N_VIEW, TILES), K // 8, K + 1)
    leading = (jnp.arange(TILES, dtype=jnp.int32) % TILES_DEV == 0)[None, :]
    return jnp.where(leading, K, lengths).astype(jnp.int32)


def place_ends(values, own_key, low, largest):
    longest = values.shape.index(max(values.shape))
    spots = []
    for shift in (0, 1):
        where = [jax.random.randint(jax.random.fold_in(own_key, axis), (), 0, length) for axis, length in enumerate(values.shape)]
        where[longest] = (where[longest] + shift) % values.shape[longest]
        spots.append(tuple(where))
    return values.at[spots[0]].set(low).at[spots[1]].set(largest)


def shard_levels(stream_key, shape, split, low, top_value):
    def one(axis_at, shards_of):
        draws = jax.random.uniform(jax.random.fold_in(jax.random.fold_in(stream_key, 6), axis_at), (shards_of,), jnp.float32, low / len(split), top_value / len(split))
        return jnp.repeat(jnp.exp(draws), shape[axis_at] // shards_of).reshape((-1,) + (1,) * (len(shape) - axis_at - 1))

    loudness = one(*split[0])
    for cut in split[1:]:
        loudness = loudness * one(*cut)
    return loudness


def setup_inputs(seed: int = 0) -> dict:
    arg_keys = jax.random.split(jax.random.key(seed), 8)
    return {
        "gaussians": draw_gaussians(jax.random.fold_in(arg_keys[7], 71), 0),
        "send_index": place_ends(jax.random.randint(arg_keys[1], (N_VIEW, N_GS * N_GS, CAP), 0, G_DEV), jax.random.fold_in(arg_keys[1], 1), 0, G_DEV - 1).astype(jnp.int32),
        "tile_list": place_ends(jax.random.randint(arg_keys[2], (N_VIEW, TILES, K), 0, SLOTS), jax.random.fold_in(arg_keys[2], 1), 0, SLOTS - 1).astype(jnp.int32),
        "tile_length": draw_tile_length(jax.random.fold_in(arg_keys[7], 71), 0),
        "camera": jnp.clip(jax.random.uniform(arg_keys[4], (N_VIEW, 5), jnp.float32, -3.140625, 3.140625), -3.140625, 3.140625),
        "exposure": jnp.clip(jnp.exp(math.log(4.0) - 2.7725887 * jax.random.uniform(arg_keys[5], (N_VIEW, BRACKETS), jnp.float32) ** shard_levels(arg_keys[5], (N_VIEW, BRACKETS), ((0, 4),), -0.2, 0.2)), 0.25, 4.0),
        "target": jnp.clip(1.0 * jax.random.uniform(arg_keys[6], (N_VIEW, 3 * BRACKETS, IMG_ROWS, COLS), jnp.float32) ** shard_levels(arg_keys[6], (N_VIEW, 3 * BRACKETS, IMG_ROWS, COLS), ((0, 4), (2, 64)), -0.2, 0.2), 0.0, 1.0),
    }


FOCAL = 16.0
DILATE = 0.3
SH_C0 = 0.28209479177387814
SH_C1 = 0.4886025119029199
SH_C2 = [1.0925484305920792, -1.0925484305920792, 0.31539156525252005, -1.0925484305920792, 0.5462742152960396]
SH_C3 = [-0.5900435899266435, 2.890611442640554, -0.4570457994644658, 0.3731763325901154, -0.4570457994644658, 1.445305721320277, -0.5900435899266435]
WINDOW_RAW = np.exp(-(np.arange(11) - 5.0) ** 2 / 4.5)
WINDOW = [float(v) for v in WINDOW_RAW / WINDOW_RAW.sum()]
FLOOR_MEAN = 0.0001
FLOOR_VAR = 0.0009

def product3(left, right):
    return [[sum((left[i][k] * right[k][j] for k in range(3))) for j in range(3)] for i in range(3)]

def camera_rotation(camera):
    yaw_cos, yaw_sin = (jnp.cos(camera[0]), jnp.sin(camera[0]))
    pitch_cos, pitch_sin = (jnp.cos(camera[1]), jnp.sin(camera[1]))
    roll_cos, roll_sin = (jnp.cos(camera[2]), jnp.sin(camera[2]))
    about_z = [[yaw_cos, -yaw_sin, 0.0], [yaw_sin, yaw_cos, 0.0], [0.0, 0.0, 1.0]]
    about_y = [[pitch_cos, 0.0, pitch_sin], [0.0, 1.0, 0.0], [-pitch_sin, 0.0, pitch_cos]]
    about_x = [[1.0, 0.0, 0.0], [0.0, roll_cos, -roll_sin], [0.0, roll_sin, roll_cos]]
    return product3(product3(about_z, about_y), about_x)

def quaternion_matrix(q0, q1, q2, q3):
    q_norm = jnp.sqrt(q0 * q0 + q1 * q1 + q2 * q2 + q3 * q3)
    w, x, y, z = (q0 / q_norm, q1 / q_norm, q2 / q_norm, q3 / q_norm)
    return [[1 - 2 * (y * y + z * z), 2 * (x * y - w * z), 2 * (x * z + w * y)], [2 * (x * y + w * z), 1 - 2 * (x * x + z * z), 2 * (y * z - w * x)], [2 * (x * z - w * y), 2 * (y * z + w * x), 1 - 2 * (x * x + y * y)]]

def harmonics(x, y, z):
    xx, yy, zz = (x * x, y * y, z * z)
    return [SH_C0 + 0.0 * x, -SH_C1 * y, SH_C1 * z, -SH_C1 * x, SH_C2[0] * x * y, SH_C2[1] * y * z, SH_C2[2] * (2 * zz - xx - yy), SH_C2[3] * x * z, SH_C2[4] * (xx - yy), SH_C3[0] * y * (3 * xx - yy), SH_C3[1] * x * y * z, SH_C3[2] * y * (4 * zz - xx - yy), SH_C3[3] * z * (2 * zz - 3 * xx - 3 * yy), SH_C3[4] * x * (4 * zz - xx - yy), SH_C3[5] * z * (xx - yy), SH_C3[6] * x * (xx - 3 * yy)]

def project(params, camera):
    rotation = camera_rotation(camera)
    translation = [0.15 * camera[3], 0.15 * camera[4], 6.0]
    position = [params[i] for i in range(3)]
    viewed = [sum((rotation[i][j] * position[j] for j in range(3))) + translation[i] for i in range(3)]
    inverse_z = 1.0 / viewed[2]
    row_x = [FOCAL * inverse_z * (rotation[0][k] - viewed[0] * inverse_z * rotation[2][k]) for k in range(3)]
    row_y = [FOCAL * inverse_z * (rotation[1][k] - viewed[1] * inverse_z * rotation[2][k]) for k in range(3)]
    orient = quaternion_matrix(params[6], params[7], params[8], params[9])
    stretch = [jnp.exp(params[3 + k]) for k in range(3)]
    image_x = [sum((row_x[i] * orient[i][k] for i in range(3))) * stretch[k] for k in range(3)]
    image_y = [sum((row_y[i] * orient[i][k] for i in range(3))) * stretch[k] for k in range(3)]
    cov_xx = sum((e * e for e in image_x)) + DILATE
    cov_yy = sum((e * e for e in image_y)) + DILATE
    cov_xy = sum((image_x[k] * image_y[k] for k in range(3)))
    determinant = cov_xx * cov_yy - cov_xy * cov_xy
    offset_x = FOCAL * viewed[0] * inverse_z
    offset_y = FOCAL * viewed[1] * inverse_z
    opacity = jax.nn.sigmoid(params[10])
    toward = [position[k] + sum((rotation[i][k] * translation[i] for i in range(3))) for k in range(3)]
    distance = jnp.sqrt(sum((e * e for e in toward)))
    harmonic = harmonics(toward[0] / distance, toward[1] / distance, toward[2] / distance)
    colour = [jnp.exp(sum((harmonic[l] * params[11 + 3 * l + c] for l in range(16)))) for c in range(3)]
    return jnp.stack([offset_x, offset_y, cov_yy / determinant, -cov_xy / determinant, cov_xx / determinant, opacity] + colour)

def render_tiles(splats, lengths):
    list_size = splats.shape[2]
    places = jnp.arange(TILE_SIDE * TILE_SIDE, dtype=jnp.int32)
    pixel_x = (places % TILE_SIDE).astype(jnp.float32) + 0.5 - 0.5 * TILE_SIDE
    pixel_y = (places // TILE_SIDE).astype(jnp.float32) + 0.5 - 0.5 * TILE_SIDE
    delta_x = pixel_x[None, None, :] - splats[0][:, :, None]
    delta_y = pixel_y[None, None, :] - splats[1][:, :, None]
    exponent = splats[2][:, :, None] * delta_x * delta_x + 2.0 * splats[3][:, :, None] * delta_x * delta_y + splats[4][:, :, None] * delta_y * delta_y
    list_order = jnp.arange(list_size, dtype=jnp.int32)
    active = (list_order[None, :] < lengths[:, None]).astype(jnp.float32)
    coverage = (splats[5] * active)[:, :, None] * jnp.exp(-0.5 * exponent)
    log_keep = jnp.log(1.0 - coverage)
    earlier = (list_order[:, None] > list_order[None, :]).astype(jnp.float32)
    before = jnp.einsum('kj,tjp->tkp', earlier, log_keep, precision=lax.Precision.HIGHEST)
    weight = coverage * jnp.exp(before)
    return jnp.einsum('ctk,tkp->tcp', splats[6:9], weight, precision=lax.Precision.HIGHEST)

def tiles_to_strip(tile_radiance):
    shaped = tile_radiance.reshape(TY, TX, 3, TILE_SIDE, TILE_SIDE)
    return jnp.transpose(shaped, (2, 0, 3, 1, 4)).reshape(3, TY * TILE_SIDE, TX * TILE_SIDE)

def tone_map(radiance_img, exposure):
    scaled = radiance_img[None] * exposure[:, None, None, None]
    mapped = scaled / (1.0 + scaled)
    return mapped.reshape(3 * exposure.shape[0], radiance_img.shape[1], radiance_img.shape[2])

def blur(values_in):
    row_count = values_in.shape[-2] - 10
    col_count = values_in.shape[-1]
    blurred = sum((WINDOW[i] * values_in[..., i:i + row_count, :] for i in range(11)))
    widened = jnp.pad(blurred, [(0, 0)] * (blurred.ndim - 1) + [(5, 5)])
    return sum((WINDOW[i] * widened[..., i:i + col_count] for i in range(11)))

def similarity(pred_pad, target_pad):
    mean_p = blur(pred_pad)
    mean_t = blur(target_pad)
    var_p = blur(pred_pad * pred_pad) - mean_p * mean_p
    var_t = blur(target_pad * target_pad) - mean_t * mean_t
    cov_pt = blur(pred_pad * target_pad) - mean_p * mean_t
    upper_part = (2.0 * mean_p * mean_t + FLOOR_MEAN) * (2.0 * cov_pt + FLOOR_VAR)
    lower_part = (mean_p * mean_p + mean_t * mean_t + FLOOR_MEAN) * (var_p + var_t + FLOOR_VAR)
    return upper_part / lower_part

def reference(gaussians, send_index, tile_list, tile_length, camera, exposure, target):
    peer_count = N_GS

    def total_loss(params):
        summed = jnp.zeros((), jnp.float32)
        images = []
        for v in range(N_VIEW):
            splats_all = project(params, camera[v])
            slot_table = send_index[v].reshape(peer_count, peer_count, CAP)
            owner_base = (jnp.arange(peer_count, dtype=jnp.int32) * G_DEV)[:, None, None]
            slot_ids = jnp.transpose(slot_table + owner_base, (1, 0, 2)).reshape(peer_count, peer_count * CAP)
            tile_ids = tile_list[v].reshape(peer_count, TILES_DEV, K)
            tile_lens = tile_length[v].reshape(peer_count, TILES_DEV)

            def strip_of(pieces):
                id_row, id_list, lens_row = pieces
                chosen = id_row[id_list]
                return tiles_to_strip(render_tiles(splats_all[:, chosen], lens_row))
            strips = lax.map(jax.checkpoint(strip_of), (slot_ids, tile_ids, tile_lens))
            full_image = jnp.transpose(strips, (1, 0, 2, 3)).reshape(3, IMG_ROWS, COLS)
            low_range = tone_map(full_image, exposure[v])
            pred_pad = jnp.pad(low_range, ((0, 0), (5, 5), (0, 0)))
            target_pad = jnp.pad(target[v], ((0, 0), (5, 5), (0, 0)))
            similar = similarity(pred_pad, target_pad)
            summed = summed + 0.8 * jnp.sum((low_range - target[v]) ** 2) + jnp.sum(1.0 - similar)
            images.append(full_image)
        return (summed, jnp.stack(images))
    param_grad, radiance = jax.grad(total_loss, has_aux=True)(gaussians)
    return (param_grad, radiance)
```

```python
import functools

import jax
import jax.numpy as jnp
import numpy as np
from jax import lax
from jax.experimental import pallas as pl
from jax.experimental.pallas import tpu as pltpu
from jax.sharding import PartitionSpec as P

MESH = pl.DeviceIdType.MESH
F32, BF16, I32 = jnp.float32, jnp.bfloat16, jnp.int32

FOCAL = 16.0
DILATE = 0.3
SH_C0 = 0.28209479177387814
SH_C1 = 0.4886025119029199
SH_C2 = [
    1.0925484305920792,
    -1.0925484305920792,
    0.31539156525252005,
    -1.0925484305920792,
    0.5462742152960396,
]
SH_C3 = [
    -0.5900435899266435,
    2.890611442640554,
    -0.4570457994644658,
    0.3731763325901154,
    -0.4570457994644658,
    1.445305721320277,
    -0.5900435899266435,
]
WINDOW_RAW = np.exp(-((np.arange(11) - 5.0) ** 2) / 4.5)
WINDOW = [float(v) for v in WINDOW_RAW / WINDOW_RAW.sum()]
FLOOR_MEAN = 0.0001
FLOOR_VAR = 0.0009

FEAT = 59
SPLAT = 9
HIGH = 32
TILES = 8
LIST = 256
ROWS = 16
COLS = 128
CHANNELS = 15
FIRST = 11
MAPS = 26


def product3(left, right):
    return [[sum((left[i][k] * right[k][j] for k in range(3))) for j in range(3)] for i in range(3)]


def camera_rotation(camera):
    yaw_cos, yaw_sin = (jnp.cos(camera[0]), jnp.sin(camera[0]))
    pitch_cos, pitch_sin = (jnp.cos(camera[1]), jnp.sin(camera[1]))
    roll_cos, roll_sin = (jnp.cos(camera[2]), jnp.sin(camera[2]))
    about_z = [[yaw_cos, -yaw_sin, 0.0], [yaw_sin, yaw_cos, 0.0], [0.0, 0.0, 1.0]]
    about_y = [[pitch_cos, 0.0, pitch_sin], [0.0, 1.0, 0.0], [-pitch_sin, 0.0, pitch_cos]]
    about_x = [[1.0, 0.0, 0.0], [0.0, roll_cos, -roll_sin], [0.0, roll_sin, roll_cos]]
    return product3(product3(about_z, about_y), about_x)


def quaternion_matrix(q0, q1, q2, q3):
    scale = 1.0 / jnp.sqrt(q0 * q0 + q1 * q1 + q2 * q2 + q3 * q3)
    w, x, y, z = (q0 * scale, q1 * scale, q2 * scale, q3 * scale)
    return [
        [1 - 2 * (y * y + z * z), 2 * (x * y - w * z), 2 * (x * z + w * y)],
        [2 * (x * y + w * z), 1 - 2 * (x * x + z * z), 2 * (y * z - w * x)],
        [2 * (x * z - w * y), 2 * (y * z + w * x), 1 - 2 * (x * x + y * y)],
    ]


def harmonics(x, y, z):
    xx, yy, zz = (x * x, y * y, z * z)
    return [
        SH_C0 + 0.0 * x,
        -SH_C1 * y,
        SH_C1 * z,
        -SH_C1 * x,
        SH_C2[0] * x * y,
        SH_C2[1] * y * z,
        SH_C2[2] * (2 * zz - xx - yy),
        SH_C2[3] * x * z,
        SH_C2[4] * (xx - yy),
        SH_C3[0] * y * (3 * xx - yy),
        SH_C3[1] * x * y * z,
        SH_C3[2] * y * (4 * zz - xx - yy),
        SH_C3[3] * z * (2 * zz - 3 * xx - 3 * yy),
        SH_C3[4] * x * (4 * zz - xx - yy),
        SH_C3[5] * z * (xx - yy),
        SH_C3[6] * x * (xx - 3 * yy),
    ]


def project(params, camera, rotation):
    translation = [0.15 * camera[3], 0.15 * camera[4], 6.0]
    position = [params[i] for i in range(3)]
    viewed = [
        sum((rotation[i][j] * position[j] for j in range(3))) + translation[i] for i in range(3)
    ]
    inverse_z = 1.0 / viewed[2]
    row_x = [
        FOCAL * inverse_z * (rotation[0][k] - viewed[0] * inverse_z * rotation[2][k])
        for k in range(3)
    ]
    row_y = [
        FOCAL * inverse_z * (rotation[1][k] - viewed[1] * inverse_z * rotation[2][k])
        for k in range(3)
    ]
    orient = quaternion_matrix(params[6], params[7], params[8], params[9])
    stretch = [jnp.exp(params[3 + k]) for k in range(3)]
    image_x = [sum((row_x[i] * orient[i][k] for i in range(3))) * stretch[k] for k in range(3)]
    image_y = [sum((row_y[i] * orient[i][k] for i in range(3))) * stretch[k] for k in range(3)]
    cov_xx = sum((e * e for e in image_x)) + DILATE
    cov_yy = sum((e * e for e in image_y)) + DILATE
    cov_xy = sum((image_x[k] * image_y[k] for k in range(3)))
    share = 1.0 / (cov_xx * cov_yy - cov_xy * cov_xy)
    opacity = 1.0 / (1.0 + jnp.exp(-params[10]))
    toward = [
        position[k] + sum((rotation[i][k] * translation[i] for i in range(3))) for k in range(3)
    ]
    closeness = 1.0 / jnp.sqrt(sum((e * e for e in toward)))
    harmonic = harmonics(*[e * closeness for e in toward])
    colour = [
        jnp.exp(sum((harmonic[l] * params[11 + 3 * l + c] for l in range(16)))) for c in range(3)
    ]
    return [
        FOCAL * viewed[0] * inverse_z,
        FOCAL * viewed[1] * inverse_z,
        cov_yy * share,
        -cov_xy * share,
        cov_xx * share,
        opacity,
    ] + colour


def iota(shape, axis):
    return lax.broadcasted_iota(I32, shape, axis)


def lane_gather(values, index):
    return jnp.take_along_axis(values, index, axis=1, mode="promise_in_bounds")


def parts(values):
    top = values.astype(BF16)
    return top, (values - top.astype(F32)).astype(BF16)


def dot(left, right):
    return jnp.dot(left, right, preferred_element_type=F32)


def dot_nt(left, right):
    return lax.dot_general(left, right, (((1,), (1,)), ((), ())), preferred_element_type=F32)


def spread_rows(gauss_ref, wide_ref):
    def one(h, carry):
        lanes = pl.ds(pl.multiple_of(h * COLS, COLS), COLS)
        for first in range(0, FEAT, 8):
            count = min(8, FEAT - first)
            wide_ref[pl.ds(first * HIGH + h, count, stride=HIGH), :] = gauss_ref[first : first + count, lanes]
        return carry

    lax.fori_loop(0, HIGH, one, 0)


def window_columns():
    column = iota((1, COLS), 1)
    taps = []
    for i in range(11):
        source = column + (i - 5)
        taps.append(jnp.where((source >= 0) & (source < COLS), WINDOW[i], 0.0))
    return taps


def along_columns(values, taps):
    total = values * taps[5]
    for i in range(11):
        if i != 5:
            total = total + taps[i] * pltpu.roll(values, (5 - i) % COLS, axis=1)
    return total


def along_rows(ref, row):
    def at(i):
        return ref[pl.ds(pl.multiple_of((row + i) * 16, 16), 16), :]

    total = WINDOW[5] * at(0)
    for i in range(1, 6):
        total = total + WINDOW[5 + i] * (at(i) + at(-i))
    return total


def step_kernel(
    n,
    nv,
    gauss_ref,
    send_ref,
    list_ref,
    len_ref,
    cam_ref,
    expo_ref,
    target_ref,
    gall_ref,
    rad_ref,
    wide_ref,
    table_ref,
    pick_ref,
    out_ref,
    recv_ref,
    splat_ref,
    cover_ref,
    weight_ref,
    top_ref,
    low_ref,
    pair_ref,
    deriv_ref,
    tile_rad_ref,
    strips_ref,
    edge_ref,
    t_ref,
    tt_ref,
    p_ref,
    pp_ref,
    pt_ref,
    mt_ref,
    btt_ref,
    gm_ref,
    gpp_ref,
    gpt_ref,
    gimg_ref,
    gtile_ref,
    sgrad_ref,
    slot_one_ref,
    slot_mask_ref,
    own_one_ref,
    own_mask_ref,
    slot_left_ref,
    slot_sum_ref,
    back_ref,
    ret_ref,
    own_left_ref,
    own_sum_ref,
    gown_ref,
    f_send,
    f_recv,
    b_send,
    b_recv,
    t_send,
    t_recv,
    h_send,
    h_recv,
    v_send,
    v_recv,
):
    me = lax.axis_index("gs")
    mv = lax.axis_index("view")
    after = lax.rem(me + 1, n)
    before = lax.rem(me + n - 1, n)
    group = min(8, n)
    groups = n // group
    halves = slot_mask_ref.shape[0]

    barrier = pltpu.get_barrier_semaphore()

    def greet(i, carry):
        pl.semaphore_signal(
            barrier, inc=1, device_id={"gs": lax.rem(me + i, n)}, device_id_type=MESH
        )
        return carry

    lax.fori_loop(1, n, greet, 0)
    for i in range(1, nv):
        pl.semaphore_signal(
            barrier, inc=1, device_id={"view": lax.rem(mv + i, nv)}, device_id_type=MESH
        )

    spread_rows(gauss_ref, wide_ref)
    camera = [jnp.full((8, COLS), cam_ref[0, i], F32) for i in range(5)]
    rotation = camera_rotation(camera)

    def project_rows(i, carry):
        rows = [
            wide_ref[pl.ds(pl.multiple_of(f * HIGH + i * 8, 8), 8), :] for f in range(FEAT)
        ]
        for f, value in enumerate(project(rows, camera, rotation)):
            table_ref[pl.ds(pl.multiple_of(f * HIGH + i * 8, 8), 8), :] = value
        return carry

    lax.fori_loop(0, HIGH // 8, project_rows, 0)
    for i in range(5):
        gown_ref[SPLAT * HIGH + i : SPLAT * HIGH + i + 1, :] = camera[i][0:1]
    gown_ref[SPLAT * HIGH + 5 : SPLAT * HIGH + 8, :] = jnp.zeros((3, COLS), F32)

    pl.semaphore_wait(barrier, n - 1 + nv - 1)

    def target_copy(peer, side):
        return pltpu.make_async_remote_copy(
            src_ref=target_ref.at[0],
            dst_ref=edge_ref.at[side],
            send_sem=t_send.at[side],
            recv_sem=t_recv.at[side],
            device_id={"gs": peer},
            device_id_type=MESH,
        )

    def strip_copy(peer, side):
        return pltpu.make_async_remote_copy(
            src_ref=strips_ref.at[1],
            dst_ref=strips_ref.at[2 * side],
            send_sem=h_send.at[side],
            recv_sem=h_recv.at[side],
            device_id={"gs": peer},
            device_id_type=MESH,
        )

    @pl.when(me < n - 1)
    def _():
        target_copy(after, 0).start()

    @pl.when(me > 0)
    def _():
        target_copy(before, 1).start()

    def forward_copy(peer, slot):
        return pltpu.make_async_remote_copy(
            src_ref=out_ref.at[peer],
            dst_ref=recv_ref.at[slot],
            send_sem=f_send.at[peer],
            recv_sem=f_recv.at[slot],
            device_id={"gs": peer},
            device_id_type=MESH,
        )

    def back_copy(peer, slot):
        return pltpu.make_async_remote_copy(
            src_ref=back_ref.at[peer],
            dst_ref=ret_ref.at[slot],
            send_sem=b_send.at[peer],
            recv_sem=b_recv.at[slot],
            device_id={"gs": peer},
            device_id_type=MESH,
        )

    my_group = me // group

    def gather_group(step, carry):
        block = lax.rem(my_group + step, groups)
        index = send_ref[0, pl.ds(pl.multiple_of(block * group, group), group), :]
        high = index >> 7
        low = index & 127

        def one(h, totals):
            chosen = high == h
            new = []
            for f in range(SPLAT):
                row = jnp.broadcast_to(table_ref[pl.ds(f * HIGH + h, 1), :], (group, COLS))
                new.append(jnp.where(chosen, lane_gather(row, low), totals[f]))
            return tuple(new)

        totals = lax.fori_loop(
            0, HIGH, one, tuple(jnp.zeros((group, COLS), F32) for _ in range(SPLAT)), unroll=4
        )
        for f in range(SPLAT):
            pick_ref[f * group : (f + 1) * group, :] = totals[f]
        for i in range(group):
            peer = block * group + i
            out_ref[peer] = pick_ref[pl.ds(i, SPLAT, stride=group), :]
        for i in range(group):
            peer = block * group + lax.rem(me + i, group)

            @pl.when(peer != me)
            def _():
                forward_copy(peer, me).start()

        return carry

    lax.fori_loop(0, groups, gather_group, 0)
    recv_ref[me] = out_ref[me]

    def own_factors(r, carry):
        index = send_ref[0, pl.ds(r, 1), :]
        lanes = pl.ds(pl.multiple_of(r * COLS, COLS), COLS)
        own_one_ref[:, lanes] = jnp.where(iota((256, COLS), 0) == (index & 255), 1.0, 0.0).astype(BF16)
        own_mask_ref[:, lanes] = jnp.where(iota((16, COLS), 0) == (index >> 8), 1.0, 0.0).astype(BF16)
        return carry

    lax.fori_loop(0, n, own_factors, 0)

    def slot_factors(j, carry):
        index = list_ref[0, pl.ds(j, 1), :]
        lanes = pl.ds(pl.multiple_of(j * LIST, LIST), LIST)
        slot_one_ref[:, lanes] = jnp.where(iota((256, LIST), 0) == (index & 255), 1.0, 0.0).astype(BF16)
        slot_mask_ref[:, lanes] = jnp.where(iota((halves, LIST), 0) == (index >> 8), 1.0, 0.0).astype(
            BF16
        )
        return carry

    lax.fori_loop(0, TILES, slot_factors, 0)

    @pl.when(me == 0)
    def _():
        edge_ref[0] = jnp.zeros((CHANNELS, ROWS, COLS), F32)
        strips_ref[0] = jnp.zeros((3, ROWS, COLS), F32)

    @pl.when(me == n - 1)
    def _():
        edge_ref[1] = jnp.zeros((CHANNELS, ROWS, COLS), F32)
        strips_ref[2] = jnp.zeros((3, ROWS, COLS), F32)

    @pl.when(me > 0)
    def _():
        target_copy(before, 0).wait_recv()

    @pl.when(me < n - 1)
    def _():
        target_copy(after, 1).wait_recv()

    for strip in range(3):
        for ch in range(16):
            if ch == CHANNELS:
                value = jnp.zeros((ROWS, COLS), F32)
            elif strip == 1:
                value = target_ref[0, ch]
            else:
                value = edge_ref[strip // 2, ch]
            t_ref[pl.ds(strip * 256 + ch, ROWS, stride=16), :] = value

    taps = window_columns()

    def square_target(row, carry):
        rows = pl.ds(pl.multiple_of(row * 16, 16), 16)
        tt_ref[rows, :] = t_ref[rows, :] * t_ref[rows, :]
        return carry

    lax.fori_loop(FIRST - 5, FIRST + MAPS + 5, square_target, 0)

    def target_maps(i, carry):
        rows = pl.ds(pl.multiple_of(i * 16, 16), 16)
        mt_ref[rows, :] = along_columns(along_rows(t_ref, FIRST + i), taps)
        btt_ref[rows, :] = along_columns(along_rows(tt_ref, FIRST + i), taps)
        return carry

    lax.fori_loop(0, MAPS, target_maps, 0)

    owner = [list_ref[0, :, 128 * h : 128 * h + 128] >> 7 for h in range(2)]
    place = [list_ref[0, :, 128 * h : 128 * h + 128] & 127 for h in range(2)]

    def take_group(step, totals):
        block = lax.rem(my_group + groups - step, groups)
        for i in range(group):
            sender = block * group + i

            @pl.when(sender != me)
            def _():
                forward_copy(sender, sender).wait_recv()

        for i in range(group):
            sender = block * group + i
            chosen = [owner[h] == sender for h in range(2)]
            new = []
            for f in range(SPLAT):
                row = jnp.broadcast_to(recv_ref[sender, f : f + 1, :], (TILES, COLS))
                for h in range(2):
                    new.append(
                        jnp.where(chosen[h], lane_gather(row, place[h]), totals[2 * f + h])
                    )
            totals = tuple(new)
        return totals

    totals = lax.fori_loop(
        0, groups, take_group, tuple(jnp.zeros((TILES, COLS), F32) for _ in range(2 * SPLAT))
    )
    tile_row = iota((TILES, COLS), 0)
    length = jnp.zeros((TILES, COLS), I32)
    for j in range(TILES):
        length = jnp.where(tile_row == j, len_ref[0, j], length)
    for f in range(SPLAT):
        for h in range(2):
            splat_ref[f * TILES : (f + 1) * TILES, 128 * h : 128 * h + 128] = totals[2 * f + h]
    for h in range(2):
        active = (iota((TILES, COLS), 1) + 128 * h) < length
        splat_ref[SPLAT * TILES : (SPLAT + 1) * TILES, 128 * h : 128 * h + 128] = jnp.where(
            active, totals[2 * 5 + h], 0.0
        )

    def splat_row(f, j):
        return splat_ref[pl.ds(f * TILES + j, 1), :]

    column_x = iota((ROWS, LIST), 0).astype(F32) + (0.5 - 8.0)
    first_of = iota((LIST, LIST), 0)
    then_of = iota((LIST, LIST), 1)
    earlier = jnp.where(first_of < then_of, 1.0, 0.0).astype(BF16)
    earlier = jnp.concatenate([earlier, earlier], axis=0)
    later = jnp.where(first_of > then_of, 1.0, 0.0).astype(BF16)
    later = jnp.concatenate([later, later], axis=0)

    def pixel_rows(j, y):
        return pl.ds(pl.multiple_of(j * 256 + y * 16, 16), 16)

    def composite(j, carry):
        ox, oy, a, b, c = [splat_row(f, j) for f in range(5)]
        opacity = splat_row(SPLAT, j)
        dx = column_x - ox
        square_part = (-0.5 * a) * dx * dx
        cross_part = (-b) * dx
        for y in range(16):
            dy = (y + 0.5 - 8.0) - oy
            power = square_part + dy * cross_part + (-0.5 * c) * dy * dy
            cover = opacity * jnp.exp(power)
            cover_ref[pixel_rows(j, y), :] = cover
            top, low = parts(jnp.log(1.0 - cover))
            pair_ref[y * 16 : y * 16 + 16, 0:LIST] = top
            pair_ref[y * 16 : y * 16 + 16, LIST : 2 * LIST] = low
        deriv_ref[...] = dot(pair_ref[...], earlier)
        for y in range(16):
            rows = pixel_rows(j, y)
            cover = cover_ref[rows, :]
            weight = cover * jnp.exp(deriv_ref[y * 16 : y * 16 + 16, :])
            cover_ref[rows, :] = cover / (1.0 - cover)
            weight_ref[rows, :] = weight
            top, low = parts(weight)
            top_ref[rows, :] = top
            low_ref[rows, :] = low
        tile_rows = pl.ds(pl.multiple_of(j * 256, 256), 256)
        colours = jnp.concatenate([splat_row(6 + c, j) for c in range(3)], axis=0)
        colour_top = colours.astype(BF16).astype(F32)
        packed = jnp.concatenate(
            [colour_top, colours - colour_top, jnp.zeros((10, LIST), F32)], axis=0
        ).astype(BF16)
        seen = dot_nt(packed, top_ref[tile_rows, :]) + dot_nt(packed, low_ref[tile_rows, :])
        for c in range(3):
            tile_rad_ref[pl.ds(c * TILES + j, 1), :] = seen[c : c + 1] + seen[c + 3 : c + 4]
        return carry

    lax.fori_loop(0, TILES, composite, 0)

    lane = iota((TILES, COLS), 1)
    in_tile = (lane >> 4) == tile_row
    for y in range(16):
        index = (lane & 15) + 16 * (y % 8)
        for c in range(3):
            half = 128 * (y // 8)
            source = tile_rad_ref[c * TILES : (c + 1) * TILES, half : half + 128]
            line = jnp.sum(jnp.where(in_tile, lane_gather(source, index), 0.0), axis=0, keepdims=True)
            strips_ref[1, c, y : y + 1, :] = line

    @pl.when(me < n - 1)
    def _():
        strip_copy(after, 0).start()

    @pl.when(me > 0)
    def _():
        strip_copy(before, 1).start()

    rad_ref[0] = strips_ref[1]

    channel = iota((16, COLS), 0)
    of_colour = [lax.rem(channel, 3) == c for c in range(3)]
    bracket = channel // 3
    exposure = jnp.zeros((16, COLS), F32)
    for b in range(5):
        exposure = jnp.where(bracket == b, expo_ref[0, b], exposure)

    @pl.when(me > 0)
    def _():
        strip_copy(before, 0).wait_recv()

    @pl.when(me < n - 1)
    def _():
        strip_copy(after, 1).wait_recv()

    def tone(row, carry):
        strip = row // ROWS
        y = lax.rem(row, ROWS)
        lines = [strips_ref[strip, c, pl.ds(y, 1), :] for c in range(3)]
        scaled = exposure * jnp.where(
            of_colour[0], lines[0], jnp.where(of_colour[1], lines[1], lines[2])
        )
        mapped = scaled / (1.0 + scaled)
        rows = pl.ds(pl.multiple_of(row * 16, 16), 16)
        p_ref[rows, :] = mapped
        pp_ref[rows, :] = mapped * mapped
        pt_ref[rows, :] = mapped * t_ref[rows, :]
        return carry

    lax.fori_loop(FIRST - 5, FIRST + MAPS + 5, tone, 0)

    def similarity_row(i, carry):
        row = FIRST + i
        rows = pl.ds(pl.multiple_of(i * 16, 16), 16)
        mean_p = along_columns(along_rows(p_ref, row), taps)
        square_p = along_columns(along_rows(pp_ref, row), taps)
        cross = along_columns(along_rows(pt_ref, row), taps)
        mean_t = mt_ref[rows, :]
        both = mean_p * mean_t
        n1 = 2.0 * both + FLOOR_MEAN
        n2 = 2.0 * (cross - both) + FLOOR_VAR
        d1 = mean_p * mean_p + mean_t * mean_t + FLOOR_MEAN
        d2 = (square_p - mean_p * mean_p) + (btt_ref[rows, :] - mean_t * mean_t) + FLOOR_VAR
        inside = ((row >= ROWS) | (me > 0)) & ((row < 2 * ROWS) | (me < n - 1))
        share = jnp.where(inside, 1.0, 0.0) / (d1 * d2)
        similar = n1 * n2 * share
        gpt_ref[rows, :] = -2.0 * n1 * share
        by_d2 = similar / d2
        gpp_ref[rows, :] = by_d2
        gm_ref[rows, :] = 2.0 * (
            mean_t * (n1 - n2) * share + mean_p * (similar / d1 - by_d2)
        )
        return carry

    lax.fori_loop(0, MAPS, similarity_row, 0)

    def radiance_row(y, carry):
        own = pl.ds(pl.multiple_of((y + ROWS) * 16, 16), 16)
        mapped = p_ref[own, :]
        wanted = t_ref[own, :]
        slope = along_columns(along_rows(gm_ref, y + 5), taps)
        slope = slope + 2.0 * mapped * along_columns(along_rows(gpp_ref, y + 5), taps)
        slope = slope + wanted * along_columns(along_rows(gpt_ref, y + 5), taps)
        slope = slope + 1.6 * (mapped - wanted)
        rest = 1.0 - mapped
        slope = slope * exposure * (rest * rest)
        for c in range(3):
            line = jnp.sum(jnp.where(of_colour[c], slope, 0.0), axis=0, keepdims=True)
            gimg_ref[pl.ds(c * ROWS + y, 1), :] = line
        return carry

    lax.fori_loop(0, ROWS, radiance_row, 0)

    spread_index = 16 * tile_row + (lane & 15)
    for c in range(3):
        for half in range(2):
            total = jnp.zeros((TILES, COLS), F32)
            for y in range(8):
                row = c * ROWS + half * 8 + y
                source = jnp.broadcast_to(gimg_ref[row : row + 1, :], (TILES, COLS))
                total = jnp.where((lane >> 4) == y, lane_gather(source, spread_index), total)
            gtile_ref[c * TILES : (c + 1) * TILES, 128 * half : 128 * half + 128] = total

    def composite_back(j, carry):
        ox, oy, a, b, c_ = [splat_row(f, j) for f in range(5)]
        colours = jnp.concatenate([splat_row(6 + c, j) for c in range(3)], axis=0)
        colour_top = colours.astype(BF16).astype(F32)
        slopes = jnp.concatenate(
            [gtile_ref[pl.ds(c * TILES + j, 1), :] for c in range(3)], axis=0
        )
        slope_top = slopes.astype(BF16).astype(F32)
        left = jnp.concatenate(
            [slope_top, slopes - slope_top, slope_top, jnp.zeros((7, LIST), F32)], axis=0
        )
        right = jnp.concatenate(
            [colour_top, colour_top, colours - colour_top, jnp.zeros((7, LIST), F32)], axis=0
        )
        deriv_ref[...] = dot(left.T.astype(BF16), right.astype(BF16))
        for y in range(16):
            rows = pixel_rows(j, y)
            value = deriv_ref[y * 16 : y * 16 + 16, :] * weight_ref[rows, :]
            weight_ref[rows, :] = value
            top, low = parts(value)
            pair_ref[y * 16 : y * 16 + 16, 0:LIST] = top
            pair_ref[y * 16 : y * 16 + 16, LIST : 2 * LIST] = low
        deriv_ref[...] = dot(pair_ref[...], later)
        dx = column_x - ox
        dxx = dx * dx
        zero = jnp.zeros((ROWS, LIST), F32)
        m0, mx, mxx = zero, zero, zero
        my, mxy, myy = zero, zero, zero
        for y in range(16):
            rows = pixel_rows(j, y)
            dy = (y + 0.5 - 8.0) - oy
            q = weight_ref[rows, :] - deriv_ref[y * 16 : y * 16 + 16, :] * cover_ref[rows, :]
            qx = q * dx
            qy = q * dy
            m0 = m0 + q
            mx = mx + qx
            my = my + qy
            mxx = mxx + q * dxx
            mxy = mxy + qx * dy
            myy = myy + qy * dy
        m0, mx, my, mxx, mxy, myy = [
            jnp.sum(m, axis=0, keepdims=True) for m in (m0, mx, my, mxx, mxy, myy)
        ]
        tile_rows = pl.ds(pl.multiple_of(j * 256, 256), 256)
        packed = left.astype(BF16)
        by_colour = dot(packed, top_ref[tile_rows, :]) + dot(packed, low_ref[tile_rows, :])
        rows = [
            a * mx + b * my,
            b * mx + c_ * my,
            -0.5 * mxx,
            -mxy,
            -0.5 * myy,
            m0 / splat_row(5, j),
        ] + [by_colour[c : c + 1] + by_colour[c + 3 : c + 4] for c in range(3)]
        lanes = pl.ds(pl.multiple_of(j * LIST, LIST), LIST)
        mask = slot_mask_ref[:, lanes]
        for f in range(SPLAT):
            top = rows[f].astype(BF16).astype(F32)
            for k, part in enumerate((top, rows[f] - top)):
                at = (k * SPLAT + f) * halves
                slot_left_ref[at : at + halves, :] = (
                    jnp.broadcast_to(part, (halves, LIST)).astype(BF16) * mask
                )
        update = dot_nt(slot_left_ref[...], slot_one_ref[:, lanes])

        @pl.when(j == 0)
        def _():
            slot_sum_ref[...] = update

        @pl.when(j > 0)
        def _():
            slot_sum_ref[...] = slot_sum_ref[...] + update

        return carry

    lax.fori_loop(0, TILES, composite_back, 0)

    count = SPLAT * halves
    for side in range(2):
        lanes = slice(side * COLS, side * COLS + COLS)
        sgrad_ref[side * count : (side + 1) * count, :] = (
            slot_sum_ref[0:count, lanes] + slot_sum_ref[count : 2 * count, lanes]
        )

    def send_back(step, carry):
        block = lax.rem(my_group + step, groups)
        for i in range(group):
            peer = block * group + i
            first = (i % 2) * count + block * (group // 2) + i // 2
            back_ref[peer] = sgrad_ref[pl.ds(first, SPLAT, stride=halves), :]
        for i in range(group):
            peer = block * group + lax.rem(me + i, group)

            @pl.when(peer != me)
            def _():
                back_copy(peer, me).start()

        return carry

    lax.fori_loop(0, groups, send_back, 0)
    ret_ref[me] = back_ref[me]

    own_sum_ref[...] = jnp.zeros_like(own_sum_ref)

    def add_group(step, carry):
        block = lax.rem(my_group + groups - step, groups)
        for i in range(group):
            sender = block * group + i

            @pl.when(sender != me)
            def _():
                back_copy(sender, sender).wait_recv()

        for i in range(group):
            sender = block * group + i
            mask = own_mask_ref[:, pl.ds(pl.multiple_of(sender * COLS, COLS), COLS)]
            message = ret_ref[sender]
            top = message.astype(BF16).astype(F32)
            for k, part in enumerate((top, message - top)):
                for f in range(SPLAT):
                    at = (k * SPLAT + f) * 16
                    own_left_ref[at : at + 16, i * COLS : (i + 1) * COLS] = (
                        jnp.broadcast_to(part[f : f + 1], (16, COLS)).astype(BF16) * mask
                    )
        lanes = pl.ds(pl.multiple_of(block * group * COLS, COLS), group * COLS)
        own_sum_ref[...] = own_sum_ref[...] + dot_nt(own_left_ref[...], own_one_ref[:, lanes])
        return carry

    lax.fori_loop(0, groups, add_group, 0)
    for f in range(SPLAT):
        for side in range(2):
            lanes = slice(side * COLS, side * COLS + COLS)
            low = (SPLAT + f) * 16
            gown_ref[pl.ds(f * HIGH + side, 16, stride=2), :] = (
                own_sum_ref[f * 16 : f * 16 + 16, lanes] + own_sum_ref[low : low + 16, lanes]
            )

    def view_copy(peer, slot):
        return pltpu.make_async_remote_copy(
            src_ref=gown_ref,
            dst_ref=gall_ref.at[slot],
            send_sem=v_send.at[peer],
            recv_sem=v_recv.at[slot],
            device_id={"view": peer},
            device_id_type=MESH,
        )

    for i in range(1, nv):
        view_copy(lax.rem(mv + i, nv), mv).start()
    gall_ref[mv] = gown_ref[...]

    def drain(i, carry):
        peer = lax.rem(me + i, n)
        forward_copy(peer, me).wait_send()
        back_copy(peer, me).wait_send()
        return carry

    lax.fori_loop(1, n, drain, 0)

    @pl.when(me < n - 1)
    def _():
        target_copy(after, 0).wait_send()
        strip_copy(after, 0).wait_send()

    @pl.when(me > 0)
    def _():
        target_copy(before, 1).wait_send()
        strip_copy(before, 1).wait_send()

    for i in range(1, nv):
        peer = lax.rem(mv + i, nv)
        view_copy(peer, mv).wait_send()
        view_copy(peer, peer).wait_recv()


def pull_back_kernel(nv, gauss_ref, gall_ref, rad_ref, grad_ref, radiance_ref, wide_ref, sum_ref):
    radiance_ref[...] = rad_ref[...]
    spread_rows(gauss_ref, wide_ref)

    def one_view(v, carry):
        camera = [
            jnp.broadcast_to(gall_ref[v, pl.ds(SPLAT * HIGH + i, 1), :], (8, COLS)) for i in range(5)
        ]
        rotation = camera_rotation(camera)

        def one_chunk(i, inner):
            def rows(f):
                return pl.ds(pl.multiple_of(f * HIGH + i * 8, 8), 8)

            params = [wide_ref[rows(f), :] for f in range(FEAT)]
            slopes = [gall_ref[v, rows(f), :] for f in range(SPLAT)]
            _, pull = jax.vjp(lambda values: project(values, camera, rotation), params)
            (grads,) = pull(slopes)
            for f in range(FEAT):
                sum_ref[rows(f), :] = jnp.where(v == 0, 0.0, sum_ref[rows(f), :]) + grads[f]
            return inner

        return lax.fori_loop(0, HIGH // 8, one_chunk, carry)

    lax.fori_loop(0, nv, one_view, 0)

    def collect(h, carry):
        lanes = pl.ds(pl.multiple_of(h * COLS, COLS), COLS)
        for first in range(0, FEAT, 8):
            size = min(8, FEAT - first)
            grad_ref[first : first + size, lanes] = sum_ref[pl.ds(first * HIGH + h, size, stride=HIGH), :]
        return carry

    lax.fori_loop(0, HIGH, collect, 0)


def shards(n, nv, gaussians, send_index, tile_list, tile_length, camera, exposure, target):
    vmem = pl.BlockSpec(memory_space=pltpu.VMEM)
    smem = pl.BlockSpec(memory_space=pltpu.SMEM)
    halves = max(16, n // 2)
    group = min(8, n)

    def scratch(shape, dtype=F32):
        return pltpu.VMEM(shape, dtype)

    pixels = TILES * 256
    scratches = [
        scratch((64 * HIGH, COLS)),
        scratch((SPLAT * HIGH, COLS)),
        scratch((SPLAT * group, COLS)),
        scratch((n, SPLAT, COLS)),
        scratch((n, SPLAT, COLS)),
        scratch(((SPLAT + 1) * TILES, LIST)),
        scratch((pixels, LIST)),
        scratch((pixels, LIST)),
        scratch((pixels, LIST), BF16),
        scratch((pixels, LIST), BF16),
        scratch((LIST, 2 * LIST), BF16),
        scratch((LIST, LIST)),
        scratch((3 * TILES, LIST)),
        scratch((3, 3, ROWS, COLS)),
        scratch((2, CHANNELS, ROWS, COLS)),
        scratch((48 * 16, COLS)),
        scratch((48 * 16, COLS)),
        scratch((48 * 16, COLS)),
        scratch((48 * 16, COLS)),
        scratch((48 * 16, COLS)),
        scratch((MAPS * 16, COLS)),
        scratch((MAPS * 16, COLS)),
        scratch((MAPS * 16, COLS)),
        scratch((MAPS * 16, COLS)),
        scratch((MAPS * 16, COLS)),
        scratch((3 * ROWS, COLS)),
        scratch((3 * TILES, LIST)),
        scratch((2 * SPLAT * halves, COLS)),
        scratch((256, TILES * LIST), BF16),
        scratch((halves, TILES * LIST), BF16),
        scratch((256, n * COLS), BF16),
        scratch((16, n * COLS), BF16),
        scratch((2 * SPLAT * halves, LIST), BF16),
        scratch((2 * SPLAT * halves, 256)),
        scratch((n, SPLAT, COLS)),
        scratch((n, SPLAT, COLS)),
        scratch((2 * SPLAT * 16, group * COLS), BF16),
        scratch((2 * SPLAT * 16, 256)),
        scratch((SPLAT * HIGH + 8, COLS)),
    ]
    sems = [pltpu.SemaphoreType.DMA((k,)) for k in (n, n, n, n, 2, 2, 2, 2, nv, nv)]
    gathered, strip = pl.pallas_call(
        functools.partial(step_kernel, n, nv),
        out_shape=(
            jax.ShapeDtypeStruct((nv, SPLAT * HIGH + 8, COLS), F32),
            jax.ShapeDtypeStruct((1, 3, ROWS, COLS), F32),
        ),
        in_specs=[vmem, vmem, vmem, smem, smem, smem, vmem],
        out_specs=(vmem, vmem),
        scratch_shapes=scratches + sems,
        compiler_params=pltpu.CompilerParams(
            collective_id=0, has_side_effects=True, vmem_limit_bytes=50 * 2**20
        ),
        name="splat_step",
    )(gaussians, send_index, tile_list, tile_length, camera, exposure, target)
    return pl.pallas_call(
        functools.partial(pull_back_kernel, nv),
        out_shape=(
            jax.ShapeDtypeStruct((FEAT, HIGH * COLS), F32),
            jax.ShapeDtypeStruct((1, 3, ROWS, COLS), F32),
        ),
        in_specs=[vmem, vmem, vmem],
        out_specs=(vmem, vmem),
        scratch_shapes=[scratch((64 * HIGH, COLS)), scratch((64 * HIGH, COLS))],
        compiler_params=pltpu.CompilerParams(vmem_limit_bytes=32 * 2**20),
        name="pull_back",
    )(gaussians, gathered, strip)


def solution(mesh):
    placed = (
        P(None, "gs"),
        P("view", "gs", None),
        P("view", "gs", None),
        P("view", "gs"),
        P("view", None),
        P("view", None),
        P("view", None, "gs", None),
    )
    return jax.shard_map(
        functools.partial(shards, mesh.shape["gs"], mesh.shape["view"]),
        mesh=mesh,
        in_specs=placed,
        out_specs=(P(None, "gs"), P("view", None, "gs", None)),
        check_vma=False,
    )
```

```python
import functools

import jax
import jax.numpy as jnp
import numpy as np
from jax import lax
from jax.experimental import pallas as pl
from jax.experimental.pallas import tpu as pltpu
from jax.sharding import PartitionSpec as P

MESH = pl.DeviceIdType.MESH
F32, BF16, I32 = jnp.float32, jnp.bfloat16, jnp.int32

FOCAL = 16.0
DILATE = 0.3
SH_C0 = 0.28209479177387814
SH_C1 = 0.4886025119029199
SH_C2 = [
    1.0925484305920792,
    -1.0925484305920792,
    0.31539156525252005,
    -1.0925484305920792,
    0.5462742152960396,
]
SH_C3 = [
    -0.5900435899266435,
    2.890611442640554,
    -0.4570457994644658,
    0.3731763325901154,
    -0.4570457994644658,
    1.445305721320277,
    -0.5900435899266435,
]
WINDOW_RAW = np.exp(-((np.arange(11) - 5.0) ** 2) / 4.5)
WINDOW = [float(v) for v in WINDOW_RAW / WINDOW_RAW.sum()]
FLOOR_MEAN = 0.0001
FLOOR_VAR = 0.0009

FEAT = 59
SPLAT = 9
HIGH = 32
TILES = 8
LIST = 256
ROWS = 16
COLS = 128
CHANNELS = 15
FIRST = 11
JAC = 45
MAPS = 26


def product3(left, right):
    return [[sum((left[i][k] * right[k][j] for k in range(3))) for j in range(3)] for i in range(3)]


def camera_rotation(camera):
    yaw_cos, yaw_sin = (jnp.cos(camera[0]), jnp.sin(camera[0]))
    pitch_cos, pitch_sin = (jnp.cos(camera[1]), jnp.sin(camera[1]))
    roll_cos, roll_sin = (jnp.cos(camera[2]), jnp.sin(camera[2]))
    about_z = [[yaw_cos, -yaw_sin, 0.0], [yaw_sin, yaw_cos, 0.0], [0.0, 0.0, 1.0]]
    about_y = [[pitch_cos, 0.0, pitch_sin], [0.0, 1.0, 0.0], [-pitch_sin, 0.0, pitch_cos]]
    about_x = [[1.0, 0.0, 0.0], [0.0, roll_cos, -roll_sin], [0.0, roll_sin, roll_cos]]
    return product3(product3(about_z, about_y), about_x)


def quaternion_matrix(q0, q1, q2, q3):
    scale = 1.0 / jnp.sqrt(q0 * q0 + q1 * q1 + q2 * q2 + q3 * q3)
    w, x, y, z = (q0 * scale, q1 * scale, q2 * scale, q3 * scale)
    return [
        [1 - 2 * (y * y + z * z), 2 * (x * y - w * z), 2 * (x * z + w * y)],
        [2 * (x * y + w * z), 1 - 2 * (x * x + z * z), 2 * (y * z - w * x)],
        [2 * (x * z - w * y), 2 * (y * z + w * x), 1 - 2 * (x * x + y * y)],
    ]


def harmonics(x, y, z):
    xx, yy, zz = (x * x, y * y, z * z)
    return [
        SH_C0 + 0.0 * x,
        -SH_C1 * y,
        SH_C1 * z,
        -SH_C1 * x,
        SH_C2[0] * x * y,
        SH_C2[1] * y * z,
        SH_C2[2] * (2 * zz - xx - yy),
        SH_C2[3] * x * z,
        SH_C2[4] * (xx - yy),
        SH_C3[0] * y * (3 * xx - yy),
        SH_C3[1] * x * y * z,
        SH_C3[2] * y * (4 * zz - xx - yy),
        SH_C3[3] * z * (2 * zz - 3 * xx - 3 * yy),
        SH_C3[4] * x * (4 * zz - xx - yy),
        SH_C3[5] * z * (xx - yy),
        SH_C3[6] * x * (xx - 3 * yy),
    ]


def project(params, camera, rotation):
    translation = [0.15 * camera[3], 0.15 * camera[4], 6.0]
    position = [params[i] for i in range(3)]
    viewed = [
        sum((rotation[i][j] * position[j] for j in range(3))) + translation[i] for i in range(3)
    ]
    inverse_z = 1.0 / viewed[2]
    row_x = [
        FOCAL * inverse_z * (rotation[0][k] - viewed[0] * inverse_z * rotation[2][k])
        for k in range(3)
    ]
    row_y = [
        FOCAL * inverse_z * (rotation[1][k] - viewed[1] * inverse_z * rotation[2][k])
        for k in range(3)
    ]
    orient = quaternion_matrix(params[6], params[7], params[8], params[9])
    stretch = [jnp.exp(params[3 + k]) for k in range(3)]
    image_x = [sum((row_x[i] * orient[i][k] for i in range(3))) * stretch[k] for k in range(3)]
    image_y = [sum((row_y[i] * orient[i][k] for i in range(3))) * stretch[k] for k in range(3)]
    cov_xx = sum((e * e for e in image_x)) + DILATE
    cov_yy = sum((e * e for e in image_y)) + DILATE
    cov_xy = sum((image_x[k] * image_y[k] for k in range(3)))
    share = 1.0 / (cov_xx * cov_yy - cov_xy * cov_xy)
    opacity = 1.0 / (1.0 + jnp.exp(-params[10]))
    toward = [
        position[k] + sum((rotation[i][k] * translation[i] for i in range(3))) for k in range(3)
    ]
    closeness = 1.0 / jnp.sqrt(sum((e * e for e in toward)))
    harmonic = harmonics(*[e * closeness for e in toward])
    colour = [
        jnp.exp(sum((harmonic[l] * params[11 + 3 * l + c] for l in range(16)))) for c in range(3)
    ]
    return [
        FOCAL * viewed[0] * inverse_z,
        FOCAL * viewed[1] * inverse_z,
        cov_yy * share,
        -cov_xy * share,
        cov_xx * share,
        opacity,
    ] + colour


def iota(shape, axis):
    return lax.broadcasted_iota(I32, shape, axis)


def lane_gather(values, index):
    return jnp.take_along_axis(values, index, axis=1, mode="promise_in_bounds")


def parts(values):
    top = values.astype(BF16)
    return top, (values - top.astype(F32)).astype(BF16)


def dot(left, right):
    return jnp.dot(left, right, preferred_element_type=F32)


def dot_nt(left, right):
    return lax.dot_general(left, right, (((1,), (1,)), ((), ())), preferred_element_type=F32)


def spread_rows(gauss_ref, wide_ref):
    def one(h, carry):
        lanes = pl.ds(pl.multiple_of(h * COLS, COLS), COLS)
        for first in range(0, FEAT, 8):
            count = min(8, FEAT - first)
            wide_ref[pl.ds(first * HIGH + h, count, stride=HIGH), :] = gauss_ref[first : first + count, lanes]
        return carry

    lax.fori_loop(0, HIGH, one, 0)


def window_columns():
    column = iota((1, COLS), 1)
    taps = []
    for i in range(11):
        source = column + (i - 5)
        taps.append(jnp.where((source >= 0) & (source < COLS), WINDOW[i], 0.0))
    return taps


def along_columns(values, taps):
    total = values * taps[5]
    for i in range(11):
        if i != 5:
            total = total + taps[i] * pltpu.roll(values, (5 - i) % COLS, axis=1)
    return total


def along_rows(ref, row):
    def at(i):
        return ref[pl.ds(pl.multiple_of((row + i) * 16, 16), 16), :]

    total = WINDOW[5] * at(0)
    for i in range(1, 6):
        total = total + WINDOW[5 + i] * (at(i) + at(-i))
    return total


def step_kernel(
    n,
    nv,
    gauss_hbm,
    send_hbm,
    list_hbm,
    len_hbm,
    cam_hbm,
    expo_hbm,
    target_hbm,
    wide_grad_ref,
    rad_ref,
    gauss_ref,
    send_ref,
    list_ref,
    len_ref,
    cam_ref,
    expo_ref,
    target_ref,
    wide_ref,
    table_ref,
    pick_ref,
    out_ref,
    recv_ref,
    splat_ref,
    cover_ref,
    weight_ref,
    top_ref,
    low_ref,
    pair_ref,
    deriv_ref,
    tile_rad_ref,
    strips_ref,
    edge_ref,
    t_ref,
    tt_ref,
    p_ref,
    pp_ref,
    pt_ref,
    mt_ref,
    btt_ref,
    gm_ref,
    gpp_ref,
    gpt_ref,
    gimg_ref,
    gtile_ref,
    sgrad_ref,
    slot_one_ref,
    slot_mask_ref,
    own_one_ref,
    own_mask_ref,
    slot_left_ref,
    slot_sum_ref,
    back_ref,
    ret_ref,
    own_left_ref,
    own_sum_ref,
    gall_ref,
    cams_ref,
    turn_ref,
    jac_ref,
    f_send,
    f_recv,
    b_send,
    b_recv,
    t_send,
    t_recv,
    h_send,
    h_recv,
    v_send,
    v_recv,
    c_send,
    c_recv,
    in_sem,
):
    me = lax.axis_index("gs")
    mv = lax.axis_index("view")
    after = lax.rem(me + 1, n)
    before = lax.rem(me + n - 1, n)
    group = min(8, n)
    groups = n // group
    halves = slot_mask_ref.shape[0]

    loads = [
        pltpu.make_async_copy(source, place, in_sem.at[i])
        for i, (source, place) in enumerate(
            [
                (gauss_hbm, gauss_ref),
                (cam_hbm, cam_ref),
                (send_hbm, send_ref),
                (target_hbm, target_ref),
                (list_hbm, list_ref),
                (len_hbm, len_ref),
                (expo_hbm, expo_ref),
            ]
        )
    ]
    for load in loads:
        load.start()

    barrier = pltpu.get_barrier_semaphore()

    def greet(i, carry):
        pl.semaphore_signal(
            barrier, inc=1, device_id={"gs": lax.rem(me + i, n)}, device_id_type=MESH
        )
        return carry

    lax.fori_loop(1, n, greet, 0)
    for i in range(1, nv):
        pl.semaphore_signal(
            barrier, inc=1, device_id={"view": lax.rem(mv + i, nv)}, device_id_type=MESH
        )

    loads[0].wait()
    loads[1].wait()
    spread_rows(gauss_ref, wide_ref)
    camera = [jnp.broadcast_to(cam_ref[0:1, i : i + 1], (8, COLS)) for i in range(5)]
    rotation = camera_rotation(camera)

    def project_rows(i, carry):
        rows = [
            wide_ref[pl.ds(pl.multiple_of(f * HIGH + i * 8, 8), 8), :] for f in range(FEAT)
        ]
        for f, value in enumerate(project(rows, camera, rotation)):
            table_ref[pl.ds(pl.multiple_of(f * HIGH + i * 8, 8), 8), :] = value
        return carry

    lax.fori_loop(0, HIGH // 8, project_rows, 0, unroll=4)
    cams_ref[mv] = jnp.concatenate(
        [camera[i][0:1] for i in range(5)] + [jnp.zeros((3, COLS), F32)], axis=0
    )

    for load in loads[2:]:
        load.wait()
    pl.semaphore_wait(barrier, n - 1 + nv - 1)

    def target_copy(peer, side):
        return pltpu.make_async_remote_copy(
            src_ref=target_ref.at[0],
            dst_ref=edge_ref.at[side],
            send_sem=t_send.at[side],
            recv_sem=t_recv.at[side],
            device_id={"gs": peer},
            device_id_type=MESH,
        )

    def strip_copy(peer, side):
        return pltpu.make_async_remote_copy(
            src_ref=strips_ref.at[1],
            dst_ref=strips_ref.at[2 * side],
            send_sem=h_send.at[side],
            recv_sem=h_recv.at[side],
            device_id={"gs": peer},
            device_id_type=MESH,
        )

    def camera_copy(peer, slot):
        return pltpu.make_async_remote_copy(
            src_ref=cams_ref.at[mv],
            dst_ref=cams_ref.at[slot],
            send_sem=c_send.at[peer],
            recv_sem=c_recv.at[slot],
            device_id={"view": peer},
            device_id_type=MESH,
        )

    @pl.when(me < n - 1)
    def _():
        target_copy(after, 0).start()

    @pl.when(me > 0)
    def _():
        target_copy(before, 1).start()

    def forward_copy(peer, slot):
        return pltpu.make_async_remote_copy(
            src_ref=out_ref.at[peer],
            dst_ref=recv_ref.at[slot],
            send_sem=f_send.at[peer],
            recv_sem=f_recv.at[slot],
            device_id={"gs": peer},
            device_id_type=MESH,
        )

    def back_copy(peer, slot):
        return pltpu.make_async_remote_copy(
            src_ref=back_ref.at[peer],
            dst_ref=ret_ref.at[slot],
            send_sem=b_send.at[peer],
            recv_sem=b_recv.at[slot],
            device_id={"gs": peer},
            device_id_type=MESH,
        )

    my_group = me // group

    def shift_of(step):
        reach = groups // 2 - (step + 1) // 2
        return jnp.where(step % 2 == 1, reach, lax.rem(groups - reach, groups))

    def gather_group(step, carry):
        block = lax.rem(my_group + shift_of(step), groups)
        index = send_ref[0, pl.ds(pl.multiple_of(block * group, group), group), :]
        high = index >> 7
        low = index & 127

        def one(h, totals):
            chosen = high == h
            new = []
            for f in range(SPLAT):
                row = jnp.broadcast_to(table_ref[pl.ds(f * HIGH + h, 1), :], (group, COLS))
                new.append(jnp.where(chosen, lane_gather(row, low), totals[f]))
            return tuple(new)

        totals = lax.fori_loop(
            0, HIGH, one, tuple(jnp.zeros((group, COLS), F32) for _ in range(SPLAT)), unroll=8
        )
        for f in range(SPLAT):
            pick_ref[f * group : (f + 1) * group, :] = totals[f]
        for i in range(group):
            peer = block * group + i
            out_ref[peer] = pick_ref[pl.ds(i, SPLAT, stride=group), :]
        for i in range(group):
            peer = block * group + lax.rem(me + i, group)

            @pl.when(peer != me)
            def _():
                forward_copy(peer, me).start()

        return carry

    lax.fori_loop(0, groups, gather_group, 0)
    recv_ref[me] = out_ref[me]
    for i in range(1, nv):
        camera_copy(lax.rem(mv + i, nv), mv).start()

    def own_factors(r, carry):
        index = send_ref[0, pl.ds(r, 1), :]
        lanes = pl.ds(pl.multiple_of(r * COLS, COLS), COLS)
        own_one_ref[:, lanes] = jnp.where(iota((256, COLS), 0) == (index & 255), 1.0, 0.0).astype(BF16)
        own_mask_ref[:, lanes] = jnp.where(iota((16, COLS), 0) == (index >> 8), 1.0, 0.0).astype(BF16)
        return carry

    lax.fori_loop(0, n, own_factors, 0, unroll=8)

    def slot_factors(j, carry):
        index = list_ref[0, pl.ds(j, 1), :]
        lanes = pl.ds(pl.multiple_of(j * LIST, LIST), LIST)
        slot_one_ref[:, lanes] = jnp.where(iota((256, LIST), 0) == (index & 255), 1.0, 0.0).astype(BF16)
        slot_mask_ref[:, lanes] = jnp.where(iota((halves, LIST), 0) == (index >> 8), 1.0, 0.0).astype(
            BF16
        )
        return carry

    lax.fori_loop(0, TILES, slot_factors, 0, unroll=8)

    @pl.when(me == 0)
    def _():
        edge_ref[0] = jnp.zeros((CHANNELS, ROWS, COLS), F32)
        strips_ref[0] = jnp.zeros((3, ROWS, COLS), F32)

    @pl.when(me == n - 1)
    def _():
        edge_ref[1] = jnp.zeros((CHANNELS, ROWS, COLS), F32)
        strips_ref[2] = jnp.zeros((3, ROWS, COLS), F32)

    @pl.when(me > 0)
    def _():
        target_copy(before, 0).wait_recv()

    @pl.when(me < n - 1)
    def _():
        target_copy(after, 1).wait_recv()

    for strip in range(3):
        for ch in range(16):
            if ch == CHANNELS:
                value = jnp.zeros((ROWS, COLS), F32)
            elif strip == 1:
                value = target_ref[0, ch]
            else:
                value = edge_ref[strip // 2, ch]
            t_ref[pl.ds(strip * 256 + ch, ROWS, stride=16), :] = value

    taps = window_columns()

    def square_target(row, carry):
        rows = pl.ds(pl.multiple_of(row * 16, 16), 16)
        tt_ref[rows, :] = t_ref[rows, :] * t_ref[rows, :]
        return carry

    lax.fori_loop(FIRST - 5, FIRST + MAPS + 5, square_target, 0, unroll=4)

    def target_maps(i, carry):
        rows = pl.ds(pl.multiple_of(i * 16, 16), 16)
        mt_ref[rows, :] = along_columns(along_rows(t_ref, FIRST + i), taps)
        btt_ref[rows, :] = along_columns(along_rows(tt_ref, FIRST + i), taps)
        return carry

    lax.fori_loop(0, MAPS, target_maps, 0, unroll=26)

    owner = [list_ref[0, :, 128 * h : 128 * h + 128] >> 7 for h in range(2)]
    place = [list_ref[0, :, 128 * h : 128 * h + 128] & 127 for h in range(2)]

    def take_group(step, totals):
        block = lax.rem(my_group + groups - shift_of(step), groups)
        for i in range(group):
            sender = block * group + i

            @pl.when(sender != me)
            def _():
                forward_copy(sender, sender).wait_recv()

        for i in range(group):
            sender = block * group + i
            chosen = [owner[h] == sender for h in range(2)]
            new = []
            for f in range(SPLAT):
                row = jnp.broadcast_to(recv_ref[sender, f : f + 1, :], (TILES, COLS))
                for h in range(2):
                    new.append(
                        jnp.where(chosen[h], lane_gather(row, place[h]), totals[2 * f + h])
                    )
            totals = tuple(new)
        return totals

    totals = lax.fori_loop(
        0, groups, take_group, tuple(jnp.zeros((TILES, COLS), F32) for _ in range(2 * SPLAT))
    )
    tile_row = iota((TILES, COLS), 0)
    length = jnp.zeros((TILES, COLS), I32)
    for j in range(TILES):
        length = jnp.where(tile_row == j, len_ref[0:1, j : j + 1], length)
    for f in range(SPLAT):
        for h in range(2):
            splat_ref[f * TILES : (f + 1) * TILES, 128 * h : 128 * h + 128] = totals[2 * f + h]
    for h in range(2):
        active = (iota((TILES, COLS), 1) + 128 * h) < length
        splat_ref[SPLAT * TILES : (SPLAT + 1) * TILES, 128 * h : 128 * h + 128] = jnp.where(
            active, totals[2 * 5 + h], 0.0
        )

    def splat_row(f, j):
        return splat_ref[pl.ds(f * TILES + j, 1), :]

    column_x = iota((ROWS, LIST), 0).astype(F32) + (0.5 - 8.0)
    first_of = iota((LIST, LIST), 0)
    then_of = iota((LIST, LIST), 1)
    earlier = jnp.where(first_of < then_of, 1.0, 0.0).astype(BF16)
    earlier = jnp.concatenate([earlier, earlier], axis=0)
    later = jnp.where(first_of > then_of, 1.0, 0.0).astype(BF16)
    later = jnp.concatenate([later, later], axis=0)

    def pixel_rows(j, y):
        return pl.ds(pl.multiple_of(j * 256 + y * 16, 16), 16)

    def composite(j, carry):
        ox, oy, a, b, c = [splat_row(f, j) for f in range(5)]
        opacity = splat_row(SPLAT, j)
        dx = column_x - ox
        square_part = (-0.5 * a) * dx * dx
        cross_part = (-b) * dx
        for y in range(16):
            dy = (y + 0.5 - 8.0) - oy
            power = square_part + dy * cross_part + (-0.5 * c) * dy * dy
            cover = opacity * jnp.exp(power)
            cover_ref[pixel_rows(j, y), :] = cover
            top, low = parts(jnp.log(1.0 - cover))
            pair_ref[y * 16 : y * 16 + 16, 0:LIST] = top
            pair_ref[y * 16 : y * 16 + 16, LIST : 2 * LIST] = low
        deriv_ref[...] = dot(pair_ref[...], earlier)
        for y in range(16):
            rows = pixel_rows(j, y)
            cover = cover_ref[rows, :]
            weight = cover * jnp.exp(deriv_ref[y * 16 : y * 16 + 16, :])
            cover_ref[rows, :] = cover / (1.0 - cover)
            weight_ref[rows, :] = weight
            top, low = parts(weight)
            top_ref[rows, :] = top
            low_ref[rows, :] = low
        tile_rows = pl.ds(pl.multiple_of(j * 256, 256), 256)
        colours = jnp.concatenate([splat_row(6 + c, j) for c in range(3)], axis=0)
        colour_top = colours.astype(BF16).astype(F32)
        packed = jnp.concatenate(
            [colour_top, colours - colour_top, jnp.zeros((10, LIST), F32)], axis=0
        ).astype(BF16)
        seen = dot_nt(packed, top_ref[tile_rows, :]) + dot_nt(packed, low_ref[tile_rows, :])
        for c in range(3):
            tile_rad_ref[pl.ds(c * TILES + j, 1), :] = seen[c : c + 1] + seen[c + 3 : c + 4]
        return carry

    lax.fori_loop(0, TILES, composite, 0, unroll=8)

    lane = iota((TILES, COLS), 1)
    in_tile = (lane >> 4) == tile_row
    for y in range(16):
        index = (lane & 15) + 16 * (y % 8)
        for c in range(3):
            half = 128 * (y // 8)
            source = tile_rad_ref[c * TILES : (c + 1) * TILES, half : half + 128]
            line = jnp.sum(jnp.where(in_tile, lane_gather(source, index), 0.0), axis=0, keepdims=True)
            strips_ref[1, c, y : y + 1, :] = line

    @pl.when(me < n - 1)
    def _():
        strip_copy(after, 0).start()

    @pl.when(me > 0)
    def _():
        strip_copy(before, 1).start()

    rad_ref[0] = strips_ref[1]

    channel = iota((16, COLS), 0)
    of_colour = [lax.rem(channel, 3) == c for c in range(3)]
    bracket = channel // 3
    exposure = jnp.zeros((16, COLS), F32)
    for b in range(5):
        exposure = jnp.where(bracket == b, expo_ref[0:1, b : b + 1], exposure)

    @pl.when(me > 0)
    def _():
        strip_copy(before, 0).wait_recv()

    @pl.when(me < n - 1)
    def _():
        strip_copy(after, 1).wait_recv()

    def tone(row, carry):
        strip = row // ROWS
        y = lax.rem(row, ROWS)
        lines = [strips_ref[strip, c, pl.ds(y, 1), :] for c in range(3)]
        scaled = exposure * jnp.where(
            of_colour[0], lines[0], jnp.where(of_colour[1], lines[1], lines[2])
        )
        mapped = scaled / (1.0 + scaled)
        rows = pl.ds(pl.multiple_of(row * 16, 16), 16)
        p_ref[rows, :] = mapped
        pp_ref[rows, :] = mapped * mapped
        pt_ref[rows, :] = mapped * t_ref[rows, :]
        return carry

    lax.fori_loop(FIRST - 5, FIRST + MAPS + 5, tone, 0, unroll=36)

    def similarity_row(i, carry):
        row = FIRST + i
        rows = pl.ds(pl.multiple_of(i * 16, 16), 16)
        mean_p = along_columns(along_rows(p_ref, row), taps)
        square_p = along_columns(along_rows(pp_ref, row), taps)
        cross = along_columns(along_rows(pt_ref, row), taps)
        mean_t = mt_ref[rows, :]
        both = mean_p * mean_t
        n1 = 2.0 * both + FLOOR_MEAN
        n2 = 2.0 * (cross - both) + FLOOR_VAR
        d1 = mean_p * mean_p + mean_t * mean_t + FLOOR_MEAN
        d2 = (square_p - mean_p * mean_p) + (btt_ref[rows, :] - mean_t * mean_t) + FLOOR_VAR
        inside = ((row >= ROWS) | (me > 0)) & ((row < 2 * ROWS) | (me < n - 1))
        share = jnp.where(inside, 1.0, 0.0) / (d1 * d2)
        similar = n1 * n2 * share
        gpt_ref[rows, :] = -2.0 * n1 * share
        by_d2 = similar / d2
        gpp_ref[rows, :] = by_d2
        gm_ref[rows, :] = 2.0 * (
            mean_t * (n1 - n2) * share + mean_p * (similar / d1 - by_d2)
        )
        return carry

    lax.fori_loop(0, MAPS, similarity_row, 0, unroll=26)

    def radiance_row(y, carry):
        own = pl.ds(pl.multiple_of((y + ROWS) * 16, 16), 16)
        mapped = p_ref[own, :]
        wanted = t_ref[own, :]
        slope = along_columns(along_rows(gm_ref, y + 5), taps)
        slope = slope + 2.0 * mapped * along_columns(along_rows(gpp_ref, y + 5), taps)
        slope = slope + wanted * along_columns(along_rows(gpt_ref, y + 5), taps)
        slope = slope + 1.6 * (mapped - wanted)
        rest = 1.0 - mapped
        slope = slope * exposure * (rest * rest)
        for c in range(3):
            line = jnp.sum(jnp.where(of_colour[c], slope, 0.0), axis=0, keepdims=True)
            gimg_ref[pl.ds(c * ROWS + y, 1), :] = line
        return carry

    lax.fori_loop(0, ROWS, radiance_row, 0, unroll=16)

    spread_index = 16 * tile_row + (lane & 15)
    for c in range(3):
        for half in range(2):
            total = jnp.zeros((TILES, COLS), F32)
            for y in range(8):
                row = c * ROWS + half * 8 + y
                source = jnp.broadcast_to(gimg_ref[row : row + 1, :], (TILES, COLS))
                total = jnp.where((lane >> 4) == y, lane_gather(source, spread_index), total)
            gtile_ref[c * TILES : (c + 1) * TILES, 128 * half : 128 * half + 128] = total

    def composite_back(j, carry):
        ox, oy, a, b, c_ = [splat_row(f, j) for f in range(5)]
        colours = jnp.concatenate([splat_row(6 + c, j) for c in range(3)], axis=0)
        colour_top = colours.astype(BF16).astype(F32)
        slopes = jnp.concatenate(
            [gtile_ref[pl.ds(c * TILES + j, 1), :] for c in range(3)], axis=0
        )
        slope_top = slopes.astype(BF16).astype(F32)
        left = jnp.concatenate(
            [slope_top, slopes - slope_top, slope_top, jnp.zeros((7, LIST), F32)], axis=0
        )
        right = jnp.concatenate(
            [colour_top, colour_top, colours - colour_top, jnp.zeros((7, LIST), F32)], axis=0
        )
        deriv_ref[...] = dot(left.T.astype(BF16), right.astype(BF16))
        for y in range(16):
            rows = pixel_rows(j, y)
            value = deriv_ref[y * 16 : y * 16 + 16, :] * weight_ref[rows, :]
            weight_ref[rows, :] = value
            top, low = parts(value)
            pair_ref[y * 16 : y * 16 + 16, 0:LIST] = top
            pair_ref[y * 16 : y * 16 + 16, LIST : 2 * LIST] = low
        deriv_ref[...] = dot(pair_ref[...], later)
        dx = column_x - ox
        dxx = dx * dx
        zero = jnp.zeros((ROWS, LIST), F32)
        m0, mx, mxx = zero, zero, zero
        my, mxy, myy = zero, zero, zero
        for y in range(16):
            rows = pixel_rows(j, y)
            dy = (y + 0.5 - 8.0) - oy
            q = weight_ref[rows, :] - deriv_ref[y * 16 : y * 16 + 16, :] * cover_ref[rows, :]
            qx = q * dx
            qy = q * dy
            m0 = m0 + q
            mx = mx + qx
            my = my + qy
            mxx = mxx + q * dxx
            mxy = mxy + qx * dy
            myy = myy + qy * dy
        m0, mx, my, mxx, mxy, myy = [
            jnp.sum(m, axis=0, keepdims=True) for m in (m0, mx, my, mxx, mxy, myy)
        ]
        tile_rows = pl.ds(pl.multiple_of(j * 256, 256), 256)
        packed = left.astype(BF16)
        by_colour = dot(packed, top_ref[tile_rows, :]) + dot(packed, low_ref[tile_rows, :])
        rows = [
            a * mx + b * my,
            b * mx + c_ * my,
            -0.5 * mxx,
            -mxy,
            -0.5 * myy,
            m0 / splat_row(5, j),
        ] + [by_colour[c : c + 1] + by_colour[c + 3 : c + 4] for c in range(3)]
        lanes = pl.ds(pl.multiple_of(j * LIST, LIST), LIST)
        mask = slot_mask_ref[:, lanes]
        for f in range(SPLAT):
            top = rows[f].astype(BF16).astype(F32)
            for k, part in enumerate((top, rows[f] - top)):
                at = (k * SPLAT + f) * halves
                slot_left_ref[at : at + halves, :] = (
                    jnp.broadcast_to(part, (halves, LIST)).astype(BF16) * mask
                )
        update = dot_nt(slot_left_ref[...], slot_one_ref[:, lanes])

        @pl.when(j == 0)
        def _():
            slot_sum_ref[...] = update

        @pl.when(j > 0)
        def _():
            slot_sum_ref[...] = slot_sum_ref[...] + update

        return carry

    lax.fori_loop(0, TILES, composite_back, 0, unroll=8)

    count = SPLAT * halves
    for side in range(2):
        lanes = slice(side * COLS, side * COLS + COLS)
        sgrad_ref[side * count : (side + 1) * count, :] = (
            slot_sum_ref[0:count, lanes] + slot_sum_ref[count : 2 * count, lanes]
        )

    def send_back(step, carry):
        block = lax.rem(my_group + shift_of(step), groups)
        for i in range(group):
            peer = block * group + i
            first = (i % 2) * count + block * (group // 2) + i // 2
            back_ref[peer] = sgrad_ref[pl.ds(first, SPLAT, stride=halves), :]
        for i in range(group):
            peer = block * group + lax.rem(me + i, group)

            @pl.when(peer != me)
            def _():
                back_copy(peer, me).start()

        return carry

    lax.fori_loop(0, groups, send_back, 0)
    ret_ref[me] = back_ref[me]

    for i in range(1, nv):
        peer = lax.rem(mv + i, nv)
        camera_copy(peer, peer).wait_recv()
    for v in range(nv):
        angles = [jnp.broadcast_to(cams_ref[v, i : i + 1, :], (8, COLS)) for i in range(5)]
        turn = camera_rotation(angles)
        shift = [0.15 * angles[3], 0.15 * angles[4], 6.0]
        flat = [jnp.broadcast_to(turn[i][k], (8, COLS)) for i in range(3) for k in range(3)]
        flat += [sum((turn[i][k] * shift[i] for i in range(3))) for k in range(3)]
        for k in range(12):
            turn_ref[v, 8 * k : 8 * k + 8, :] = flat[k]

    def chunk_rows(f, i):
        return pl.ds(pl.multiple_of(f * HIGH + i * 8, 8), 8)

    def turn_of(v):
        flat = [turn_ref[v, 8 * k : 8 * k + 8, :] for k in range(12)]
        return [flat[0:3], flat[3:6], flat[6:9]], flat[9:12]

    def prepare(i, carry):
        position = [wide_ref[chunk_rows(f, i), :] for f in range(3)]
        stretch = [jnp.exp(wide_ref[chunk_rows(3 + k, i), :]) for k in range(3)]
        orient = quaternion_matrix(*[wide_ref[chunk_rows(6 + k, i), :] for k in range(4)])
        for v in range(nv):
            turn, away = turn_of(v)
            shift = [
                0.15 * jnp.broadcast_to(cams_ref[v, 3:4, :], (8, COLS)),
                0.15 * jnp.broadcast_to(cams_ref[v, 4:5, :], (8, COLS)),
                6.0,
            ]
            viewed = [
                sum((turn[r][k] * position[k] for k in range(3))) + shift[r] for r in range(3)
            ]
            inverse_z = 1.0 / viewed[2]
            slant_x = viewed[0] * inverse_z
            slant_y = viewed[1] * inverse_z
            focal_z = FOCAL * inverse_z
            row_x = [focal_z * (turn[0][k] - slant_x * turn[2][k]) for k in range(3)]
            row_y = [focal_z * (turn[1][k] - slant_y * turn[2][k]) for k in range(3)]
            image_x = [
                sum((row_x[r] * orient[r][k] for r in range(3))) * stretch[k] for k in range(3)
            ]
            image_y = [
                sum((row_y[r] * orient[r][k] for r in range(3))) * stretch[k] for k in range(3)
            ]
            cov_xx = sum((e * e for e in image_x)) + DILATE
            cov_yy = sum((e * e for e in image_y)) + DILATE
            cov_xy = sum((image_x[k] * image_y[k] for k in range(3)))
            share = 1.0 / (cov_xx * cov_yy - cov_xy * cov_xy)
            toward = [position[k] + away[k] for k in range(3)]
            closeness = 1.0 / jnp.sqrt(sum((e * e for e in toward)))
            direction = [e * closeness for e in toward]
            harmonic, pull = jax.vjp(harmonics, *direction)
            colours, moves = [], []
            for c in range(3):
                factors = [wide_ref[chunk_rows(11 + 3 * l + c, i), :] for l in range(16)]
                colour = jnp.exp(sum((harmonic[l] * factors[l] for l in range(16))))
                slope = pull(factors)
                along = sum((direction[k] * slope[k] for k in range(3)))
                reach = closeness * colour
                colours.append(colour)
                moves += [(slope[k] - direction[k] * along) * reach for k in range(3)]
            kept = (
                harmonic[1:]
                + colours
                + moves
                + [cov_yy * share, -cov_xy * share, cov_xx * share]
                + image_x
                + image_y
                + row_x
                + row_y
                + [inverse_z, slant_x, slant_y]
            )
            for k in range(JAC):
                jac_ref[v, chunk_rows(k, i), :] = kept[k]
        return carry

    lax.fori_loop(0, HIGH // 8, prepare, 0)

    own_sum_ref[...] = jnp.zeros_like(own_sum_ref)

    def add_group(step, carry):
        block = lax.rem(my_group + groups - shift_of(step), groups)
        for i in range(group):
            sender = block * group + i

            @pl.when(sender != me)
            def _():
                back_copy(sender, sender).wait_recv()

        for i in range(group):
            sender = block * group + i
            mask = own_mask_ref[:, pl.ds(pl.multiple_of(sender * COLS, COLS), COLS)]
            message = ret_ref[sender]
            top = message.astype(BF16).astype(F32)
            for k, part in enumerate((top, message - top)):
                for f in range(SPLAT):
                    at = (k * SPLAT + f) * 16
                    own_left_ref[at : at + 16, i * COLS : (i + 1) * COLS] = (
                        jnp.broadcast_to(part[f : f + 1], (16, COLS)).astype(BF16) * mask
                    )
        lanes = pl.ds(pl.multiple_of(block * group * COLS, COLS), group * COLS)
        own_sum_ref[...] = own_sum_ref[...] + dot_nt(own_left_ref[...], own_one_ref[:, lanes])
        return carry

    lax.fori_loop(0, groups, add_group, 0)
    for f in range(SPLAT):
        for side in range(2):
            lanes = slice(side * COLS, side * COLS + COLS)
            low = (SPLAT + f) * 16
            gall_ref[mv, pl.ds(f * HIGH + side, 16, stride=2), :] = (
                own_sum_ref[f * 16 : f * 16 + 16, lanes] + own_sum_ref[low : low + 16, lanes]
            )

    up = lax.rem(mv + 1, nv)
    down = lax.rem(mv + nv - 1, nv)
    half = SPLAT * HIGH // 2
    lower, upper = pl.ds(0, half), pl.ds(half, half)

    def view_copy(slot, rows, peer, k):
        return pltpu.make_async_remote_copy(
            src_ref=gall_ref.at[slot, rows],
            dst_ref=gall_ref.at[slot, rows],
            send_sem=v_send.at[k],
            recv_sem=v_recv.at[k],
            device_id={"view": peer},
            device_id_type=MESH,
        )

    sent = [view_copy(mv, lower, up, 0), view_copy(mv, upper, down, 1)]
    if nv > 2:
        sent += [view_copy(mv, upper, up, 2), view_copy(mv, lower, down, 3)]
    for copy in sent:
        copy.start()
    if nv > 2:
        view_copy(down, lower, up, 0).wait_recv()
        sent.append(view_copy(down, lower, up, 4))
        sent[-1].start()
        view_copy(up, upper, down, 1).wait_recv()
        sent.append(view_copy(up, upper, down, 5))
        sent[-1].start()
        view_copy(down, upper, up, 2).wait_recv()
        view_copy(up, lower, down, 3).wait_recv()
        far = lax.rem(mv + 2, nv)
        view_copy(far, lower, up, 4).wait_recv()
        view_copy(far, upper, down, 5).wait_recv()
    else:
        view_copy(down, lower, up, 0).wait_recv()
        view_copy(up, upper, down, 1).wait_recv()

    def pull_back(i, carry):
        stretch = [jnp.exp(wide_ref[chunk_rows(3 + k, i), :]) for k in range(3)]
        quaternion = [wide_ref[chunk_rows(6 + k, i), :] for k in range(4)]
        orient, pull = jax.vjp(quaternion_matrix, *quaternion)
        opacity = 1.0 / (1.0 + jnp.exp(-wide_ref[chunk_rows(10, i), :]))
        by_position, by_scale, by_orient, by_opacity = [0.0] * 3, [0.0] * 3, [[0.0] * 3] * 3, 0.0
        by_colour = []
        for v in range(nv):
            slope = [gall_ref[v, chunk_rows(f, i), :] for f in range(SPLAT)]

            def kept(k):
                return jac_ref[v, chunk_rows(k, i), :]

            turn, _ = turn_of(v)
            a, b, c = [kept(27 + k) for k in range(3)]
            image_x = [kept(30 + k) for k in range(3)]
            image_y = [kept(33 + k) for k in range(3)]
            row_x = [kept(36 + k) for k in range(3)]
            row_y = [kept(39 + k) for k in range(3)]
            inverse_z, slant_x, slant_y = [kept(42 + k) for k in range(3)]
            ab, bb, bc = a * b, b * b, b * c
            by_xx = -(a * a * slope[2] + ab * slope[3] + bb * slope[4])
            by_yy = -(bb * slope[2] + bc * slope[3] + c * c * slope[4])
            by_xy = -(2 * ab * slope[2] + (bb + a * c) * slope[3] + 2 * bc * slope[4])
            by_x = [2 * by_xx * image_x[k] + by_xy * image_y[k] for k in range(3)]
            by_y = [2 * by_yy * image_y[k] + by_xy * image_x[k] for k in range(3)]
            by_scale = [
                by_scale[k] + by_x[k] * image_x[k] + by_y[k] * image_y[k] for k in range(3)
            ]
            by_x = [by_x[k] * stretch[k] for k in range(3)]
            by_y = [by_y[k] * stretch[k] for k in range(3)]
            by_orient = [
                [by_orient[r][k] + row_x[r] * by_x[k] + row_y[r] * by_y[k] for k in range(3)]
                for r in range(3)
            ]
            by_row_x = [sum((orient[r][k] * by_x[k] for k in range(3))) for r in range(3)]
            by_row_y = [sum((orient[r][k] * by_y[k] for k in range(3))) for r in range(3)]
            pulled = sum((by_row_x[r] * row_x[r] + by_row_y[r] * row_y[r] for r in range(3)))
            depth_x = sum((by_row_x[r] * turn[2][r] for r in range(3)))
            depth_y = sum((by_row_y[r] * turn[2][r] for r in range(3)))
            by_slant_x = FOCAL * (slope[0] - inverse_z * depth_x)
            by_slant_y = FOCAL * (slope[1] - inverse_z * depth_y)
            by_viewed = [
                by_slant_x * inverse_z,
                by_slant_y * inverse_z,
                -inverse_z * (pulled + by_slant_x * slant_x + by_slant_y * slant_y),
            ]
            by_position = [
                by_position[k]
                + sum((turn[r][k] * by_viewed[r] for r in range(3)))
                + sum((slope[6 + c_] * kept(18 + 3 * c_ + k) for c_ in range(3)))
                for k in range(3)
            ]
            by_opacity = by_opacity + slope[5]
            by_colour.append([slope[6 + c_] * kept(15 + c_) for c_ in range(3)])
        by_quaternion = pull(by_orient)
        grads = (
            by_position + by_scale + list(by_quaternion) + [by_opacity * opacity * (1.0 - opacity)]
        )
        for f in range(11):
            wide_grad_ref[chunk_rows(f, i), :] = grads[f]
        for l in range(16):
            for c_ in range(3):
                if l == 0:
                    total = SH_C0 * sum((by_colour[v][c_] for v in range(nv)))
                else:
                    total = sum(
                        (by_colour[v][c_] * jac_ref[v, chunk_rows(l - 1, i), :] for v in range(nv))
                    )
                wide_grad_ref[chunk_rows(11 + 3 * l + c_, i), :] = total
        return carry

    lax.fori_loop(0, HIGH // 8, pull_back, 0)

    def drain(i, carry):
        peer = lax.rem(me + i, n)
        forward_copy(peer, me).wait_send()
        back_copy(peer, me).wait_send()
        return carry

    lax.fori_loop(1, n, drain, 0)

    @pl.when(me < n - 1)
    def _():
        target_copy(after, 0).wait_send()
        strip_copy(after, 0).wait_send()

    @pl.when(me > 0)
    def _():
        target_copy(before, 1).wait_send()
        strip_copy(before, 1).wait_send()

    for copy in sent:
        copy.wait_send()
    for i in range(1, nv):
        camera_copy(lax.rem(mv + i, nv), mv).wait_send()


def row_order_kernel(wide_hbm, rad_hbm, grad_ref, radiance_ref, wide_ref, sems):
    groups = [(first, min(8, FEAT - first)) for first in range(0, FEAT, 8)]
    loads = [pltpu.make_async_copy(rad_hbm, radiance_ref, sems.at[len(groups)])]
    for g, (first, size) in enumerate(groups):
        rows = pl.ds(first * HIGH, size * HIGH)
        loads.append(pltpu.make_async_copy(wide_hbm.at[rows], wide_ref.at[rows], sems.at[g]))
    for load in loads:
        load.start()
    for g, (first, size) in enumerate(groups):
        loads[g + 1].wait()
        for h in range(HIGH):
            grad_ref[first : first + size, h * COLS : (h + 1) * COLS] = wide_ref[
                pl.ds(first * HIGH + h, size, stride=HIGH), :
            ]
    loads[0].wait()


def shards(n, nv, gaussians, send_index, tile_list, tile_length, camera, exposure, target):
    vmem = pl.BlockSpec(memory_space=pltpu.VMEM)
    halves = max(16, n // 2)
    group = min(8, n)

    def scratch(shape, dtype=F32):
        return pltpu.VMEM(shape, dtype)

    pixels = TILES * 256
    scratches = [
        scratch((FEAT, HIGH * COLS)),
        scratch((1, n, COLS), I32),
        scratch((1, TILES, LIST), I32),
        scratch((1, TILES), I32),
        scratch((1, 5)),
        scratch((1, 5)),
        scratch((1, CHANNELS, ROWS, COLS)),
        scratch((64 * HIGH, COLS)),
        scratch((SPLAT * HIGH, COLS)),
        scratch((SPLAT * group, COLS)),
        scratch((n, SPLAT, COLS)),
        scratch((n, SPLAT, COLS)),
        scratch(((SPLAT + 1) * TILES, LIST)),
        scratch((pixels, LIST)),
        scratch((pixels, LIST)),
        scratch((pixels, LIST), BF16),
        scratch((pixels, LIST), BF16),
        scratch((LIST, 2 * LIST), BF16),
        scratch((LIST, LIST)),
        scratch((3 * TILES, LIST)),
        scratch((3, 3, ROWS, COLS)),
        scratch((2, CHANNELS, ROWS, COLS)),
        scratch((48 * 16, COLS)),
        scratch((48 * 16, COLS)),
        scratch((48 * 16, COLS)),
        scratch((48 * 16, COLS)),
        scratch((48 * 16, COLS)),
        scratch((MAPS * 16, COLS)),
        scratch((MAPS * 16, COLS)),
        scratch((MAPS * 16, COLS)),
        scratch((MAPS * 16, COLS)),
        scratch((MAPS * 16, COLS)),
        scratch((3 * ROWS, COLS)),
        scratch((3 * TILES, LIST)),
        scratch((2 * SPLAT * halves, COLS)),
        scratch((256, TILES * LIST), BF16),
        scratch((halves, TILES * LIST), BF16),
        scratch((256, n * COLS), BF16),
        scratch((16, n * COLS), BF16),
        scratch((2 * SPLAT * halves, LIST), BF16),
        scratch((2 * SPLAT * halves, 256)),
        scratch((n, SPLAT, COLS)),
        scratch((n, SPLAT, COLS)),
        scratch((2 * SPLAT * 16, group * COLS), BF16),
        scratch((2 * SPLAT * 16, 256)),
        scratch((nv, SPLAT * HIGH, COLS)),
        scratch((nv, 8, COLS)),
        scratch((nv, 12 * 8, COLS)),
        scratch((nv, JAC * HIGH, COLS)),
    ]
    sems = [pltpu.SemaphoreType.DMA((k,)) for k in (n, n, n, n, 2, 2, 2, 2, 6, 6, nv, nv, 7)]
    wide_grad, strip = pl.pallas_call(
        functools.partial(step_kernel, n, nv),
        out_shape=(
            jax.ShapeDtypeStruct((FEAT * HIGH, COLS), F32),
            jax.ShapeDtypeStruct((1, 3, ROWS, COLS), F32),
        ),
        in_specs=[pl.BlockSpec(memory_space=pl.ANY)] * 7,
        out_specs=(vmem, vmem),
        scratch_shapes=scratches + sems,
        compiler_params=pltpu.CompilerParams(
            collective_id=0, has_side_effects=True, vmem_limit_bytes=56 * 2**20
        ),
        name="splat_step",
    )(gaussians, send_index, tile_list, tile_length, camera, exposure, target)
    return pl.pallas_call(
        row_order_kernel,
        out_shape=(
            jax.ShapeDtypeStruct((FEAT, HIGH * COLS), F32),
            jax.ShapeDtypeStruct((1, 3, ROWS, COLS), F32),
        ),
        in_specs=[pl.BlockSpec(memory_space=pl.ANY)] * 2,
        out_specs=(vmem, vmem),
        scratch_shapes=[scratch((FEAT * HIGH, COLS)), pltpu.SemaphoreType.DMA((9,))],
        name="row_order",
    )(wide_grad, strip)


def solution(mesh):
    placed = (
        P(None, "gs"),
        P("view", "gs", None),
        P("view", "gs", None),
        P("view", "gs"),
        P("view", None),
        P("view", None),
        P("view", None, "gs", None),
    )
    return jax.shard_map(
        functools.partial(shards, mesh.shape["gs"], mesh.shape["view"]),
        mesh=mesh,
        in_specs=placed,
        out_specs=(P(None, "gs"), P("view", None, "gs", None)),
        check_vma=False,
    )
```

```python
import functools

import jax
import jax.numpy as jnp
import numpy as np
from jax import lax
from jax.experimental import pallas as pl
from jax.experimental.pallas import tpu as pltpu
from jax.sharding import PartitionSpec as P

MESH = pl.DeviceIdType.MESH
F32, BF16, I32 = jnp.float32, jnp.bfloat16, jnp.int32

FOCAL = 16.0
DILATE = 0.3
SH_C0 = 0.28209479177387814
SH_C1 = 0.4886025119029199
SH_C2 = [
    1.0925484305920792,
    -1.0925484305920792,
    0.31539156525252005,
    -1.0925484305920792,
    0.5462742152960396,
]
SH_C3 = [
    -0.5900435899266435,
    2.890611442640554,
    -0.4570457994644658,
    0.3731763325901154,
    -0.4570457994644658,
    1.445305721320277,
    -0.5900435899266435,
]
WINDOW_RAW = np.exp(-((np.arange(11) - 5.0) ** 2) / 4.5)
WINDOW = [float(v) for v in WINDOW_RAW / WINDOW_RAW.sum()]
FLOOR_MEAN = 0.0001
FLOOR_VAR = 0.0009

FEAT = 59
SPLAT = 9
HIGH = 32
TILES = 8
LIST = 256
ROWS = 16
COLS = 128
CHANNELS = 15
FIRST = 11
JAC = 45
MAPS = 26


def product3(left, right):
    return [[sum((left[i][k] * right[k][j] for k in range(3))) for j in range(3)] for i in range(3)]


def camera_rotation(camera):
    yaw_cos, yaw_sin = (jnp.cos(camera[0]), jnp.sin(camera[0]))
    pitch_cos, pitch_sin = (jnp.cos(camera[1]), jnp.sin(camera[1]))
    roll_cos, roll_sin = (jnp.cos(camera[2]), jnp.sin(camera[2]))
    about_z = [[yaw_cos, -yaw_sin, 0.0], [yaw_sin, yaw_cos, 0.0], [0.0, 0.0, 1.0]]
    about_y = [[pitch_cos, 0.0, pitch_sin], [0.0, 1.0, 0.0], [-pitch_sin, 0.0, pitch_cos]]
    about_x = [[1.0, 0.0, 0.0], [0.0, roll_cos, -roll_sin], [0.0, roll_sin, roll_cos]]
    return product3(product3(about_z, about_y), about_x)


def quaternion_matrix(q0, q1, q2, q3):
    scale = 1.0 / jnp.sqrt(q0 * q0 + q1 * q1 + q2 * q2 + q3 * q3)
    w, x, y, z = (q0 * scale, q1 * scale, q2 * scale, q3 * scale)
    return [
        [1 - 2 * (y * y + z * z), 2 * (x * y - w * z), 2 * (x * z + w * y)],
        [2 * (x * y + w * z), 1 - 2 * (x * x + z * z), 2 * (y * z - w * x)],
        [2 * (x * z - w * y), 2 * (y * z + w * x), 1 - 2 * (x * x + y * y)],
    ]


def harmonics(x, y, z):
    xx, yy, zz = (x * x, y * y, z * z)
    return [
        SH_C0 + 0.0 * x,
        -SH_C1 * y,
        SH_C1 * z,
        -SH_C1 * x,
        SH_C2[0] * x * y,
        SH_C2[1] * y * z,
        SH_C2[2] * (2 * zz - xx - yy),
        SH_C2[3] * x * z,
        SH_C2[4] * (xx - yy),
        SH_C3[0] * y * (3 * xx - yy),
        SH_C3[1] * x * y * z,
        SH_C3[2] * y * (4 * zz - xx - yy),
        SH_C3[3] * z * (2 * zz - 3 * xx - 3 * yy),
        SH_C3[4] * x * (4 * zz - xx - yy),
        SH_C3[5] * z * (xx - yy),
        SH_C3[6] * x * (xx - 3 * yy),
    ]


def project(params, camera, rotation):
    translation = [0.15 * camera[3], 0.15 * camera[4], 6.0]
    position = [params[i] for i in range(3)]
    viewed = [
        sum((rotation[i][j] * position[j] for j in range(3))) + translation[i] for i in range(3)
    ]
    inverse_z = 1.0 / viewed[2]
    row_x = [
        FOCAL * inverse_z * (rotation[0][k] - viewed[0] * inverse_z * rotation[2][k])
        for k in range(3)
    ]
    row_y = [
        FOCAL * inverse_z * (rotation[1][k] - viewed[1] * inverse_z * rotation[2][k])
        for k in range(3)
    ]
    orient = quaternion_matrix(params[6], params[7], params[8], params[9])
    stretch = [jnp.exp(params[3 + k]) for k in range(3)]
    image_x = [sum((row_x[i] * orient[i][k] for i in range(3))) * stretch[k] for k in range(3)]
    image_y = [sum((row_y[i] * orient[i][k] for i in range(3))) * stretch[k] for k in range(3)]
    cov_xx = sum((e * e for e in image_x)) + DILATE
    cov_yy = sum((e * e for e in image_y)) + DILATE
    cov_xy = sum((image_x[k] * image_y[k] for k in range(3)))
    share = 1.0 / (cov_xx * cov_yy - cov_xy * cov_xy)
    opacity = 1.0 / (1.0 + jnp.exp(-params[10]))
    toward = [
        position[k] + sum((rotation[i][k] * translation[i] for i in range(3))) for k in range(3)
    ]
    closeness = 1.0 / jnp.sqrt(sum((e * e for e in toward)))
    harmonic = harmonics(*[e * closeness for e in toward])
    colour = [
        jnp.exp(sum((harmonic[l] * params[11 + 3 * l + c] for l in range(16)))) for c in range(3)
    ]
    return [
        FOCAL * viewed[0] * inverse_z,
        FOCAL * viewed[1] * inverse_z,
        cov_yy * share,
        -cov_xy * share,
        cov_xx * share,
        opacity,
    ] + colour


def iota(shape, axis):
    return lax.broadcasted_iota(I32, shape, axis)


def lane_gather(values, index):
    return jnp.take_along_axis(values, index, axis=1, mode="promise_in_bounds")


def parts(values):
    top = values.astype(BF16)
    return top, (values - top.astype(F32)).astype(BF16)


def dot(left, right):
    return jnp.dot(left, right, preferred_element_type=F32)


def dot_nt(left, right):
    return lax.dot_general(left, right, (((1,), (1,)), ((), ())), preferred_element_type=F32)


def spread_rows(gauss_ref, wide_ref):
    def one(h, carry):
        lanes = pl.ds(pl.multiple_of(h * COLS, COLS), COLS)
        for first in range(0, FEAT, 8):
            count = min(8, FEAT - first)
            wide_ref[pl.ds(first * HIGH + h, count, stride=HIGH), :] = gauss_ref[first : first + count, lanes]
        return carry

    lax.fori_loop(0, HIGH, one, 0)


def window_band():
    distance = iota((COLS, COLS), 0) - iota((COLS, COLS), 1)
    band = jnp.zeros((COLS, COLS), F32)
    for i in range(11):
        band = jnp.where(distance == i - 5, WINDOW[i], band)
    return band


def band_factors():
    band = window_band()
    top = band.astype(BF16).astype(F32)
    middle = (band - top).astype(BF16).astype(F32)
    low = band - top - middle
    none = jnp.zeros((COLS, COLS), F32)
    left = jnp.concatenate([top, top, top, low], axis=0)
    right = jnp.concatenate([middle, middle, none, none], axis=0)
    return jnp.concatenate([left, right], axis=1).astype(BF16)


def split_three(values, place_ref, rows):
    top = values.astype(BF16)
    rest = values - top.astype(F32)
    middle = rest.astype(BF16)
    place_ref[rows, 0:COLS] = top
    place_ref[rows, COLS : 2 * COLS] = middle
    place_ref[rows, 2 * COLS : 3 * COLS] = (rest - middle.astype(F32)).astype(BF16)
    place_ref[rows, 3 * COLS : 4 * COLS] = top


def along_rows(ref, row):
    def at(i):
        return ref[pl.ds(pl.multiple_of((row + i) * 16, 16), 16), :]

    total = WINDOW[5] * at(0)
    for i in range(1, 6):
        total = total + WINDOW[5 + i] * (at(i) + at(-i))
    return total


def step_kernel(
    n,
    nv,
    gauss_hbm,
    send_hbm,
    list_hbm,
    len_hbm,
    cam_hbm,
    expo_hbm,
    target_hbm,
    wide_grad_ref,
    rad_ref,
    gauss_ref,
    send_ref,
    list_ref,
    len_ref,
    cam_ref,
    expo_ref,
    target_ref,
    wide_ref,
    table_ref,
    pick_ref,
    out_ref,
    recv_ref,
    splat_ref,
    cover_ref,
    weight_ref,
    top_ref,
    low_ref,
    pair_ref,
    deriv_ref,
    tile_rad_ref,
    strips_ref,
    edge_ref,
    t_ref,
    tt_ref,
    p_ref,
    pp_ref,
    pt_ref,
    mt_ref,
    btt_ref,
    gm_ref,
    gpp_ref,
    gpt_ref,
    bm_ref,
    bpp_ref,
    bpt_ref,
    split_ref,
    gimg_ref,
    gtile_ref,
    sgrad_ref,
    slot_one_ref,
    slot_mask_ref,
    own_one_ref,
    own_mask_ref,
    slot_left_ref,
    slot_sum_ref,
    back_ref,
    ret_ref,
    own_left_ref,
    own_sum_ref,
    gall_ref,
    cams_ref,
    turn_ref,
    jac_ref,
    f_send,
    f_recv,
    b_send,
    b_recv,
    t_send,
    t_recv,
    h_send,
    h_recv,
    v_send,
    v_recv,
    c_send,
    c_recv,
    in_sem,
):
    me = lax.axis_index("gs")
    mv = lax.axis_index("view")
    after = lax.rem(me + 1, n)
    before = lax.rem(me + n - 1, n)
    group = min(8, n)
    groups = n // group
    halves = slot_mask_ref.shape[0]

    loads = [
        pltpu.make_async_copy(source, place, in_sem.at[i])
        for i, (source, place) in enumerate(
            [
                (gauss_hbm, gauss_ref),
                (cam_hbm, cam_ref),
                (send_hbm, send_ref),
                (target_hbm, target_ref),
                (list_hbm, list_ref),
                (len_hbm, len_ref),
                (expo_hbm, expo_ref),
            ]
        )
    ]
    for load in loads:
        load.start()

    barrier = pltpu.get_barrier_semaphore()

    def greet(i, carry):
        pl.semaphore_signal(
            barrier, inc=1, device_id={"gs": lax.rem(me + i, n)}, device_id_type=MESH
        )
        return carry

    lax.fori_loop(1, n, greet, 0)
    for i in range(1, nv):
        pl.semaphore_signal(
            barrier, inc=1, device_id={"view": lax.rem(mv + i, nv)}, device_id_type=MESH
        )

    loads[0].wait()
    loads[1].wait()
    spread_rows(gauss_ref, wide_ref)
    camera = [jnp.broadcast_to(cam_ref[0:1, i : i + 1], (8, COLS)) for i in range(5)]
    rotation = camera_rotation(camera)

    def project_rows(i, carry):
        rows = [
            wide_ref[pl.ds(pl.multiple_of(f * HIGH + i * 8, 8), 8), :] for f in range(FEAT)
        ]
        for f, value in enumerate(project(rows, camera, rotation)):
            table_ref[pl.ds(pl.multiple_of(f * HIGH + i * 8, 8), 8), :] = value
        return carry

    lax.fori_loop(0, HIGH // 8, project_rows, 0, unroll=4)
    cams_ref[mv] = jnp.concatenate(
        [camera[i][0:1] for i in range(5)] + [jnp.zeros((3, COLS), F32)], axis=0
    )

    for load in loads[2:]:
        load.wait()
    pl.semaphore_wait(barrier, n - 1 + nv - 1)

    def target_copy(peer, side):
        return pltpu.make_async_remote_copy(
            src_ref=target_ref.at[0],
            dst_ref=edge_ref.at[side],
            send_sem=t_send.at[side],
            recv_sem=t_recv.at[side],
            device_id={"gs": peer},
            device_id_type=MESH,
        )

    def strip_copy(peer, side):
        return pltpu.make_async_remote_copy(
            src_ref=strips_ref.at[1],
            dst_ref=strips_ref.at[2 * side],
            send_sem=h_send.at[side],
            recv_sem=h_recv.at[side],
            device_id={"gs": peer},
            device_id_type=MESH,
        )

    def camera_copy(peer, slot):
        return pltpu.make_async_remote_copy(
            src_ref=cams_ref.at[mv],
            dst_ref=cams_ref.at[slot],
            send_sem=c_send.at[peer],
            recv_sem=c_recv.at[slot],
            device_id={"view": peer},
            device_id_type=MESH,
        )

    def forward_copy(peer, slot):
        return pltpu.make_async_remote_copy(
            src_ref=out_ref.at[peer],
            dst_ref=recv_ref.at[slot],
            send_sem=f_send.at[peer],
            recv_sem=f_recv.at[slot],
            device_id={"gs": peer},
            device_id_type=MESH,
        )

    def back_copy(peer, slot):
        return pltpu.make_async_remote_copy(
            src_ref=back_ref.at[peer],
            dst_ref=ret_ref.at[slot],
            send_sem=b_send.at[peer],
            recv_sem=b_recv.at[slot],
            device_id={"gs": peer},
            device_id_type=MESH,
        )

    my_group = me // group

    def shift_of(step):
        reach = groups // 2 - (step + 1) // 2
        return jnp.where(step % 2 == 1, reach, lax.rem(groups - reach, groups))

    def gather_group(step, carry):
        block = lax.rem(my_group + shift_of(step), groups)
        index = send_ref[0, pl.ds(pl.multiple_of(block * group, group), group), :]
        high = index >> 7
        low = index & 127

        def one(h, totals):
            chosen = high == h
            new = []
            for f in range(SPLAT):
                row = jnp.broadcast_to(table_ref[pl.ds(f * HIGH + h, 1), :], (group, COLS))
                new.append(jnp.where(chosen, lane_gather(row, low), totals[f]))
            return tuple(new)

        totals = lax.fori_loop(
            0, HIGH, one, tuple(jnp.zeros((group, COLS), F32) for _ in range(SPLAT)), unroll=8
        )
        for f in range(SPLAT):
            pick_ref[f * group : (f + 1) * group, :] = totals[f]
        for i in range(group):
            peer = block * group + i
            out_ref[peer] = pick_ref[pl.ds(i, SPLAT, stride=group), :]
        for i in range(group):
            peer = block * group + lax.rem(me + i, group)

            @pl.when(peer != me)
            def _():
                forward_copy(peer, me).start()

        return carry

    lax.fori_loop(0, groups, gather_group, 0)
    recv_ref[me] = out_ref[me]
    @pl.when(me < n - 1)
    def _():
        target_copy(after, 0).start()

    @pl.when(me > 0)
    def _():
        target_copy(before, 1).start()

    for i in range(1, nv):
        camera_copy(lax.rem(mv + i, nv), mv).start()

    def own_factors(r, carry):
        index = send_ref[0, pl.ds(r, 1), :]
        lanes = pl.ds(pl.multiple_of(r * COLS, COLS), COLS)
        own_one_ref[:, lanes] = jnp.where(iota((256, COLS), 0) == (index & 255), 1.0, 0.0).astype(BF16)
        own_mask_ref[:, lanes] = jnp.where(iota((16, COLS), 0) == (index >> 8), 1.0, 0.0).astype(BF16)
        return carry

    lax.fori_loop(0, n, own_factors, 0, unroll=8)

    def slot_factors(j, carry):
        index = list_ref[0, pl.ds(j, 1), :]
        lanes = pl.ds(pl.multiple_of(j * LIST, LIST), LIST)
        slot_one_ref[:, lanes] = jnp.where(iota((256, LIST), 0) == (index & 255), 1.0, 0.0).astype(BF16)
        slot_mask_ref[:, lanes] = jnp.where(iota((halves, LIST), 0) == (index >> 8), 1.0, 0.0).astype(
            BF16
        )
        return carry

    lax.fori_loop(0, TILES, slot_factors, 0, unroll=8)

    owner = [list_ref[0, :, 128 * h : 128 * h + 128] >> 7 for h in range(2)]
    place = [list_ref[0, :, 128 * h : 128 * h + 128] & 127 for h in range(2)]

    def take_group(step, totals):
        block = lax.rem(my_group + groups - shift_of(step), groups)
        for i in range(group):
            sender = block * group + i

            @pl.when(sender != me)
            def _():
                forward_copy(sender, sender).wait_recv()

        for i in range(group):
            sender = block * group + i
            chosen = [owner[h] == sender for h in range(2)]
            new = []
            for f in range(SPLAT):
                row = jnp.broadcast_to(recv_ref[sender, f : f + 1, :], (TILES, COLS))
                for h in range(2):
                    new.append(
                        jnp.where(chosen[h], lane_gather(row, place[h]), totals[2 * f + h])
                    )
            totals = tuple(new)
        return totals

    totals = lax.fori_loop(
        0, groups, take_group, tuple(jnp.zeros((TILES, COLS), F32) for _ in range(2 * SPLAT))
    )
    tile_row = iota((TILES, COLS), 0)
    length = jnp.zeros((TILES, COLS), I32)
    for j in range(TILES):
        length = jnp.where(tile_row == j, len_ref[0:1, j : j + 1], length)
    for f in range(SPLAT):
        for h in range(2):
            splat_ref[f * TILES : (f + 1) * TILES, 128 * h : 128 * h + 128] = totals[2 * f + h]
    for h in range(2):
        active = (iota((TILES, COLS), 1) + 128 * h) < length
        splat_ref[SPLAT * TILES : (SPLAT + 1) * TILES, 128 * h : 128 * h + 128] = jnp.where(
            active, totals[2 * 5 + h], 0.0
        )

    def splat_row(f, j):
        return splat_ref[pl.ds(f * TILES + j, 1), :]

    column_x = iota((ROWS, LIST), 0).astype(F32) + (0.5 - 8.0)
    first_of = iota((LIST, LIST), 0)
    then_of = iota((LIST, LIST), 1)
    earlier = jnp.where(first_of < then_of, 1.0, 0.0).astype(BF16)
    earlier = jnp.concatenate([earlier, earlier], axis=0)
    later = jnp.where(first_of > then_of, 1.0, 0.0).astype(BF16)
    later = jnp.concatenate([later, later], axis=0)

    def pixel_rows(j, y):
        return pl.ds(pl.multiple_of(j * 256 + y * 16, 16), 16)

    def composite(j, carry):
        ox, oy, a, b, c = [splat_row(f, j) for f in range(5)]
        opacity = splat_row(SPLAT, j)
        dx = column_x - ox
        square_part = (-0.5 * a) * dx * dx
        cross_part = (-b) * dx
        for y in range(16):
            dy = (y + 0.5 - 8.0) - oy
            power = square_part + dy * cross_part + (-0.5 * c) * dy * dy
            cover = opacity * jnp.exp(power)
            cover_ref[pixel_rows(j, y), :] = cover
            top, low = parts(jnp.log(1.0 - cover))
            pair_ref[y * 16 : y * 16 + 16, 0:LIST] = top
            pair_ref[y * 16 : y * 16 + 16, LIST : 2 * LIST] = low
        deriv_ref[...] = dot(pair_ref[...], earlier)
        for y in range(16):
            rows = pixel_rows(j, y)
            cover = cover_ref[rows, :]
            weight = cover * jnp.exp(deriv_ref[y * 16 : y * 16 + 16, :])
            cover_ref[rows, :] = cover / (1.0 - cover)
            weight_ref[rows, :] = weight
            top, low = parts(weight)
            top_ref[rows, :] = top
            low_ref[rows, :] = low
        tile_rows = pl.ds(pl.multiple_of(j * 256, 256), 256)
        colours = jnp.concatenate([splat_row(6 + c, j) for c in range(3)], axis=0)
        colour_top = colours.astype(BF16).astype(F32)
        packed = jnp.concatenate(
            [colour_top, colours - colour_top, jnp.zeros((10, LIST), F32)], axis=0
        ).astype(BF16)
        seen = dot_nt(packed, top_ref[tile_rows, :]) + dot_nt(packed, low_ref[tile_rows, :])
        for c in range(3):
            tile_rad_ref[pl.ds(c * TILES + j, 1), :] = seen[c : c + 1] + seen[c + 3 : c + 4]
        return carry

    lax.fori_loop(0, TILES, composite, 0, unroll=8)

    lane = iota((TILES, COLS), 1)
    in_tile = (lane >> 4) == tile_row
    for y in range(16):
        index = (lane & 15) + 16 * (y % 8)
        for c in range(3):
            half = 128 * (y // 8)
            source = tile_rad_ref[c * TILES : (c + 1) * TILES, half : half + 128]
            line = jnp.sum(jnp.where(in_tile, lane_gather(source, index), 0.0), axis=0, keepdims=True)
            strips_ref[1, c, y : y + 1, :] = line

    @pl.when(me < n - 1)
    def _():
        strip_copy(after, 0).start()

    @pl.when(me > 0)
    def _():
        strip_copy(before, 1).start()

    @pl.when(me == 0)
    def _():
        edge_ref[0] = jnp.zeros((CHANNELS, ROWS, COLS), F32)
        strips_ref[0] = jnp.zeros((3, ROWS, COLS), F32)

    @pl.when(me == n - 1)
    def _():
        edge_ref[1] = jnp.zeros((CHANNELS, ROWS, COLS), F32)
        strips_ref[2] = jnp.zeros((3, ROWS, COLS), F32)

    @pl.when(me > 0)
    def _():
        target_copy(before, 0).wait_recv()

    @pl.when(me < n - 1)
    def _():
        target_copy(after, 1).wait_recv()

    for strip in range(3):
        for ch in range(16):
            if ch == CHANNELS:
                value = jnp.zeros((ROWS, COLS), F32)
            elif strip == 1:
                value = target_ref[0, ch]
            else:
                value = edge_ref[strip // 2, ch]
            t_ref[pl.ds(strip * 256 + ch, ROWS, stride=16), :] = value

    band = band_factors()

    def square_target(row, carry):
        rows = pl.ds(pl.multiple_of(row * 16, 16), 16)
        tt_ref[rows, :] = t_ref[rows, :] * t_ref[rows, :]
        return carry

    lax.fori_loop(FIRST - 5, FIRST + MAPS + 5, square_target, 0, unroll=4)

    def target_maps(i, carry):
        rows = pl.ds(pl.multiple_of(i * 16, 16), 16)
        second = pl.ds(pl.multiple_of((MAPS + i) * 16, 16), 16)
        split_three(along_rows(t_ref, FIRST + i), split_ref, rows)
        split_three(along_rows(tt_ref, FIRST + i), split_ref, second)
        return carry

    lax.fori_loop(0, MAPS, target_maps, 0, unroll=MAPS)
    count = MAPS * 16
    for k, maps in enumerate((mt_ref, btt_ref)):
        both = dot(split_ref[k * count : (k + 1) * count, :], band)
        maps[...] = both[:, 0:COLS] + both[:, COLS:]

    rad_ref[0] = strips_ref[1]

    channel = iota((16, COLS), 0)
    of_colour = [lax.rem(channel, 3) == c for c in range(3)]
    bracket = channel // 3
    exposure = jnp.zeros((16, COLS), F32)
    for b in range(5):
        exposure = jnp.where(bracket == b, expo_ref[0:1, b : b + 1], exposure)

    def tone(row, carry):
        strip = row // ROWS
        y = lax.rem(row, ROWS)
        lines = [strips_ref[strip, c, pl.ds(y, 1), :] for c in range(3)]
        scaled = exposure * jnp.where(
            of_colour[0], lines[0], jnp.where(of_colour[1], lines[1], lines[2])
        )
        mapped = scaled / (1.0 + scaled)
        rows = pl.ds(pl.multiple_of(row * 16, 16), 16)
        p_ref[rows, :] = mapped
        pp_ref[rows, :] = mapped * mapped
        pt_ref[rows, :] = mapped * t_ref[rows, :]
        return carry

    lax.fori_loop(ROWS, 2 * ROWS, tone, 0, unroll=ROWS)

    @pl.when(me > 0)
    def _():
        strip_copy(before, 0).wait_recv()

    @pl.when(me < n - 1)
    def _():
        strip_copy(after, 1).wait_recv()

    lax.fori_loop(FIRST - 5, ROWS, tone, 0, unroll=10)
    lax.fori_loop(2 * ROWS, FIRST + MAPS + 5, tone, 0, unroll=10)

    def filter_rows(i, carry):
        rows = pl.ds(pl.multiple_of(i * 16, 16), 16)
        second = pl.ds(pl.multiple_of((MAPS + i) * 16, 16), 16)
        third = pl.ds(pl.multiple_of((2 * MAPS + i) * 16, 16), 16)
        split_three(along_rows(p_ref, FIRST + i), split_ref, rows)
        split_three(along_rows(pp_ref, FIRST + i), split_ref, second)
        split_three(along_rows(pt_ref, FIRST + i), split_ref, third)
        return carry

    lax.fori_loop(0, MAPS, filter_rows, 0, unroll=MAPS)
    for k, maps in enumerate((gm_ref, gpp_ref, gpt_ref)):
        both = dot(split_ref[k * count : (k + 1) * count, :], band)
        maps[...] = both[:, 0:COLS] + both[:, COLS:]

    def similarity_row(i, carry):
        row = FIRST + i
        rows = pl.ds(pl.multiple_of(i * 16, 16), 16)
        mean_p = gm_ref[rows, :]
        square_p = gpp_ref[rows, :]
        cross = gpt_ref[rows, :]
        mean_t = mt_ref[rows, :]
        both = mean_p * mean_t
        n1 = 2.0 * both + FLOOR_MEAN
        n2 = 2.0 * (cross - both) + FLOOR_VAR
        d1 = mean_p * mean_p + mean_t * mean_t + FLOOR_MEAN
        d2 = (square_p - mean_p * mean_p) + (btt_ref[rows, :] - mean_t * mean_t) + FLOOR_VAR
        inside = ((row >= ROWS) | (me > 0)) & ((row < 2 * ROWS) | (me < n - 1))
        share = jnp.where(inside, 1.0, 0.0) / (d1 * d2)
        similar = n1 * n2 * share
        gpt_ref[rows, :] = -2.0 * n1 * share
        by_d2 = similar / d2
        gpp_ref[rows, :] = by_d2
        gm_ref[rows, :] = 2.0 * (
            mean_t * (n1 - n2) * share + mean_p * (similar / d1 - by_d2)
        )
        return carry

    lax.fori_loop(0, MAPS, similarity_row, 0, unroll=26)

    def filter_back(y, carry):
        for k, source in enumerate((gm_ref, gpp_ref, gpt_ref)):
            rows = pl.ds(pl.multiple_of((k * ROWS + y) * 16, 16), 16)
            split_three(along_rows(source, y + 5), split_ref, rows)
        return carry

    lax.fori_loop(0, ROWS, filter_back, 0, unroll=ROWS)
    for k, maps in enumerate((bm_ref, bpp_ref, bpt_ref)):
        both = dot(split_ref[k * ROWS * 16 : (k + 1) * ROWS * 16, :], band)
        maps[...] = both[:, 0:COLS] + both[:, COLS:]

    def radiance_row(y, carry):
        own = pl.ds(pl.multiple_of((y + ROWS) * 16, 16), 16)
        mapped = p_ref[own, :]
        wanted = t_ref[own, :]
        rows = pl.ds(pl.multiple_of(y * 16, 16), 16)
        slope = bm_ref[rows, :] + 2.0 * mapped * bpp_ref[rows, :] + wanted * bpt_ref[rows, :]
        slope = slope + 1.6 * (mapped - wanted)
        rest = 1.0 - mapped
        slope = slope * exposure * (rest * rest)
        for c in range(3):
            line = jnp.sum(jnp.where(of_colour[c], slope, 0.0), axis=0, keepdims=True)
            gimg_ref[pl.ds(c * ROWS + y, 1), :] = line
        return carry

    lax.fori_loop(0, ROWS, radiance_row, 0, unroll=16)

    spread_index = 16 * tile_row + (lane & 15)
    for c in range(3):
        for half in range(2):
            total = jnp.zeros((TILES, COLS), F32)
            for y in range(8):
                row = c * ROWS + half * 8 + y
                source = jnp.broadcast_to(gimg_ref[row : row + 1, :], (TILES, COLS))
                total = jnp.where((lane >> 4) == y, lane_gather(source, spread_index), total)
            gtile_ref[c * TILES : (c + 1) * TILES, 128 * half : 128 * half + 128] = total

    def composite_back(j, carry):
        ox, oy, a, b, c_ = [splat_row(f, j) for f in range(5)]
        colours = jnp.concatenate([splat_row(6 + c, j) for c in range(3)], axis=0)
        colour_top = colours.astype(BF16).astype(F32)
        slopes = jnp.concatenate(
            [gtile_ref[pl.ds(c * TILES + j, 1), :] for c in range(3)], axis=0
        )
        slope_top = slopes.astype(BF16).astype(F32)
        left = jnp.concatenate(
            [slope_top, slopes - slope_top, slope_top, jnp.zeros((7, LIST), F32)], axis=0
        )
        right = jnp.concatenate(
            [colour_top, colour_top, colours - colour_top, jnp.zeros((7, LIST), F32)], axis=0
        )
        deriv_ref[...] = dot(left.T.astype(BF16), right.astype(BF16))
        for y in range(16):
            rows = pixel_rows(j, y)
            value = deriv_ref[y * 16 : y * 16 + 16, :] * weight_ref[rows, :]
            weight_ref[rows, :] = value
            top, low = parts(value)
            pair_ref[y * 16 : y * 16 + 16, 0:LIST] = top
            pair_ref[y * 16 : y * 16 + 16, LIST : 2 * LIST] = low
        deriv_ref[...] = dot(pair_ref[...], later)
        dx = column_x - ox
        dxx = dx * dx
        zero = jnp.zeros((ROWS, LIST), F32)
        m0, mx, mxx = zero, zero, zero
        my, mxy, myy = zero, zero, zero
        for y in range(16):
            rows = pixel_rows(j, y)
            dy = (y + 0.5 - 8.0) - oy
            q = weight_ref[rows, :] - deriv_ref[y * 16 : y * 16 + 16, :] * cover_ref[rows, :]
            qx = q * dx
            qy = q * dy
            m0 = m0 + q
            mx = mx + qx
            my = my + qy
            mxx = mxx + q * dxx
            mxy = mxy + qx * dy
            myy = myy + qy * dy
        m0, mx, my, mxx, mxy, myy = [
            jnp.sum(m, axis=0, keepdims=True) for m in (m0, mx, my, mxx, mxy, myy)
        ]
        tile_rows = pl.ds(pl.multiple_of(j * 256, 256), 256)
        packed = left.astype(BF16)
        by_colour = dot(packed, top_ref[tile_rows, :]) + dot(packed, low_ref[tile_rows, :])
        rows = [
            a * mx + b * my,
            b * mx + c_ * my,
            -0.5 * mxx,
            -mxy,
            -0.5 * myy,
            m0 / splat_row(5, j),
        ] + [by_colour[c : c + 1] + by_colour[c + 3 : c + 4] for c in range(3)]
        lanes = pl.ds(pl.multiple_of(j * LIST, LIST), LIST)
        mask = slot_mask_ref[:, lanes]
        for f in range(SPLAT):
            top = rows[f].astype(BF16).astype(F32)
            for k, part in enumerate((top, rows[f] - top)):
                at = (k * SPLAT + f) * halves
                slot_left_ref[at : at + halves, :] = (
                    jnp.broadcast_to(part, (halves, LIST)).astype(BF16) * mask
                )
        update = dot_nt(slot_left_ref[...], slot_one_ref[:, lanes])

        @pl.when(j == 0)
        def _():
            slot_sum_ref[...] = update

        @pl.when(j > 0)
        def _():
            slot_sum_ref[...] = slot_sum_ref[...] + update

        return carry

    lax.fori_loop(0, TILES, composite_back, 0, unroll=8)

    count = SPLAT * halves
    for side in range(2):
        lanes = slice(side * COLS, side * COLS + COLS)
        sgrad_ref[side * count : (side + 1) * count, :] = (
            slot_sum_ref[0:count, lanes] + slot_sum_ref[count : 2 * count, lanes]
        )

    def send_back(step, carry):
        block = lax.rem(my_group + shift_of(step), groups)
        for i in range(group):
            peer = block * group + i
            first = (i % 2) * count + block * (group // 2) + i // 2
            back_ref[peer] = sgrad_ref[pl.ds(first, SPLAT, stride=halves), :]
        for i in range(group):
            peer = block * group + lax.rem(me + i, group)

            @pl.when(peer != me)
            def _():
                back_copy(peer, me).start()

        return carry

    lax.fori_loop(0, groups, send_back, 0)
    ret_ref[me] = back_ref[me]

    for i in range(1, nv):
        peer = lax.rem(mv + i, nv)
        camera_copy(peer, peer).wait_recv()
    for v in range(nv):
        angles = [jnp.broadcast_to(cams_ref[v, i : i + 1, :], (8, COLS)) for i in range(5)]
        turn = camera_rotation(angles)
        shift = [0.15 * angles[3], 0.15 * angles[4], 6.0]
        flat = [jnp.broadcast_to(turn[i][k], (8, COLS)) for i in range(3) for k in range(3)]
        flat += [sum((turn[i][k] * shift[i] for i in range(3))) for k in range(3)]
        for k in range(12):
            turn_ref[v, 8 * k : 8 * k + 8, :] = flat[k]

    def chunk_rows(f, i):
        return pl.ds(pl.multiple_of(f * HIGH + i * 8, 8), 8)

    def turn_of(v):
        flat = [turn_ref[v, 8 * k : 8 * k + 8, :] for k in range(12)]
        return [flat[0:3], flat[3:6], flat[6:9]], flat[9:12]

    def prepare(i, carry):
        position = [wide_ref[chunk_rows(f, i), :] for f in range(3)]
        stretch = [jnp.exp(wide_ref[chunk_rows(3 + k, i), :]) for k in range(3)]
        orient = quaternion_matrix(*[wide_ref[chunk_rows(6 + k, i), :] for k in range(4)])
        for v in range(nv):
            turn, away = turn_of(v)
            shift = [
                0.15 * jnp.broadcast_to(cams_ref[v, 3:4, :], (8, COLS)),
                0.15 * jnp.broadcast_to(cams_ref[v, 4:5, :], (8, COLS)),
                6.0,
            ]
            viewed = [
                sum((turn[r][k] * position[k] for k in range(3))) + shift[r] for r in range(3)
            ]
            inverse_z = 1.0 / viewed[2]
            slant_x = viewed[0] * inverse_z
            slant_y = viewed[1] * inverse_z
            focal_z = FOCAL * inverse_z
            row_x = [focal_z * (turn[0][k] - slant_x * turn[2][k]) for k in range(3)]
            row_y = [focal_z * (turn[1][k] - slant_y * turn[2][k]) for k in range(3)]
            image_x = [
                sum((row_x[r] * orient[r][k] for r in range(3))) * stretch[k] for k in range(3)
            ]
            image_y = [
                sum((row_y[r] * orient[r][k] for r in range(3))) * stretch[k] for k in range(3)
            ]
            cov_xx = sum((e * e for e in image_x)) + DILATE
            cov_yy = sum((e * e for e in image_y)) + DILATE
            cov_xy = sum((image_x[k] * image_y[k] for k in range(3)))
            share = 1.0 / (cov_xx * cov_yy - cov_xy * cov_xy)
            toward = [position[k] + away[k] for k in range(3)]
            closeness = 1.0 / jnp.sqrt(sum((e * e for e in toward)))
            direction = [e * closeness for e in toward]
            harmonic, pull = jax.vjp(harmonics, *direction)
            colours, moves = [], []
            for c in range(3):
                factors = [wide_ref[chunk_rows(11 + 3 * l + c, i), :] for l in range(16)]
                colour = jnp.exp(sum((harmonic[l] * factors[l] for l in range(16))))
                slope = pull(factors)
                along = sum((direction[k] * slope[k] for k in range(3)))
                reach = closeness * colour
                colours.append(colour)
                moves += [(slope[k] - direction[k] * along) * reach for k in range(3)]
            kept = (
                harmonic[1:]
                + colours
                + moves
                + [cov_yy * share, -cov_xy * share, cov_xx * share]
                + image_x
                + image_y
                + row_x
                + row_y
                + [inverse_z, slant_x, slant_y]
            )
            for k in range(JAC):
                jac_ref[v, chunk_rows(k, i), :] = kept[k]
        return carry

    lax.fori_loop(0, HIGH // 8, prepare, 0)

    own_sum_ref[...] = jnp.zeros_like(own_sum_ref)

    def add_group(step, carry):
        block = lax.rem(my_group + groups - shift_of(step), groups)
        for i in range(group):
            sender = block * group + i

            @pl.when(sender != me)
            def _():
                back_copy(sender, sender).wait_recv()

        for i in range(group):
            sender = block * group + i
            mask = own_mask_ref[:, pl.ds(pl.multiple_of(sender * COLS, COLS), COLS)]
            message = ret_ref[sender]
            top = message.astype(BF16).astype(F32)
            for k, part in enumerate((top, message - top)):
                for f in range(SPLAT):
                    at = (k * SPLAT + f) * 16
                    own_left_ref[at : at + 16, i * COLS : (i + 1) * COLS] = (
                        jnp.broadcast_to(part[f : f + 1], (16, COLS)).astype(BF16) * mask
                    )
        lanes = pl.ds(pl.multiple_of(block * group * COLS, COLS), group * COLS)
        own_sum_ref[...] = own_sum_ref[...] + dot_nt(own_left_ref[...], own_one_ref[:, lanes])
        return carry

    lax.fori_loop(0, groups, add_group, 0)
    for f in range(SPLAT):
        for side in range(2):
            lanes = slice(side * COLS, side * COLS + COLS)
            low = (SPLAT + f) * 16
            gall_ref[mv, pl.ds(f * HIGH + side, 16, stride=2), :] = (
                own_sum_ref[f * 16 : f * 16 + 16, lanes] + own_sum_ref[low : low + 16, lanes]
            )

    up = lax.rem(mv + 1, nv)
    down = lax.rem(mv + nv - 1, nv)
    half = SPLAT * HIGH // 2
    lower, upper = pl.ds(0, half), pl.ds(half, half)

    def view_copy(slot, rows, peer, k):
        return pltpu.make_async_remote_copy(
            src_ref=gall_ref.at[slot, rows],
            dst_ref=gall_ref.at[slot, rows],
            send_sem=v_send.at[k],
            recv_sem=v_recv.at[k],
            device_id={"view": peer},
            device_id_type=MESH,
        )

    sent = [view_copy(mv, lower, up, 0), view_copy(mv, upper, down, 1)]
    if nv > 2:
        sent += [view_copy(mv, upper, up, 2), view_copy(mv, lower, down, 3)]
    for copy in sent:
        copy.start()
    def drain(i, carry):
        peer = lax.rem(me + i, n)
        forward_copy(peer, me).wait_send()
        back_copy(peer, me).wait_send()
        return carry

    lax.fori_loop(1, n, drain, 0)

    @pl.when(me < n - 1)
    def _():
        target_copy(after, 0).wait_send()
        strip_copy(after, 0).wait_send()

    @pl.when(me > 0)
    def _():
        target_copy(before, 1).wait_send()
        strip_copy(before, 1).wait_send()

    if nv > 2:
        view_copy(down, lower, up, 0).wait_recv()
        sent.append(view_copy(down, lower, up, 4))
        sent[-1].start()
        view_copy(up, upper, down, 1).wait_recv()
        sent.append(view_copy(up, upper, down, 5))
        sent[-1].start()
        view_copy(down, upper, up, 2).wait_recv()
        view_copy(up, lower, down, 3).wait_recv()
        far = lax.rem(mv + 2, nv)
        view_copy(far, lower, up, 4).wait_recv()
        view_copy(far, upper, down, 5).wait_recv()
    else:
        view_copy(down, lower, up, 0).wait_recv()
        view_copy(up, upper, down, 1).wait_recv()

    def pull_back(i, carry):
        stretch = [jnp.exp(wide_ref[chunk_rows(3 + k, i), :]) for k in range(3)]
        quaternion = [wide_ref[chunk_rows(6 + k, i), :] for k in range(4)]
        orient, pull = jax.vjp(quaternion_matrix, *quaternion)
        opacity = 1.0 / (1.0 + jnp.exp(-wide_ref[chunk_rows(10, i), :]))
        by_position, by_scale, by_orient, by_opacity = [0.0] * 3, [0.0] * 3, [[0.0] * 3] * 3, 0.0
        by_colour = []
        for v in range(nv):
            slope = [gall_ref[v, chunk_rows(f, i), :] for f in range(SPLAT)]

            def kept(k):
                return jac_ref[v, chunk_rows(k, i), :]

            turn, _ = turn_of(v)
            a, b, c = [kept(27 + k) for k in range(3)]
            image_x = [kept(30 + k) for k in range(3)]
            image_y = [kept(33 + k) for k in range(3)]
            row_x = [kept(36 + k) for k in range(3)]
            row_y = [kept(39 + k) for k in range(3)]
            inverse_z, slant_x, slant_y = [kept(42 + k) for k in range(3)]
            ab, bb, bc = a * b, b * b, b * c
            by_xx = -(a * a * slope[2] + ab * slope[3] + bb * slope[4])
            by_yy = -(bb * slope[2] + bc * slope[3] + c * c * slope[4])
            by_xy = -(2 * ab * slope[2] + (bb + a * c) * slope[3] + 2 * bc * slope[4])
            by_x = [2 * by_xx * image_x[k] + by_xy * image_y[k] for k in range(3)]
            by_y = [2 * by_yy * image_y[k] + by_xy * image_x[k] for k in range(3)]
            by_scale = [
                by_scale[k] + by_x[k] * image_x[k] + by_y[k] * image_y[k] for k in range(3)
            ]
            by_x = [by_x[k] * stretch[k] for k in range(3)]
            by_y = [by_y[k] * stretch[k] for k in range(3)]
            by_orient = [
                [by_orient[r][k] + row_x[r] * by_x[k] + row_y[r] * by_y[k] for k in range(3)]
                for r in range(3)
            ]
            by_row_x = [sum((orient[r][k] * by_x[k] for k in range(3))) for r in range(3)]
            by_row_y = [sum((orient[r][k] * by_y[k] for k in range(3))) for r in range(3)]
            pulled = sum((by_row_x[r] * row_x[r] + by_row_y[r] * row_y[r] for r in range(3)))
            depth_x = sum((by_row_x[r] * turn[2][r] for r in range(3)))
            depth_y = sum((by_row_y[r] * turn[2][r] for r in range(3)))
            by_slant_x = FOCAL * (slope[0] - inverse_z * depth_x)
            by_slant_y = FOCAL * (slope[1] - inverse_z * depth_y)
            by_viewed = [
                by_slant_x * inverse_z,
                by_slant_y * inverse_z,
                -inverse_z * (pulled + by_slant_x * slant_x + by_slant_y * slant_y),
            ]
            by_position = [
                by_position[k]
                + sum((turn[r][k] * by_viewed[r] for r in range(3)))
                + sum((slope[6 + c_] * kept(18 + 3 * c_ + k) for c_ in range(3)))
                for k in range(3)
            ]
            by_opacity = by_opacity + slope[5]
            by_colour.append([slope[6 + c_] * kept(15 + c_) for c_ in range(3)])
        by_quaternion = pull(by_orient)
        grads = (
            by_position + by_scale + list(by_quaternion) + [by_opacity * opacity * (1.0 - opacity)]
        )
        for f in range(11):
            wide_grad_ref[chunk_rows(f, i), :] = grads[f]
        for l in range(16):
            for c_ in range(3):
                if l == 0:
                    total = SH_C0 * sum((by_colour[v][c_] for v in range(nv)))
                else:
                    total = sum(
                        (by_colour[v][c_] * jac_ref[v, chunk_rows(l - 1, i), :] for v in range(nv))
                    )
                wide_grad_ref[chunk_rows(11 + 3 * l + c_, i), :] = total
        return carry

    lax.fori_loop(0, HIGH // 8, pull_back, 0)

    for copy in sent:
        copy.wait_send()
    for i in range(1, nv):
        camera_copy(lax.rem(mv + i, nv), mv).wait_send()


def row_order_kernel(wide_hbm, rad_hbm, grad_hbm, radiance_hbm, grad_ref, wide_ref, sems, out_sems):
    groups = [(first, min(8, FEAT - first)) for first in range(0, FEAT, 8)]
    loads = [pltpu.make_async_copy(rad_hbm, radiance_hbm, sems.at[len(groups)])]
    stores = []
    for g, (first, size) in enumerate(groups):
        rows = pl.ds(first * HIGH, size * HIGH)
        loads.append(pltpu.make_async_copy(wide_hbm.at[rows], wide_ref.at[rows], sems.at[g]))
    for load in loads:
        load.start()
    for g, (first, size) in enumerate(groups):
        loads[g + 1].wait()
        for h in range(HIGH):
            grad_ref[first : first + size, h * COLS : (h + 1) * COLS] = wide_ref[
                pl.ds(first * HIGH + h, size, stride=HIGH), :
            ]
        rows = pl.ds(first, size)
        stores.append(pltpu.make_async_copy(grad_ref.at[rows], grad_hbm.at[rows], out_sems.at[g]))
        stores[-1].start()
    for copy in stores + loads[:1]:
        copy.wait()


def shards(n, nv, gaussians, send_index, tile_list, tile_length, camera, exposure, target):
    vmem = pl.BlockSpec(memory_space=pltpu.VMEM)
    halves = max(16, n // 2)
    group = min(8, n)

    def scratch(shape, dtype=F32):
        return pltpu.VMEM(shape, dtype)

    pixels = TILES * 256
    scratches = [
        scratch((FEAT, HIGH * COLS)),
        scratch((1, n, COLS), I32),
        scratch((1, TILES, LIST), I32),
        scratch((1, TILES), I32),
        scratch((1, 5)),
        scratch((1, 5)),
        scratch((1, CHANNELS, ROWS, COLS)),
        scratch((64 * HIGH, COLS)),
        scratch((SPLAT * HIGH, COLS)),
        scratch((SPLAT * group, COLS)),
        scratch((n, SPLAT, COLS)),
        scratch((n, SPLAT, COLS)),
        scratch(((SPLAT + 1) * TILES, LIST)),
        scratch((pixels, LIST)),
        scratch((pixels, LIST)),
        scratch((pixels, LIST), BF16),
        scratch((pixels, LIST), BF16),
        scratch((LIST, 2 * LIST), BF16),
        scratch((LIST, LIST)),
        scratch((3 * TILES, LIST)),
        scratch((3, 3, ROWS, COLS)),
        scratch((2, CHANNELS, ROWS, COLS)),
        scratch((48 * 16, COLS)),
        scratch((48 * 16, COLS)),
        scratch((48 * 16, COLS)),
        scratch((48 * 16, COLS)),
        scratch((48 * 16, COLS)),
        scratch((MAPS * 16, COLS)),
        scratch((MAPS * 16, COLS)),
        scratch((MAPS * 16, COLS)),
        scratch((MAPS * 16, COLS)),
        scratch((MAPS * 16, COLS)),
        scratch((ROWS * 16, COLS)),
        scratch((ROWS * 16, COLS)),
        scratch((ROWS * 16, COLS)),
        scratch((3 * MAPS * 16, 4 * COLS), BF16),
        scratch((3 * ROWS, COLS)),
        scratch((3 * TILES, LIST)),
        scratch((2 * SPLAT * halves, COLS)),
        scratch((256, TILES * LIST), BF16),
        scratch((halves, TILES * LIST), BF16),
        scratch((256, n * COLS), BF16),
        scratch((16, n * COLS), BF16),
        scratch((2 * SPLAT * halves, LIST), BF16),
        scratch((2 * SPLAT * halves, 256)),
        scratch((n, SPLAT, COLS)),
        scratch((n, SPLAT, COLS)),
        scratch((2 * SPLAT * 16, group * COLS), BF16),
        scratch((2 * SPLAT * 16, 256)),
        scratch((nv, SPLAT * HIGH, COLS)),
        scratch((nv, 8, COLS)),
        scratch((nv, 12 * 8, COLS)),
        scratch((nv, JAC * HIGH, COLS)),
    ]
    sems = [pltpu.SemaphoreType.DMA((k,)) for k in (n, n, n, n, 2, 2, 2, 2, 6, 6, nv, nv, 7)]
    wide_grad, strip = pl.pallas_call(
        functools.partial(step_kernel, n, nv),
        out_shape=(
            jax.ShapeDtypeStruct((FEAT * HIGH, COLS), F32),
            jax.ShapeDtypeStruct((1, 3, ROWS, COLS), F32),
        ),
        in_specs=[pl.BlockSpec(memory_space=pl.ANY)] * 7,
        out_specs=(vmem, vmem),
        scratch_shapes=scratches + sems,
        compiler_params=pltpu.CompilerParams(
            collective_id=0, has_side_effects=True, vmem_limit_bytes=56 * 2**20
        ),
        name="splat_step",
    )(gaussians, send_index, tile_list, tile_length, camera, exposure, target)
    return pl.pallas_call(
        row_order_kernel,
        out_shape=(
            jax.ShapeDtypeStruct((FEAT, HIGH * COLS), F32),
            jax.ShapeDtypeStruct((1, 3, ROWS, COLS), F32),
        ),
        in_specs=[pl.BlockSpec(memory_space=pl.ANY)] * 2,
        out_specs=(pl.BlockSpec(memory_space=pl.ANY),) * 2,
        scratch_shapes=[
            scratch((FEAT, HIGH * COLS)),
            scratch((FEAT * HIGH, COLS)),
            pltpu.SemaphoreType.DMA((9,)),
            pltpu.SemaphoreType.DMA((8,)),
        ],
        name="row_order",
    )(wide_grad, strip)


def solution(mesh):
    placed = (
        P(None, "gs"),
        P("view", "gs", None),
        P("view", "gs", None),
        P("view", "gs"),
        P("view", None),
        P("view", None),
        P("view", None, "gs", None),
    )
    return jax.shard_map(
        functools.partial(shards, mesh.shape["gs"], mesh.shape["view"]),
        mesh=mesh,
        in_specs=placed,
        out_specs=(P(None, "gs"), P("view", None, "gs", None)),
        check_vma=False,
    )
```

```python
import functools

import jax
import jax.numpy as jnp
import numpy as np
from jax import lax
from jax.experimental import pallas as pl
from jax.experimental.pallas import tpu as pltpu
from jax.sharding import PartitionSpec as P

MESH = pl.DeviceIdType.MESH
F32, BF16, I32 = jnp.float32, jnp.bfloat16, jnp.int32

FOCAL = 16.0
DILATE = 0.3
SH_C0 = 0.28209479177387814
SH_C1 = 0.4886025119029199
SH_C2 = [
    1.0925484305920792,
    -1.0925484305920792,
    0.31539156525252005,
    -1.0925484305920792,
    0.5462742152960396,
]
SH_C3 = [
    -0.5900435899266435,
    2.890611442640554,
    -0.4570457994644658,
    0.3731763325901154,
    -0.4570457994644658,
    1.445305721320277,
    -0.5900435899266435,
]
WINDOW_RAW = np.exp(-((np.arange(11) - 5.0) ** 2) / 4.5)
WINDOW = [float(v) for v in WINDOW_RAW / WINDOW_RAW.sum()]
FLOOR_MEAN = 0.0001
FLOOR_VAR = 0.0009

FEAT = 59
SPLAT = 9
HIGH = 32
TILES = 8
LIST = 256
ROWS = 16
LOG2E = 1.4426950408889634
COLS = 128
CHANNELS = 15
FIRST = 11
JAC = 45
MAPS = 26


def product3(left, right):
    return [[sum((left[i][k] * right[k][j] for k in range(3))) for j in range(3)] for i in range(3)]


def camera_rotation(camera):
    yaw_cos, yaw_sin = (jnp.cos(camera[0]), jnp.sin(camera[0]))
    pitch_cos, pitch_sin = (jnp.cos(camera[1]), jnp.sin(camera[1]))
    roll_cos, roll_sin = (jnp.cos(camera[2]), jnp.sin(camera[2]))
    about_z = [[yaw_cos, -yaw_sin, 0.0], [yaw_sin, yaw_cos, 0.0], [0.0, 0.0, 1.0]]
    about_y = [[pitch_cos, 0.0, pitch_sin], [0.0, 1.0, 0.0], [-pitch_sin, 0.0, pitch_cos]]
    about_x = [[1.0, 0.0, 0.0], [0.0, roll_cos, -roll_sin], [0.0, roll_sin, roll_cos]]
    return product3(product3(about_z, about_y), about_x)


def quaternion_matrix(q0, q1, q2, q3):
    scale = 1.0 / jnp.sqrt(q0 * q0 + q1 * q1 + q2 * q2 + q3 * q3)
    w, x, y, z = (q0 * scale, q1 * scale, q2 * scale, q3 * scale)
    return [
        [1 - 2 * (y * y + z * z), 2 * (x * y - w * z), 2 * (x * z + w * y)],
        [2 * (x * y + w * z), 1 - 2 * (x * x + z * z), 2 * (y * z - w * x)],
        [2 * (x * z - w * y), 2 * (y * z + w * x), 1 - 2 * (x * x + y * y)],
    ]


def harmonics(x, y, z):
    xx, yy, zz = (x * x, y * y, z * z)
    return [
        SH_C0 + 0.0 * x,
        -SH_C1 * y,
        SH_C1 * z,
        -SH_C1 * x,
        SH_C2[0] * x * y,
        SH_C2[1] * y * z,
        SH_C2[2] * (2 * zz - xx - yy),
        SH_C2[3] * x * z,
        SH_C2[4] * (xx - yy),
        SH_C3[0] * y * (3 * xx - yy),
        SH_C3[1] * x * y * z,
        SH_C3[2] * y * (4 * zz - xx - yy),
        SH_C3[3] * z * (2 * zz - 3 * xx - 3 * yy),
        SH_C3[4] * x * (4 * zz - xx - yy),
        SH_C3[5] * z * (xx - yy),
        SH_C3[6] * x * (xx - 3 * yy),
    ]


def project(params, camera, rotation):
    translation = [0.15 * camera[3], 0.15 * camera[4], 6.0]
    position = [params[i] for i in range(3)]
    viewed = [
        sum((rotation[i][j] * position[j] for j in range(3))) + translation[i] for i in range(3)
    ]
    inverse_z = 1.0 / viewed[2]
    row_x = [
        FOCAL * inverse_z * (rotation[0][k] - viewed[0] * inverse_z * rotation[2][k])
        for k in range(3)
    ]
    row_y = [
        FOCAL * inverse_z * (rotation[1][k] - viewed[1] * inverse_z * rotation[2][k])
        for k in range(3)
    ]
    orient = quaternion_matrix(params[6], params[7], params[8], params[9])
    stretch = [jnp.exp(params[3 + k]) for k in range(3)]
    image_x = [sum((row_x[i] * orient[i][k] for i in range(3))) * stretch[k] for k in range(3)]
    image_y = [sum((row_y[i] * orient[i][k] for i in range(3))) * stretch[k] for k in range(3)]
    cov_xx = sum((e * e for e in image_x)) + DILATE
    cov_yy = sum((e * e for e in image_y)) + DILATE
    cov_xy = sum((image_x[k] * image_y[k] for k in range(3)))
    share = 1.0 / (cov_xx * cov_yy - cov_xy * cov_xy)
    opacity = 1.0 / (1.0 + jnp.exp(-params[10]))
    toward = [
        position[k] + sum((rotation[i][k] * translation[i] for i in range(3))) for k in range(3)
    ]
    closeness = 1.0 / jnp.sqrt(sum((e * e for e in toward)))
    harmonic = harmonics(*[e * closeness for e in toward])
    colour = [
        jnp.exp(sum((harmonic[l] * params[11 + 3 * l + c] for l in range(16)))) for c in range(3)
    ]
    return [
        FOCAL * viewed[0] * inverse_z,
        FOCAL * viewed[1] * inverse_z,
        cov_yy * share,
        -cov_xy * share,
        cov_xx * share,
        opacity,
    ] + colour


def iota(shape, axis):
    return lax.broadcasted_iota(I32, shape, axis)


def lane_gather(values, index):
    return jnp.take_along_axis(values, index, axis=1, mode="promise_in_bounds")


def parts(values):
    top = values.astype(BF16)
    return top, (values - top.astype(F32)).astype(BF16)


def dot(left, right):
    return jnp.dot(left, right, preferred_element_type=F32)


def dot_nt(left, right):
    return lax.dot_general(left, right, (((1,), (1,)), ((), ())), preferred_element_type=F32)


def spread_rows(gauss_ref, wide_ref):
    def one(h, carry):
        lanes = pl.ds(pl.multiple_of(h * COLS, COLS), COLS)
        for first in range(0, FEAT, 8):
            count = min(8, FEAT - first)
            wide_ref[pl.ds(first * HIGH + h, count, stride=HIGH), :] = gauss_ref[first : first + count, lanes]
        return carry

    lax.fori_loop(0, HIGH, one, 0)


def window_band():
    distance = iota((COLS, COLS), 0) - iota((COLS, COLS), 1)
    band = jnp.zeros((COLS, COLS), F32)
    for i in range(11):
        band = jnp.where(distance == i - 5, WINDOW[i], band)
    return band


def band_factors():
    band = window_band()
    top = band.astype(BF16).astype(F32)
    middle = (band - top).astype(BF16).astype(F32)
    low = band - top - middle
    none = jnp.zeros((COLS, COLS), F32)
    left = jnp.concatenate([top, top, top, low], axis=0)
    right = jnp.concatenate([middle, middle, none, none], axis=0)
    return jnp.concatenate([left, right], axis=1).astype(BF16)


def split_three(values, place_ref, rows):
    top = values.astype(BF16)
    rest = values - top.astype(F32)
    middle = rest.astype(BF16)
    place_ref[rows, 0:COLS] = top
    place_ref[rows, COLS : 2 * COLS] = middle
    place_ref[rows, 2 * COLS : 3 * COLS] = (rest - middle.astype(F32)).astype(BF16)
    place_ref[rows, 3 * COLS : 4 * COLS] = top


def along_rows(ref, row):
    def at(i):
        return ref[pl.ds(pl.multiple_of((row + i) * 16, 16), 16), :]

    total = WINDOW[5] * at(0)
    for i in range(1, 6):
        total = total + WINDOW[5 + i] * (at(i) + at(-i))
    return total


def step_kernel(
    n,
    nv,
    gauss_hbm,
    send_hbm,
    list_hbm,
    len_hbm,
    cam_hbm,
    expo_hbm,
    target_hbm,
    wide_grad_ref,
    rad_ref,
    gauss_ref,
    send_ref,
    list_ref,
    len_ref,
    cam_ref,
    expo_ref,
    target_ref,
    wide_ref,
    table_ref,
    pick_ref,
    out_ref,
    recv_ref,
    splat_ref,
    cover_ref,
    weight_ref,
    top_ref,
    low_ref,
    pair_ref,
    deriv_ref,
    tile_rad_ref,
    strips_ref,
    edge_ref,
    t_ref,
    tt_ref,
    p_ref,
    pp_ref,
    pt_ref,
    mt_ref,
    btt_ref,
    gm_ref,
    gpp_ref,
    gpt_ref,
    bm_ref,
    bpp_ref,
    bpt_ref,
    split_ref,
    gimg_ref,
    gtile_ref,
    sgrad_ref,
    slot_one_ref,
    slot_mask_ref,
    own_one_ref,
    own_mask_ref,
    slot_left_ref,
    slot_sum_ref,
    back_ref,
    ret_ref,
    own_left_ref,
    own_sum_ref,
    gall_ref,
    cams_ref,
    turn_ref,
    jac_ref,
    f_send,
    f_recv,
    b_send,
    b_recv,
    t_send,
    t_recv,
    h_send,
    h_recv,
    v_send,
    v_recv,
    c_send,
    c_recv,
    in_sem,
):
    me = lax.axis_index("gs")
    mv = lax.axis_index("view")
    after = lax.rem(me + 1, n)
    before = lax.rem(me + n - 1, n)
    group = min(8, n)
    groups = n // group
    halves = slot_mask_ref.shape[0]

    loads = [
        pltpu.make_async_copy(source, place, in_sem.at[i])
        for i, (source, place) in enumerate(
            [
                (gauss_hbm, gauss_ref),
                (cam_hbm, cam_ref),
                (send_hbm, send_ref),
                (target_hbm, target_ref),
                (list_hbm, list_ref),
                (len_hbm, len_ref),
                (expo_hbm, expo_ref),
            ]
        )
    ]
    for load in loads:
        load.start()

    barrier = pltpu.get_barrier_semaphore()

    def greet(i, carry):
        pl.semaphore_signal(
            barrier, inc=1, device_id={"gs": lax.rem(me + i, n)}, device_id_type=MESH
        )
        return carry

    lax.fori_loop(1, n, greet, 0)
    for i in range(1, nv):
        pl.semaphore_signal(
            barrier, inc=1, device_id={"view": lax.rem(mv + i, nv)}, device_id_type=MESH
        )

    loads[0].wait()
    loads[1].wait()
    spread_rows(gauss_ref, wide_ref)
    camera = [jnp.broadcast_to(cam_ref[0:1, i : i + 1], (8, COLS)) for i in range(5)]
    rotation = camera_rotation(camera)

    def project_rows(i, carry):
        rows = [
            wide_ref[pl.ds(pl.multiple_of(f * HIGH + i * 8, 8), 8), :] for f in range(FEAT)
        ]
        for f, value in enumerate(project(rows, camera, rotation)):
            table_ref[pl.ds(pl.multiple_of(f * HIGH + i * 8, 8), 8), :] = value
        return carry

    lax.fori_loop(0, HIGH // 8, project_rows, 0, unroll=4)
    cams_ref[mv] = jnp.concatenate(
        [camera[i][0:1] for i in range(5)] + [jnp.zeros((3, COLS), F32)], axis=0
    )


    def target_copy(peer, side):
        return pltpu.make_async_remote_copy(
            src_ref=target_ref.at[0],
            dst_ref=edge_ref.at[side],
            send_sem=t_send.at[side],
            recv_sem=t_recv.at[side],
            device_id={"gs": peer},
            device_id_type=MESH,
        )

    def strip_copy(peer, side):
        return pltpu.make_async_remote_copy(
            src_ref=strips_ref.at[1],
            dst_ref=strips_ref.at[2 * side],
            send_sem=h_send.at[side],
            recv_sem=h_recv.at[side],
            device_id={"gs": peer},
            device_id_type=MESH,
        )

    def camera_copy(peer, slot):
        return pltpu.make_async_remote_copy(
            src_ref=cams_ref.at[mv],
            dst_ref=cams_ref.at[slot],
            send_sem=c_send.at[peer],
            recv_sem=c_recv.at[slot],
            device_id={"view": peer},
            device_id_type=MESH,
        )

    def forward_copy(peer, slot):
        return pltpu.make_async_remote_copy(
            src_ref=out_ref.at[peer],
            dst_ref=recv_ref.at[slot],
            send_sem=f_send.at[peer],
            recv_sem=f_recv.at[slot],
            device_id={"gs": peer},
            device_id_type=MESH,
        )

    def back_copy(peer, slot):
        return pltpu.make_async_remote_copy(
            src_ref=back_ref.at[peer],
            dst_ref=ret_ref.at[slot],
            send_sem=b_send.at[peer],
            recv_sem=b_recv.at[slot],
            device_id={"gs": peer},
            device_id_type=MESH,
        )

    my_group = me // group

    def shift_of(step):
        reach = groups // 2 - (step + 1) // 2
        return jnp.where(step % 2 == 1, reach, lax.rem(groups - reach, groups))

    def gather_group(step, carry):
        block = lax.rem(my_group + shift_of(step), groups)
        index = send_ref[0, pl.ds(pl.multiple_of(block * group, group), group), :]
        high = index >> 7
        low = index & 127

        def one(h, totals):
            chosen = high == h
            new = []
            for f in range(SPLAT):
                row = jnp.broadcast_to(table_ref[pl.ds(f * HIGH + h, 1), :], (group, COLS))
                new.append(jnp.where(chosen, lane_gather(row, low), totals[f]))
            return tuple(new)

        totals = lax.fori_loop(
            0, HIGH, one, tuple(jnp.zeros((group, COLS), F32) for _ in range(SPLAT)), unroll=8
        )
        for f in range(SPLAT):
            pick_ref[f * group : (f + 1) * group, :] = totals[f]
        for i in range(group):
            peer = block * group + i
            out_ref[peer] = pick_ref[pl.ds(i, SPLAT, stride=group), :]
        return carry

    def send_group(step, carry):
        block = lax.rem(my_group + shift_of(step), groups)
        for i in range(group):
            peer = block * group + lax.rem(me + i, group)

            @pl.when(peer != me)
            def _():
                forward_copy(peer, me).start()

        return carry

    def gather_and_send(step, carry):
        send_group(step, carry)
        return gather_group(step + ahead, carry)

    for load in loads[2:]:
        load.wait()
    ahead = min(2, groups)
    lax.fori_loop(0, ahead, gather_group, 0)
    pl.semaphore_wait(barrier, n - 1 + nv - 1)
    lax.fori_loop(0, groups - ahead, gather_and_send, 0)
    lax.fori_loop(groups - ahead, groups, send_group, 0)
    recv_ref[me] = out_ref[me]
    @pl.when(me < n - 1)
    def _():
        target_copy(after, 0).start()

    @pl.when(me > 0)
    def _():
        target_copy(before, 1).start()

    for i in range(1, nv):
        camera_copy(lax.rem(mv + i, nv), mv).start()

    def own_factors(r, carry):
        index = send_ref[0, pl.ds(r, 1), :]
        lanes = pl.ds(pl.multiple_of(r * COLS, COLS), COLS)
        own_one_ref[:, lanes] = jnp.where(iota((256, COLS), 0) == (index & 255), 1.0, 0.0).astype(BF16)
        own_mask_ref[:, lanes] = jnp.where(iota((16, COLS), 0) == (index >> 8), 1.0, 0.0).astype(BF16)
        return carry

    lax.fori_loop(0, n, own_factors, 0, unroll=8)

    def slot_factors(j, carry):
        index = list_ref[0, pl.ds(j, 1), :]
        lanes = pl.ds(pl.multiple_of(j * LIST, LIST), LIST)
        slot_one_ref[:, lanes] = jnp.where(iota((256, LIST), 0) == (index & 255), 1.0, 0.0).astype(BF16)
        slot_mask_ref[:, lanes] = jnp.where(iota((halves, LIST), 0) == (index >> 8), 1.0, 0.0).astype(
            BF16
        )
        return carry

    lax.fori_loop(0, TILES, slot_factors, 0, unroll=8)

    owner = [list_ref[0, :, 128 * h : 128 * h + 128] >> 7 for h in range(2)]
    place = [list_ref[0, :, 128 * h : 128 * h + 128] & 127 for h in range(2)]

    def take_group(step, totals):
        block = lax.rem(my_group + groups - shift_of(step), groups)
        for i in range(group):
            sender = block * group + i

            @pl.when(sender != me)
            def _():
                forward_copy(sender, sender).wait_recv()

        for i in range(group):
            sender = block * group + i
            chosen = [owner[h] == sender for h in range(2)]
            new = []
            for f in range(SPLAT):
                row = jnp.broadcast_to(recv_ref[sender, f : f + 1, :], (TILES, COLS))
                for h in range(2):
                    new.append(
                        jnp.where(chosen[h], lane_gather(row, place[h]), totals[2 * f + h])
                    )
            totals = tuple(new)
        return totals

    totals = lax.fori_loop(
        0, groups, take_group, tuple(jnp.zeros((TILES, COLS), F32) for _ in range(2 * SPLAT))
    )
    tile_row = iota((TILES, COLS), 0)
    length = jnp.zeros((TILES, COLS), I32)
    for j in range(TILES):
        length = jnp.where(tile_row == j, len_ref[0:1, j : j + 1], length)
    for f in range(SPLAT):
        for h in range(2):
            splat_ref[f * TILES : (f + 1) * TILES, 128 * h : 128 * h + 128] = totals[2 * f + h]
    for h in range(2):
        active = (iota((TILES, COLS), 1) + 128 * h) < length
        splat_ref[SPLAT * TILES : (SPLAT + 1) * TILES, 128 * h : 128 * h + 128] = jnp.where(
            active, totals[2 * 5 + h], 0.0
        )

    def splat_row(f, j):
        return splat_ref[pl.ds(f * TILES + j, 1), :]

    column_x = iota((ROWS, LIST), 0).astype(F32) + (0.5 - 8.0)
    first_of = iota((LIST, LIST), 0)
    then_of = iota((LIST, LIST), 1)
    earlier = jnp.where(first_of < then_of, 1.0, 0.0).astype(BF16)
    earlier = jnp.concatenate([earlier, earlier], axis=0)
    later = jnp.where(first_of > then_of, 1.0, 0.0).astype(BF16)
    later = jnp.concatenate([later, later], axis=0)

    def pixel_rows(j, y):
        return pl.ds(pl.multiple_of(j * 256 + y * 16, 16), 16)

    def composite(j, carry):
        ox, oy, a, b, c = [splat_row(f, j) for f in range(5)]
        opacity = splat_row(SPLAT, j)
        dx = column_x - ox
        square_part = (-0.5 * LOG2E * a) * dx * dx
        cross_part = (-LOG2E * b) * dx
        for y in range(16):
            dy = (y + 0.5 - 8.0) - oy
            power = square_part + dy * cross_part + (-0.5 * LOG2E * c) * dy * dy
            cover = opacity * jnp.exp2(power)
            cover_ref[pixel_rows(j, y), :] = cover
            top, low = parts(jnp.log(1.0 - cover))
            pair_ref[y * 16 : y * 16 + 16, 0:LIST] = top
            pair_ref[y * 16 : y * 16 + 16, LIST : 2 * LIST] = low
        deriv_ref[...] = dot(pair_ref[...], earlier)
        for y in range(16):
            rows = pixel_rows(j, y)
            cover = cover_ref[rows, :]
            weight = cover * jnp.exp(deriv_ref[y * 16 : y * 16 + 16, :])
            cover_ref[rows, :] = cover / (1.0 - cover)
            weight_ref[rows, :] = weight
            top, low = parts(weight)
            top_ref[rows, :] = top
            low_ref[rows, :] = low
        tile_rows = pl.ds(pl.multiple_of(j * 256, 256), 256)
        colours = jnp.concatenate([splat_row(6 + c, j) for c in range(3)], axis=0)
        colour_top = colours.astype(BF16).astype(F32)
        packed = jnp.concatenate(
            [colour_top, colours - colour_top, jnp.zeros((10, LIST), F32)], axis=0
        ).astype(BF16)
        seen = dot_nt(packed, top_ref[tile_rows, :]) + dot_nt(packed, low_ref[tile_rows, :])
        for c in range(3):
            tile_rad_ref[pl.ds(c * TILES + j, 1), :] = seen[c : c + 1] + seen[c + 3 : c + 4]
        return carry

    lax.fori_loop(0, TILES, composite, 0, unroll=8)

    lane = iota((TILES, COLS), 1)
    in_tile = (lane >> 4) == tile_row
    for y in range(16):
        index = (lane & 15) + 16 * (y % 8)
        for c in range(3):
            half = 128 * (y // 8)
            source = tile_rad_ref[c * TILES : (c + 1) * TILES, half : half + 128]
            line = jnp.sum(jnp.where(in_tile, lane_gather(source, index), 0.0), axis=0, keepdims=True)
            strips_ref[1, c, y : y + 1, :] = line

    @pl.when(me < n - 1)
    def _():
        strip_copy(after, 0).start()

    @pl.when(me > 0)
    def _():
        strip_copy(before, 1).start()

    @pl.when(me == 0)
    def _():
        edge_ref[0] = jnp.zeros((CHANNELS, ROWS, COLS), F32)
        strips_ref[0] = jnp.zeros((3, ROWS, COLS), F32)

    @pl.when(me == n - 1)
    def _():
        edge_ref[1] = jnp.zeros((CHANNELS, ROWS, COLS), F32)
        strips_ref[2] = jnp.zeros((3, ROWS, COLS), F32)

    @pl.when(me > 0)
    def _():
        target_copy(before, 0).wait_recv()

    @pl.when(me < n - 1)
    def _():
        target_copy(after, 1).wait_recv()

    for strip in range(3):
        for ch in range(16):
            if ch == CHANNELS:
                value = jnp.zeros((ROWS, COLS), F32)
            elif strip == 1:
                value = target_ref[0, ch]
            else:
                value = edge_ref[strip // 2, ch]
            t_ref[pl.ds(strip * 256 + ch, ROWS, stride=16), :] = value

    band = band_factors()

    def square_target(row, carry):
        rows = pl.ds(pl.multiple_of(row * 16, 16), 16)
        tt_ref[rows, :] = t_ref[rows, :] * t_ref[rows, :]
        return carry

    lax.fori_loop(FIRST - 5, FIRST + MAPS + 5, square_target, 0, unroll=4)

    def target_maps(i, carry):
        rows = pl.ds(pl.multiple_of(i * 16, 16), 16)
        second = pl.ds(pl.multiple_of((MAPS + i) * 16, 16), 16)
        split_three(along_rows(t_ref, FIRST + i), split_ref, rows)
        split_three(along_rows(tt_ref, FIRST + i), split_ref, second)
        return carry

    lax.fori_loop(0, MAPS, target_maps, 0, unroll=MAPS)
    count = MAPS * 16
    for k, maps in enumerate((mt_ref, btt_ref)):
        both = dot(split_ref[k * count : (k + 1) * count, :], band)
        maps[...] = both[:, 0:COLS] + both[:, COLS:]

    rad_ref[0] = strips_ref[1]

    channel = iota((16, COLS), 0)
    of_colour = [lax.rem(channel, 3) == c for c in range(3)]
    bracket = channel // 3
    exposure = jnp.zeros((16, COLS), F32)
    for b in range(5):
        exposure = jnp.where(bracket == b, expo_ref[0:1, b : b + 1], exposure)

    def tone(row, carry):
        strip = row // ROWS
        y = lax.rem(row, ROWS)
        lines = [strips_ref[strip, c, pl.ds(y, 1), :] for c in range(3)]
        scaled = exposure * jnp.where(
            of_colour[0], lines[0], jnp.where(of_colour[1], lines[1], lines[2])
        )
        mapped = scaled / (1.0 + scaled)
        rows = pl.ds(pl.multiple_of(row * 16, 16), 16)
        p_ref[rows, :] = mapped
        pp_ref[rows, :] = mapped * mapped
        pt_ref[rows, :] = mapped * t_ref[rows, :]
        return carry

    lax.fori_loop(ROWS, 2 * ROWS, tone, 0, unroll=ROWS)

    @pl.when(me > 0)
    def _():
        strip_copy(before, 0).wait_recv()

    @pl.when(me < n - 1)
    def _():
        strip_copy(after, 1).wait_recv()

    lax.fori_loop(FIRST - 5, ROWS, tone, 0, unroll=10)
    lax.fori_loop(2 * ROWS, FIRST + MAPS + 5, tone, 0, unroll=10)

    def filter_rows(i, carry):
        rows = pl.ds(pl.multiple_of(i * 16, 16), 16)
        second = pl.ds(pl.multiple_of((MAPS + i) * 16, 16), 16)
        third = pl.ds(pl.multiple_of((2 * MAPS + i) * 16, 16), 16)
        split_three(along_rows(p_ref, FIRST + i), split_ref, rows)
        split_three(along_rows(pp_ref, FIRST + i), split_ref, second)
        split_three(along_rows(pt_ref, FIRST + i), split_ref, third)
        return carry

    lax.fori_loop(0, MAPS, filter_rows, 0, unroll=MAPS)
    for k, maps in enumerate((gm_ref, gpp_ref, gpt_ref)):
        both = dot(split_ref[k * count : (k + 1) * count, :], band)
        maps[...] = both[:, 0:COLS] + both[:, COLS:]

    def similarity_row(i, carry):
        row = FIRST + i
        rows = pl.ds(pl.multiple_of(i * 16, 16), 16)
        mean_p = gm_ref[rows, :]
        square_p = gpp_ref[rows, :]
        cross = gpt_ref[rows, :]
        mean_t = mt_ref[rows, :]
        both = mean_p * mean_t
        n1 = 2.0 * both + FLOOR_MEAN
        n2 = 2.0 * (cross - both) + FLOOR_VAR
        d1 = mean_p * mean_p + mean_t * mean_t + FLOOR_MEAN
        d2 = (square_p - mean_p * mean_p) + (btt_ref[rows, :] - mean_t * mean_t) + FLOOR_VAR
        inside = ((row >= ROWS) | (me > 0)) & ((row < 2 * ROWS) | (me < n - 1))
        share = jnp.where(inside, 1.0, 0.0) / (d1 * d2)
        similar = n1 * n2 * share
        gpt_ref[rows, :] = -2.0 * n1 * share
        by_d2 = similar / d2
        gpp_ref[rows, :] = by_d2
        gm_ref[rows, :] = 2.0 * (
            mean_t * (n1 - n2) * share + mean_p * (similar / d1 - by_d2)
        )
        return carry

    lax.fori_loop(0, MAPS, similarity_row, 0, unroll=26)

    def filter_back(y, carry):
        for k, source in enumerate((gm_ref, gpp_ref, gpt_ref)):
            rows = pl.ds(pl.multiple_of((k * ROWS + y) * 16, 16), 16)
            split_three(along_rows(source, y + 5), split_ref, rows)
        return carry

    lax.fori_loop(0, ROWS, filter_back, 0, unroll=ROWS)
    for k, maps in enumerate((bm_ref, bpp_ref, bpt_ref)):
        both = dot(split_ref[k * ROWS * 16 : (k + 1) * ROWS * 16, :], band)
        maps[...] = both[:, 0:COLS] + both[:, COLS:]

    def radiance_row(y, carry):
        own = pl.ds(pl.multiple_of((y + ROWS) * 16, 16), 16)
        mapped = p_ref[own, :]
        wanted = t_ref[own, :]
        rows = pl.ds(pl.multiple_of(y * 16, 16), 16)
        slope = bm_ref[rows, :] + 2.0 * mapped * bpp_ref[rows, :] + wanted * bpt_ref[rows, :]
        slope = slope + 1.6 * (mapped - wanted)
        rest = 1.0 - mapped
        slope = slope * exposure * (rest * rest)
        for c in range(3):
            line = jnp.sum(jnp.where(of_colour[c], slope, 0.0), axis=0, keepdims=True)
            gimg_ref[pl.ds(c * ROWS + y, 1), :] = line
        return carry

    lax.fori_loop(0, ROWS, radiance_row, 0, unroll=16)

    spread_index = 16 * tile_row + (lane & 15)
    for c in range(3):
        for half in range(2):
            total = jnp.zeros((TILES, COLS), F32)
            for y in range(8):
                row = c * ROWS + half * 8 + y
                source = jnp.broadcast_to(gimg_ref[row : row + 1, :], (TILES, COLS))
                total = jnp.where((lane >> 4) == y, lane_gather(source, spread_index), total)
            gtile_ref[c * TILES : (c + 1) * TILES, 128 * half : 128 * half + 128] = total

    def composite_back(j, carry):
        ox, oy, a, b, c_ = [splat_row(f, j) for f in range(5)]
        colours = jnp.concatenate([splat_row(6 + c, j) for c in range(3)], axis=0)
        colour_top = colours.astype(BF16).astype(F32)
        slopes = jnp.concatenate(
            [gtile_ref[pl.ds(c * TILES + j, 1), :] for c in range(3)], axis=0
        )
        slope_top = slopes.astype(BF16).astype(F32)
        left = jnp.concatenate(
            [slope_top, slopes - slope_top, slope_top, jnp.zeros((7, LIST), F32)], axis=0
        )
        right = jnp.concatenate(
            [colour_top, colour_top, colours - colour_top, jnp.zeros((7, LIST), F32)], axis=0
        )
        deriv_ref[...] = dot(left.T.astype(BF16), right.astype(BF16))
        for y in range(16):
            rows = pixel_rows(j, y)
            value = deriv_ref[y * 16 : y * 16 + 16, :] * weight_ref[rows, :]
            weight_ref[rows, :] = value
            top, low = parts(value)
            pair_ref[y * 16 : y * 16 + 16, 0:LIST] = top
            pair_ref[y * 16 : y * 16 + 16, LIST : 2 * LIST] = low
        deriv_ref[...] = dot(pair_ref[...], later)
        dx = column_x - ox
        dxx = dx * dx
        zero = jnp.zeros((ROWS, LIST), F32)
        m0, mx, mxx = zero, zero, zero
        my, mxy, myy = zero, zero, zero
        for y in range(16):
            rows = pixel_rows(j, y)
            dy = (y + 0.5 - 8.0) - oy
            q = weight_ref[rows, :] - deriv_ref[y * 16 : y * 16 + 16, :] * cover_ref[rows, :]
            qx = q * dx
            qy = q * dy
            m0 = m0 + q
            mx = mx + qx
            my = my + qy
            mxx = mxx + q * dxx
            mxy = mxy + qx * dy
            myy = myy + qy * dy
        m0, mx, my, mxx, mxy, myy = [
            jnp.sum(m, axis=0, keepdims=True) for m in (m0, mx, my, mxx, mxy, myy)
        ]
        tile_rows = pl.ds(pl.multiple_of(j * 256, 256), 256)
        packed = left.astype(BF16)
        by_colour = dot(packed, top_ref[tile_rows, :]) + dot(packed, low_ref[tile_rows, :])
        rows = [
            a * mx + b * my,
            b * mx + c_ * my,
            -0.5 * mxx,
            -mxy,
            -0.5 * myy,
            m0 / splat_row(5, j),
        ] + [by_colour[c : c + 1] + by_colour[c + 3 : c + 4] for c in range(3)]
        lanes = pl.ds(pl.multiple_of(j * LIST, LIST), LIST)
        mask = slot_mask_ref[:, lanes]
        for f in range(SPLAT):
            top = rows[f].astype(BF16).astype(F32)
            for k, part in enumerate((top, rows[f] - top)):
                at = (k * SPLAT + f) * halves
                slot_left_ref[at : at + halves, :] = (
                    jnp.broadcast_to(part, (halves, LIST)).astype(BF16) * mask
                )
        update = dot_nt(slot_left_ref[...], slot_one_ref[:, lanes])

        @pl.when(j == 0)
        def _():
            slot_sum_ref[...] = update

        @pl.when(j > 0)
        def _():
            slot_sum_ref[...] = slot_sum_ref[...] + update

        return carry

    lax.fori_loop(0, TILES, composite_back, 0, unroll=8)

    count = SPLAT * halves
    for side in range(2):
        lanes = slice(side * COLS, side * COLS + COLS)
        sgrad_ref[side * count : (side + 1) * count, :] = (
            slot_sum_ref[0:count, lanes] + slot_sum_ref[count : 2 * count, lanes]
        )

    def send_back(step, carry):
        block = lax.rem(my_group + shift_of(step), groups)
        for i in range(group):
            peer = block * group + i
            first = (i % 2) * count + block * (group // 2) + i // 2
            back_ref[peer] = sgrad_ref[pl.ds(first, SPLAT, stride=halves), :]
        for i in range(group):
            peer = block * group + lax.rem(me + i, group)

            @pl.when(peer != me)
            def _():
                back_copy(peer, me).start()

        return carry

    lax.fori_loop(0, groups, send_back, 0)
    ret_ref[me] = back_ref[me]

    for i in range(1, nv):
        peer = lax.rem(mv + i, nv)
        camera_copy(peer, peer).wait_recv()
    for v in range(nv):
        angles = [jnp.broadcast_to(cams_ref[v, i : i + 1, :], (8, COLS)) for i in range(5)]
        turn = camera_rotation(angles)
        shift = [0.15 * angles[3], 0.15 * angles[4], 6.0]
        flat = [jnp.broadcast_to(turn[i][k], (8, COLS)) for i in range(3) for k in range(3)]
        flat += [sum((turn[i][k] * shift[i] for i in range(3))) for k in range(3)]
        for k in range(12):
            turn_ref[v, 8 * k : 8 * k + 8, :] = flat[k]

    def chunk_rows(f, i):
        return pl.ds(pl.multiple_of(f * HIGH + i * 8, 8), 8)

    def turn_of(v):
        flat = [turn_ref[v, 8 * k : 8 * k + 8, :] for k in range(12)]
        return [flat[0:3], flat[3:6], flat[6:9]], flat[9:12]

    def prepare(i, carry):
        position = [wide_ref[chunk_rows(f, i), :] for f in range(3)]
        stretch = [jnp.exp(wide_ref[chunk_rows(3 + k, i), :]) for k in range(3)]
        orient = quaternion_matrix(*[wide_ref[chunk_rows(6 + k, i), :] for k in range(4)])
        for v in range(nv):
            turn, away = turn_of(v)
            shift = [
                0.15 * jnp.broadcast_to(cams_ref[v, 3:4, :], (8, COLS)),
                0.15 * jnp.broadcast_to(cams_ref[v, 4:5, :], (8, COLS)),
                6.0,
            ]
            viewed = [
                sum((turn[r][k] * position[k] for k in range(3))) + shift[r] for r in range(3)
            ]
            inverse_z = 1.0 / viewed[2]
            slant_x = viewed[0] * inverse_z
            slant_y = viewed[1] * inverse_z
            focal_z = FOCAL * inverse_z
            row_x = [focal_z * (turn[0][k] - slant_x * turn[2][k]) for k in range(3)]
            row_y = [focal_z * (turn[1][k] - slant_y * turn[2][k]) for k in range(3)]
            image_x = [
                sum((row_x[r] * orient[r][k] for r in range(3))) * stretch[k] for k in range(3)
            ]
            image_y = [
                sum((row_y[r] * orient[r][k] for r in range(3))) * stretch[k] for k in range(3)
            ]
            cov_xx = sum((e * e for e in image_x)) + DILATE
            cov_yy = sum((e * e for e in image_y)) + DILATE
            cov_xy = sum((image_x[k] * image_y[k] for k in range(3)))
            share = 1.0 / (cov_xx * cov_yy - cov_xy * cov_xy)
            toward = [position[k] + away[k] for k in range(3)]
            closeness = 1.0 / jnp.sqrt(sum((e * e for e in toward)))
            direction = [e * closeness for e in toward]
            harmonic, pull = jax.vjp(harmonics, *direction)
            colours, moves = [], []
            for c in range(3):
                factors = [wide_ref[chunk_rows(11 + 3 * l + c, i), :] for l in range(16)]
                colour = jnp.exp(sum((harmonic[l] * factors[l] for l in range(16))))
                slope = pull(factors)
                along = sum((direction[k] * slope[k] for k in range(3)))
                reach = closeness * colour
                colours.append(colour)
                moves += [(slope[k] - direction[k] * along) * reach for k in range(3)]
            kept = (
                harmonic[1:]
                + colours
                + moves
                + [cov_yy * share, -cov_xy * share, cov_xx * share]
                + image_x
                + image_y
                + row_x
                + row_y
                + [inverse_z, slant_x, slant_y]
            )
            for k in range(JAC):
                jac_ref[v, chunk_rows(k, i), :] = kept[k]
        return carry

    lax.fori_loop(0, HIGH // 8, prepare, 0)

    own_sum_ref[...] = jnp.zeros_like(own_sum_ref)

    def add_group(step, carry):
        block = lax.rem(my_group + groups - shift_of(step), groups)
        for i in range(group):
            sender = block * group + i

            @pl.when(sender != me)
            def _():
                back_copy(sender, sender).wait_recv()

        for i in range(group):
            sender = block * group + i
            mask = own_mask_ref[:, pl.ds(pl.multiple_of(sender * COLS, COLS), COLS)]
            message = ret_ref[sender]
            top = message.astype(BF16).astype(F32)
            for k, part in enumerate((top, message - top)):
                for f in range(SPLAT):
                    at = (k * SPLAT + f) * 16
                    own_left_ref[at : at + 16, i * COLS : (i + 1) * COLS] = (
                        jnp.broadcast_to(part[f : f + 1], (16, COLS)).astype(BF16) * mask
                    )
        lanes = pl.ds(pl.multiple_of(block * group * COLS, COLS), group * COLS)
        own_sum_ref[...] = own_sum_ref[...] + dot_nt(own_left_ref[...], own_one_ref[:, lanes])
        return carry

    lax.fori_loop(0, groups, add_group, 0)
    for f in range(SPLAT):
        for side in range(2):
            lanes = slice(side * COLS, side * COLS + COLS)
            low = (SPLAT + f) * 16
            gall_ref[mv, pl.ds(f * HIGH + side, 16, stride=2), :] = (
                own_sum_ref[f * 16 : f * 16 + 16, lanes] + own_sum_ref[low : low + 16, lanes]
            )

    up = lax.rem(mv + 1, nv)
    down = lax.rem(mv + nv - 1, nv)
    half = SPLAT * HIGH // 2
    lower, upper = pl.ds(0, half), pl.ds(half, half)

    def view_copy(slot, rows, peer, k):
        return pltpu.make_async_remote_copy(
            src_ref=gall_ref.at[slot, rows],
            dst_ref=gall_ref.at[slot, rows],
            send_sem=v_send.at[k],
            recv_sem=v_recv.at[k],
            device_id={"view": peer},
            device_id_type=MESH,
        )

    sent = [view_copy(mv, lower, up, 0), view_copy(mv, upper, down, 1)]
    if nv > 2:
        sent += [view_copy(mv, upper, up, 2), view_copy(mv, lower, down, 3)]
    for copy in sent:
        copy.start()
    def drain(i, carry):
        peer = lax.rem(me + i, n)
        forward_copy(peer, me).wait_send()
        back_copy(peer, me).wait_send()
        return carry

    lax.fori_loop(1, n, drain, 0)

    @pl.when(me < n - 1)
    def _():
        target_copy(after, 0).wait_send()
        strip_copy(after, 0).wait_send()

    @pl.when(me > 0)
    def _():
        target_copy(before, 1).wait_send()
        strip_copy(before, 1).wait_send()

    if nv > 2:
        view_copy(down, lower, up, 0).wait_recv()
        sent.append(view_copy(down, lower, up, 4))
        sent[-1].start()
        view_copy(up, upper, down, 1).wait_recv()
        sent.append(view_copy(up, upper, down, 5))
        sent[-1].start()
        view_copy(down, upper, up, 2).wait_recv()
        view_copy(up, lower, down, 3).wait_recv()
        far = lax.rem(mv + 2, nv)
        view_copy(far, lower, up, 4).wait_recv()
        view_copy(far, upper, down, 5).wait_recv()
    else:
        view_copy(down, lower, up, 0).wait_recv()
        view_copy(up, upper, down, 1).wait_recv()

    def pull_back(i, carry):
        stretch = [jnp.exp(wide_ref[chunk_rows(3 + k, i), :]) for k in range(3)]
        quaternion = [wide_ref[chunk_rows(6 + k, i), :] for k in range(4)]
        orient, pull = jax.vjp(quaternion_matrix, *quaternion)
        opacity = 1.0 / (1.0 + jnp.exp(-wide_ref[chunk_rows(10, i), :]))
        by_position, by_scale, by_orient, by_opacity = [0.0] * 3, [0.0] * 3, [[0.0] * 3] * 3, 0.0
        by_colour = []
        for v in range(nv):
            slope = [gall_ref[v, chunk_rows(f, i), :] for f in range(SPLAT)]

            def kept(k):
                return jac_ref[v, chunk_rows(k, i), :]

            turn, _ = turn_of(v)
            a, b, c = [kept(27 + k) for k in range(3)]
            image_x = [kept(30 + k) for k in range(3)]
            image_y = [kept(33 + k) for k in range(3)]
            row_x = [kept(36 + k) for k in range(3)]
            row_y = [kept(39 + k) for k in range(3)]
            inverse_z, slant_x, slant_y = [kept(42 + k) for k in range(3)]
            ab, bb, bc = a * b, b * b, b * c
            by_xx = -(a * a * slope[2] + ab * slope[3] + bb * slope[4])
            by_yy = -(bb * slope[2] + bc * slope[3] + c * c * slope[4])
            by_xy = -(2 * ab * slope[2] + (bb + a * c) * slope[3] + 2 * bc * slope[4])
            by_x = [2 * by_xx * image_x[k] + by_xy * image_y[k] for k in range(3)]
            by_y = [2 * by_yy * image_y[k] + by_xy * image_x[k] for k in range(3)]
            by_scale = [
                by_scale[k] + by_x[k] * image_x[k] + by_y[k] * image_y[k] for k in range(3)
            ]
            by_x = [by_x[k] * stretch[k] for k in range(3)]
            by_y = [by_y[k] * stretch[k] for k in range(3)]
            by_orient = [
                [by_orient[r][k] + row_x[r] * by_x[k] + row_y[r] * by_y[k] for k in range(3)]
                for r in range(3)
            ]
            by_row_x = [sum((orient[r][k] * by_x[k] for k in range(3))) for r in range(3)]
            by_row_y = [sum((orient[r][k] * by_y[k] for k in range(3))) for r in range(3)]
            pulled = sum((by_row_x[r] * row_x[r] + by_row_y[r] * row_y[r] for r in range(3)))
            depth_x = sum((by_row_x[r] * turn[2][r] for r in range(3)))
            depth_y = sum((by_row_y[r] * turn[2][r] for r in range(3)))
            by_slant_x = FOCAL * (slope[0] - inverse_z * depth_x)
            by_slant_y = FOCAL * (slope[1] - inverse_z * depth_y)
            by_viewed = [
                by_slant_x * inverse_z,
                by_slant_y * inverse_z,
                -inverse_z * (pulled + by_slant_x * slant_x + by_slant_y * slant_y),
            ]
            by_position = [
                by_position[k]
                + sum((turn[r][k] * by_viewed[r] for r in range(3)))
                + sum((slope[6 + c_] * kept(18 + 3 * c_ + k) for c_ in range(3)))
                for k in range(3)
            ]
            by_opacity = by_opacity + slope[5]
            by_colour.append([slope[6 + c_] * kept(15 + c_) for c_ in range(3)])
        by_quaternion = pull(by_orient)
        grads = (
            by_position + by_scale + list(by_quaternion) + [by_opacity * opacity * (1.0 - opacity)]
        )
        for f in range(11):
            wide_grad_ref[chunk_rows(f, i), :] = grads[f]
        for l in range(16):
            for c_ in range(3):
                if l == 0:
                    total = SH_C0 * sum((by_colour[v][c_] for v in range(nv)))
                else:
                    total = sum(
                        (by_colour[v][c_] * jac_ref[v, chunk_rows(l - 1, i), :] for v in range(nv))
                    )
                wide_grad_ref[chunk_rows(11 + 3 * l + c_, i), :] = total
        return carry

    lax.fori_loop(0, HIGH // 8, pull_back, 0)

    for copy in sent:
        copy.wait_send()
    for i in range(1, nv):
        camera_copy(lax.rem(mv + i, nv), mv).wait_send()


def row_order_kernel(wide_hbm, rad_hbm, grad_hbm, radiance_hbm, grad_ref, wide_ref, sems, out_sems):
    groups = [(first, min(8, FEAT - first)) for first in range(0, FEAT, 8)]
    loads = [pltpu.make_async_copy(rad_hbm, radiance_hbm, sems.at[len(groups)])]
    stores = []
    for g, (first, size) in enumerate(groups):
        rows = pl.ds(first * HIGH, size * HIGH)
        loads.append(pltpu.make_async_copy(wide_hbm.at[rows], wide_ref.at[rows], sems.at[g]))
    for load in loads:
        load.start()
    for g, (first, size) in enumerate(groups):
        loads[g + 1].wait()
        for h in range(HIGH):
            grad_ref[first : first + size, h * COLS : (h + 1) * COLS] = wide_ref[
                pl.ds(first * HIGH + h, size, stride=HIGH), :
            ]
        rows = pl.ds(first, size)
        stores.append(pltpu.make_async_copy(grad_ref.at[rows], grad_hbm.at[rows], out_sems.at[g]))
        stores[-1].start()
    for copy in stores + loads[:1]:
        copy.wait()


def shards(n, nv, gaussians, send_index, tile_list, tile_length, camera, exposure, target):
    vmem = pl.BlockSpec(memory_space=pltpu.VMEM)
    halves = max(16, n // 2)
    group = min(8, n)

    def scratch(shape, dtype=F32):
        return pltpu.VMEM(shape, dtype)

    pixels = TILES * 256
    scratches = [
        scratch((FEAT, HIGH * COLS)),
        scratch((1, n, COLS), I32),
        scratch((1, TILES, LIST), I32),
        scratch((1, TILES), I32),
        scratch((1, 5)),
        scratch((1, 5)),
        scratch((1, CHANNELS, ROWS, COLS)),
        scratch((64 * HIGH, COLS)),
        scratch((SPLAT * HIGH, COLS)),
        scratch((SPLAT * group, COLS)),
        scratch((n, SPLAT, COLS)),
        scratch((n, SPLAT, COLS)),
        scratch(((SPLAT + 1) * TILES, LIST)),
        scratch((pixels, LIST)),
        scratch((pixels, LIST)),
        scratch((pixels, LIST), BF16),
        scratch((pixels, LIST), BF16),
        scratch((LIST, 2 * LIST), BF16),
        scratch((LIST, LIST)),
        scratch((3 * TILES, LIST)),
        scratch((3, 3, ROWS, COLS)),
        scratch((2, CHANNELS, ROWS, COLS)),
        scratch((48 * 16, COLS)),
        scratch((48 * 16, COLS)),
        scratch((48 * 16, COLS)),
        scratch((48 * 16, COLS)),
        scratch((48 * 16, COLS)),
        scratch((MAPS * 16, COLS)),
        scratch((MAPS * 16, COLS)),
        scratch((MAPS * 16, COLS)),
        scratch((MAPS * 16, COLS)),
        scratch((MAPS * 16, COLS)),
        scratch((ROWS * 16, COLS)),
        scratch((ROWS * 16, COLS)),
        scratch((ROWS * 16, COLS)),
        scratch((3 * MAPS * 16, 4 * COLS), BF16),
        scratch((3 * ROWS, COLS)),
        scratch((3 * TILES, LIST)),
        scratch((2 * SPLAT * halves, COLS)),
        scratch((256, TILES * LIST), BF16),
        scratch((halves, TILES * LIST), BF16),
        scratch((256, n * COLS), BF16),
        scratch((16, n * COLS), BF16),
        scratch((2 * SPLAT * halves, LIST), BF16),
        scratch((2 * SPLAT * halves, 256)),
        scratch((n, SPLAT, COLS)),
        scratch((n, SPLAT, COLS)),
        scratch((2 * SPLAT * 16, group * COLS), BF16),
        scratch((2 * SPLAT * 16, 256)),
        scratch((nv, SPLAT * HIGH, COLS)),
        scratch((nv, 8, COLS)),
        scratch((nv, 12 * 8, COLS)),
        scratch((nv, JAC * HIGH, COLS)),
    ]
    sems = [pltpu.SemaphoreType.DMA((k,)) for k in (n, n, n, n, 2, 2, 2, 2, 6, 6, nv, nv, 7)]
    wide_grad, strip = pl.pallas_call(
        functools.partial(step_kernel, n, nv),
        out_shape=(
            jax.ShapeDtypeStruct((FEAT * HIGH, COLS), F32),
            jax.ShapeDtypeStruct((1, 3, ROWS, COLS), F32),
        ),
        in_specs=[pl.BlockSpec(memory_space=pl.ANY)] * 7,
        out_specs=(vmem, vmem),
        scratch_shapes=scratches + sems,
        compiler_params=pltpu.CompilerParams(
            collective_id=0, has_side_effects=True, vmem_limit_bytes=56 * 2**20
        ),
        name="splat_step",
    )(gaussians, send_index, tile_list, tile_length, camera, exposure, target)
    return pl.pallas_call(
        row_order_kernel,
        out_shape=(
            jax.ShapeDtypeStruct((FEAT, HIGH * COLS), F32),
            jax.ShapeDtypeStruct((1, 3, ROWS, COLS), F32),
        ),
        in_specs=[pl.BlockSpec(memory_space=pl.ANY)] * 2,
        out_specs=(pl.BlockSpec(memory_space=pl.ANY),) * 2,
        scratch_shapes=[
            scratch((FEAT, HIGH * COLS)),
            scratch((FEAT * HIGH, COLS)),
            pltpu.SemaphoreType.DMA((9,)),
            pltpu.SemaphoreType.DMA((8,)),
        ],
        name="row_order",
    )(wide_grad, strip)


def solution(mesh):
    placed = (
        P(None, "gs"),
        P("view", "gs", None),
        P("view", "gs", None),
        P("view", "gs"),
        P("view", None),
        P("view", None),
        P("view", None, "gs", None),
    )
    return jax.shard_map(
        functools.partial(shards, mesh.shape["gs"], mesh.shape["view"]),
        mesh=mesh,
        in_specs=placed,
        out_specs=(P(None, "gs"), P("view", None, "gs", None)),
        check_vma=False,
    )
```

```python
import functools

import jax
import jax.numpy as jnp
import numpy as np
from jax import lax
from jax.experimental import pallas as pl
from jax.experimental.pallas import tpu as pltpu
from jax.sharding import PartitionSpec as P

MESH = pl.DeviceIdType.MESH
F32, BF16, I32 = jnp.float32, jnp.bfloat16, jnp.int32

FOCAL = 16.0
DILATE = 0.3
SH_C0 = 0.28209479177387814
SH_C1 = 0.4886025119029199
SH_C2 = [
    1.0925484305920792,
    -1.0925484305920792,
    0.31539156525252005,
    -1.0925484305920792,
    0.5462742152960396,
]
SH_C3 = [
    -0.5900435899266435,
    2.890611442640554,
    -0.4570457994644658,
    0.3731763325901154,
    -0.4570457994644658,
    1.445305721320277,
    -0.5900435899266435,
]
WINDOW_RAW = np.exp(-((np.arange(11) - 5.0) ** 2) / 4.5)
WINDOW = [float(v) for v in WINDOW_RAW / WINDOW_RAW.sum()]
FLOOR_MEAN = 0.0001
FLOOR_VAR = 0.0009

FEAT = 59
SPLAT = 9
HIGH = 32
TILES = 8
LIST = 256
ROWS = 16
LOG2E = 1.4426950408889634
COLS = 128
CHANNELS = 15
FIRST = 11
JAC = 45
MAPS = 26


def product3(left, right):
    return [[sum((left[i][k] * right[k][j] for k in range(3))) for j in range(3)] for i in range(3)]


def camera_rotation(camera):
    yaw_cos, yaw_sin = (jnp.cos(camera[0]), jnp.sin(camera[0]))
    pitch_cos, pitch_sin = (jnp.cos(camera[1]), jnp.sin(camera[1]))
    roll_cos, roll_sin = (jnp.cos(camera[2]), jnp.sin(camera[2]))
    about_z = [[yaw_cos, -yaw_sin, 0.0], [yaw_sin, yaw_cos, 0.0], [0.0, 0.0, 1.0]]
    about_y = [[pitch_cos, 0.0, pitch_sin], [0.0, 1.0, 0.0], [-pitch_sin, 0.0, pitch_cos]]
    about_x = [[1.0, 0.0, 0.0], [0.0, roll_cos, -roll_sin], [0.0, roll_sin, roll_cos]]
    return product3(product3(about_z, about_y), about_x)


def quaternion_matrix(q0, q1, q2, q3):
    scale = 1.0 / jnp.sqrt(q0 * q0 + q1 * q1 + q2 * q2 + q3 * q3)
    w, x, y, z = (q0 * scale, q1 * scale, q2 * scale, q3 * scale)
    return [
        [1 - 2 * (y * y + z * z), 2 * (x * y - w * z), 2 * (x * z + w * y)],
        [2 * (x * y + w * z), 1 - 2 * (x * x + z * z), 2 * (y * z - w * x)],
        [2 * (x * z - w * y), 2 * (y * z + w * x), 1 - 2 * (x * x + y * y)],
    ]


def harmonics(x, y, z):
    xx, yy, zz = (x * x, y * y, z * z)
    return [
        SH_C0 + 0.0 * x,
        -SH_C1 * y,
        SH_C1 * z,
        -SH_C1 * x,
        SH_C2[0] * x * y,
        SH_C2[1] * y * z,
        SH_C2[2] * (2 * zz - xx - yy),
        SH_C2[3] * x * z,
        SH_C2[4] * (xx - yy),
        SH_C3[0] * y * (3 * xx - yy),
        SH_C3[1] * x * y * z,
        SH_C3[2] * y * (4 * zz - xx - yy),
        SH_C3[3] * z * (2 * zz - 3 * xx - 3 * yy),
        SH_C3[4] * x * (4 * zz - xx - yy),
        SH_C3[5] * z * (xx - yy),
        SH_C3[6] * x * (xx - 3 * yy),
    ]


def project(params, camera, rotation):
    translation = [0.15 * camera[3], 0.15 * camera[4], 6.0]
    position = [params[i] for i in range(3)]
    viewed = [
        sum((rotation[i][j] * position[j] for j in range(3))) + translation[i] for i in range(3)
    ]
    inverse_z = 1.0 / viewed[2]
    row_x = [
        FOCAL * inverse_z * (rotation[0][k] - viewed[0] * inverse_z * rotation[2][k])
        for k in range(3)
    ]
    row_y = [
        FOCAL * inverse_z * (rotation[1][k] - viewed[1] * inverse_z * rotation[2][k])
        for k in range(3)
    ]
    orient = quaternion_matrix(params[6], params[7], params[8], params[9])
    stretch = [jnp.exp(params[3 + k]) for k in range(3)]
    image_x = [sum((row_x[i] * orient[i][k] for i in range(3))) * stretch[k] for k in range(3)]
    image_y = [sum((row_y[i] * orient[i][k] for i in range(3))) * stretch[k] for k in range(3)]
    cov_xx = sum((e * e for e in image_x)) + DILATE
    cov_yy = sum((e * e for e in image_y)) + DILATE
    cov_xy = sum((image_x[k] * image_y[k] for k in range(3)))
    share = 1.0 / (cov_xx * cov_yy - cov_xy * cov_xy)
    opacity = 1.0 / (1.0 + jnp.exp(-params[10]))
    toward = [
        position[k] + sum((rotation[i][k] * translation[i] for i in range(3))) for k in range(3)
    ]
    closeness = 1.0 / jnp.sqrt(sum((e * e for e in toward)))
    harmonic = harmonics(*[e * closeness for e in toward])
    colour = [
        jnp.exp(sum((harmonic[l] * params[11 + 3 * l + c] for l in range(16)))) for c in range(3)
    ]
    return [
        FOCAL * viewed[0] * inverse_z,
        FOCAL * viewed[1] * inverse_z,
        cov_yy * share,
        -cov_xy * share,
        cov_xx * share,
        opacity,
    ] + colour


def iota(shape, axis):
    return lax.broadcasted_iota(I32, shape, axis)


def lane_gather(values, index):
    return jnp.take_along_axis(values, index, axis=1, mode="promise_in_bounds")


def parts(values):
    top = values.astype(BF16)
    return top, (values - top.astype(F32)).astype(BF16)


def dot(left, right):
    return jnp.dot(left, right, preferred_element_type=F32)


def dot_nt(left, right):
    return lax.dot_general(left, right, (((1,), (1,)), ((), ())), preferred_element_type=F32)


def spread_rows(gauss_ref, wide_ref):
    def one(h, carry):
        lanes = pl.ds(pl.multiple_of(h * COLS, COLS), COLS)
        for first in range(0, FEAT, 8):
            count = min(8, FEAT - first)
            wide_ref[pl.ds(first * HIGH + h, count, stride=HIGH), :] = gauss_ref[first : first + count, lanes]
        return carry

    lax.fori_loop(0, HIGH, one, 0)


def window_band():
    distance = iota((COLS, COLS), 0) - iota((COLS, COLS), 1)
    band = jnp.zeros((COLS, COLS), F32)
    for i in range(11):
        band = jnp.where(distance == i - 5, WINDOW[i], band)
    return band


def band_factors():
    band = window_band()
    top = band.astype(BF16).astype(F32)
    middle = (band - top).astype(BF16).astype(F32)
    low = band - top - middle
    none = jnp.zeros((COLS, COLS), F32)
    left = jnp.concatenate([top, top, top, low], axis=0)
    right = jnp.concatenate([middle, middle, none, none], axis=0)
    return jnp.concatenate([left, right], axis=1).astype(BF16)


def split_three(values, place_ref, rows):
    top = values.astype(BF16)
    rest = values - top.astype(F32)
    middle = rest.astype(BF16)
    place_ref[rows, 0:COLS] = top
    place_ref[rows, COLS : 2 * COLS] = middle
    place_ref[rows, 2 * COLS : 3 * COLS] = (rest - middle.astype(F32)).astype(BF16)
    place_ref[rows, 3 * COLS : 4 * COLS] = top


def along_rows(ref, row):
    def at(i):
        return ref[pl.ds(pl.multiple_of((row + i) * 16, 16), 16), :]

    total = WINDOW[5] * at(0)
    for i in range(1, 6):
        total = total + WINDOW[5 + i] * (at(i) + at(-i))
    return total


def step_kernel(
    n,
    nv,
    gauss_hbm,
    send_hbm,
    list_hbm,
    len_hbm,
    cam_hbm,
    expo_hbm,
    target_hbm,
    wide_grad_ref,
    rad_ref,
    gauss_ref,
    send_ref,
    list_ref,
    len_ref,
    cam_ref,
    expo_ref,
    target_ref,
    wide_ref,
    table_ref,
    pick_ref,
    out_ref,
    recv_ref,
    splat_ref,
    cover_ref,
    weight_ref,
    top_ref,
    low_ref,
    pair_ref,
    deriv_ref,
    tile_rad_ref,
    strips_ref,
    edge_ref,
    t_ref,
    tt_ref,
    p_ref,
    pp_ref,
    pt_ref,
    mt_ref,
    btt_ref,
    gm_ref,
    gpp_ref,
    gpt_ref,
    bm_ref,
    bpp_ref,
    bpt_ref,
    split_ref,
    gimg_ref,
    gtile_ref,
    sgrad_ref,
    slot_one_ref,
    slot_mask_ref,
    own_one_ref,
    own_mask_ref,
    slot_left_ref,
    slot_sum_ref,
    back_ref,
    ret_ref,
    own_left_ref,
    own_sum_ref,
    gall_ref,
    cams_ref,
    turn_ref,
    jac_ref,
    f_send,
    f_recv,
    b_send,
    b_recv,
    t_send,
    t_recv,
    h_send,
    h_recv,
    v_send,
    v_recv,
    c_send,
    c_recv,
    in_sem,
):
    me = lax.axis_index("gs")
    mv = lax.axis_index("view")
    after = lax.rem(me + 1, n)
    before = lax.rem(me + n - 1, n)
    group = min(8, n)
    groups = n // group
    halves = slot_mask_ref.shape[0]

    loads = [
        pltpu.make_async_copy(source, place, in_sem.at[i])
        for i, (source, place) in enumerate(
            [
                (gauss_hbm, gauss_ref),
                (cam_hbm, cam_ref),
                (send_hbm, send_ref),
                (target_hbm, target_ref),
                (list_hbm, list_ref),
                (len_hbm, len_ref),
                (expo_hbm, expo_ref),
            ]
        )
    ]
    for load in loads:
        load.start()

    barrier = pltpu.get_barrier_semaphore()

    def greet(i, carry):
        pl.semaphore_signal(
            barrier, inc=1, device_id={"gs": lax.rem(me + i, n)}, device_id_type=MESH
        )
        return carry

    lax.fori_loop(1, n, greet, 0)
    for i in range(1, nv):
        pl.semaphore_signal(
            barrier, inc=1, device_id={"view": lax.rem(mv + i, nv)}, device_id_type=MESH
        )

    loads[0].wait()
    loads[1].wait()
    spread_rows(gauss_ref, wide_ref)
    camera = [jnp.broadcast_to(cam_ref[0:1, i : i + 1], (8, COLS)) for i in range(5)]
    rotation = camera_rotation(camera)

    def project_rows(i, carry):
        rows = [
            wide_ref[pl.ds(pl.multiple_of(f * HIGH + i * 8, 8), 8), :] for f in range(FEAT)
        ]
        for f, value in enumerate(project(rows, camera, rotation)):
            table_ref[pl.ds(pl.multiple_of(f * HIGH + i * 8, 8), 8), :] = value
        return carry

    lax.fori_loop(0, HIGH // 8, project_rows, 0, unroll=4)
    cams_ref[mv] = jnp.concatenate(
        [camera[i][0:1] for i in range(5)] + [jnp.zeros((3, COLS), F32)], axis=0
    )


    def target_copy(peer, side):
        return pltpu.make_async_remote_copy(
            src_ref=target_ref.at[0],
            dst_ref=edge_ref.at[side],
            send_sem=t_send.at[side],
            recv_sem=t_recv.at[side],
            device_id={"gs": peer},
            device_id_type=MESH,
        )

    def strip_copy(peer, side):
        return pltpu.make_async_remote_copy(
            src_ref=strips_ref.at[1],
            dst_ref=strips_ref.at[2 * side],
            send_sem=h_send.at[side],
            recv_sem=h_recv.at[side],
            device_id={"gs": peer},
            device_id_type=MESH,
        )

    def camera_copy(peer, slot):
        return pltpu.make_async_remote_copy(
            src_ref=cams_ref.at[mv],
            dst_ref=cams_ref.at[slot],
            send_sem=c_send.at[peer],
            recv_sem=c_recv.at[slot],
            device_id={"view": peer},
            device_id_type=MESH,
        )

    def forward_copy(peer, slot):
        return pltpu.make_async_remote_copy(
            src_ref=out_ref.at[peer],
            dst_ref=recv_ref.at[slot],
            send_sem=f_send.at[peer],
            recv_sem=f_recv.at[slot],
            device_id={"gs": peer},
            device_id_type=MESH,
        )

    def back_copy(peer, slot):
        return pltpu.make_async_remote_copy(
            src_ref=back_ref.at[peer],
            dst_ref=ret_ref.at[slot],
            send_sem=b_send.at[peer],
            recv_sem=b_recv.at[slot],
            device_id={"gs": peer},
            device_id_type=MESH,
        )

    my_group = me // group

    def shift_of(step):
        reach = groups // 2 - (step + 1) // 2
        return jnp.where(step % 2 == 1, reach, lax.rem(groups - reach, groups))

    def gather_group(step, carry):
        block = lax.rem(my_group + shift_of(step), groups)
        index = send_ref[0, pl.ds(pl.multiple_of(block * group, group), group), :]
        high = index >> 7
        low = index & 127

        def one(h, totals):
            chosen = high == h
            new = []
            for f in range(SPLAT):
                row = jnp.broadcast_to(table_ref[pl.ds(f * HIGH + h, 1), :], (group, COLS))
                new.append(jnp.where(chosen, lane_gather(row, low), totals[f]))
            return tuple(new)

        totals = lax.fori_loop(
            0, HIGH, one, tuple(jnp.zeros((group, COLS), F32) for _ in range(SPLAT)), unroll=8
        )
        for f in range(SPLAT):
            pick_ref[f * group : (f + 1) * group, :] = totals[f]
        for i in range(group):
            peer = block * group + i
            out_ref[peer] = pick_ref[pl.ds(i, SPLAT, stride=group), :]
        return carry

    def send_group(step, carry):
        block = lax.rem(my_group + shift_of(step), groups)
        for i in range(group):
            peer = block * group + lax.rem(me + i, group)

            @pl.when(peer != me)
            def _():
                forward_copy(peer, me).start()

        return carry

    def gather_and_send(step, carry):
        send_group(step, carry)
        return gather_group(step + ahead, carry)

    for load in loads[2:]:
        load.wait()
    ahead = min(3, groups)
    lax.fori_loop(0, ahead, gather_group, 0)
    pl.semaphore_wait(barrier, n - 1 + nv - 1)
    lax.fori_loop(0, groups - ahead, gather_and_send, 0)
    lax.fori_loop(groups - ahead, groups, send_group, 0)
    recv_ref[me] = out_ref[me]
    @pl.when(me < n - 1)
    def _():
        target_copy(after, 0).start()

    @pl.when(me > 0)
    def _():
        target_copy(before, 1).start()

    for i in range(1, nv):
        camera_copy(lax.rem(mv + i, nv), mv).start()

    def own_factors(r, carry):
        index = send_ref[0, pl.ds(r, 1), :]
        lanes = pl.ds(pl.multiple_of(r * COLS, COLS), COLS)
        own_one_ref[:, lanes] = jnp.where(iota((256, COLS), 0) == (index & 255), 1.0, 0.0).astype(BF16)
        own_mask_ref[:, lanes] = jnp.where(iota((16, COLS), 0) == (index >> 8), 1.0, 0.0).astype(BF16)
        return carry

    lax.fori_loop(0, n, own_factors, 0, unroll=8)

    def slot_factors(j, carry):
        index = list_ref[0, pl.ds(j, 1), :]
        lanes = pl.ds(pl.multiple_of(j * LIST, LIST), LIST)
        slot_one_ref[:, lanes] = jnp.where(iota((256, LIST), 0) == (index & 255), 1.0, 0.0).astype(BF16)
        slot_mask_ref[:, lanes] = jnp.where(iota((halves, LIST), 0) == (index >> 8), 1.0, 0.0).astype(
            BF16
        )
        return carry

    lax.fori_loop(0, TILES, slot_factors, 0, unroll=8)

    owner = [list_ref[0, :, 128 * h : 128 * h + 128] >> 7 for h in range(2)]
    place = [list_ref[0, :, 128 * h : 128 * h + 128] & 127 for h in range(2)]

    def take_group(step, totals):
        block = lax.rem(my_group + groups - shift_of(step), groups)
        for i in range(group):
            sender = block * group + i

            @pl.when(sender != me)
            def _():
                forward_copy(sender, sender).wait_recv()

        for i in range(group):
            sender = block * group + i
            chosen = [owner[h] == sender for h in range(2)]
            new = []
            for f in range(SPLAT):
                row = jnp.broadcast_to(recv_ref[sender, f : f + 1, :], (TILES, COLS))
                for h in range(2):
                    new.append(
                        jnp.where(chosen[h], lane_gather(row, place[h]), totals[2 * f + h])
                    )
            totals = tuple(new)
        return totals

    totals = lax.fori_loop(
        0, groups, take_group, tuple(jnp.zeros((TILES, COLS), F32) for _ in range(2 * SPLAT))
    )
    tile_row = iota((TILES, COLS), 0)
    length = jnp.zeros((TILES, COLS), I32)
    for j in range(TILES):
        length = jnp.where(tile_row == j, len_ref[0:1, j : j + 1], length)
    for f in range(SPLAT):
        for h in range(2):
            splat_ref[f * TILES : (f + 1) * TILES, 128 * h : 128 * h + 128] = totals[2 * f + h]
    for h in range(2):
        active = (iota((TILES, COLS), 1) + 128 * h) < length
        splat_ref[SPLAT * TILES : (SPLAT + 1) * TILES, 128 * h : 128 * h + 128] = jnp.where(
            active, totals[2 * 5 + h], 0.0
        )

    def splat_row(f, j):
        return splat_ref[pl.ds(f * TILES + j, 1), :]

    column_x = iota((ROWS, LIST), 0).astype(F32) + (0.5 - 8.0)
    first_of = iota((LIST, LIST), 0)
    then_of = iota((LIST, LIST), 1)
    earlier = jnp.where(first_of < then_of, 1.0, 0.0).astype(BF16)
    earlier = jnp.concatenate([earlier, earlier], axis=0)
    later = jnp.where(first_of > then_of, 1.0, 0.0).astype(BF16)
    later = jnp.concatenate([later, later], axis=0)

    def pixel_rows(j, y):
        return pl.ds(pl.multiple_of(j * 256 + y * 16, 16), 16)

    def composite(j, carry):
        ox, oy, a, b, c = [splat_row(f, j) for f in range(5)]
        opacity = splat_row(SPLAT, j)
        dx = column_x - ox
        square_part = (-0.5 * LOG2E * a) * dx * dx
        cross_part = (-LOG2E * b) * dx
        for y in range(16):
            dy = (y + 0.5 - 8.0) - oy
            power = square_part + dy * cross_part + (-0.5 * LOG2E * c) * dy * dy
            cover = opacity * jnp.exp2(power)
            cover_ref[pixel_rows(j, y), :] = cover
            top, low = parts(jnp.log(1.0 - cover))
            pair_ref[y * 16 : y * 16 + 16, 0:LIST] = top
            pair_ref[y * 16 : y * 16 + 16, LIST : 2 * LIST] = low
        deriv_ref[...] = dot(pair_ref[...], earlier)
        for y in range(16):
            rows = pixel_rows(j, y)
            cover = cover_ref[rows, :]
            weight = cover * jnp.exp(deriv_ref[y * 16 : y * 16 + 16, :])
            cover_ref[rows, :] = cover / (1.0 - cover)
            weight_ref[rows, :] = weight
            top, low = parts(weight)
            top_ref[rows, :] = top
            low_ref[rows, :] = low
        tile_rows = pl.ds(pl.multiple_of(j * 256, 256), 256)
        colours = jnp.concatenate([splat_row(6 + c, j) for c in range(3)], axis=0)
        colour_top = colours.astype(BF16).astype(F32)
        packed = jnp.concatenate(
            [colour_top, colours - colour_top, jnp.zeros((10, LIST), F32)], axis=0
        ).astype(BF16)
        seen = dot_nt(packed, top_ref[tile_rows, :]) + dot_nt(packed, low_ref[tile_rows, :])
        for c in range(3):
            tile_rad_ref[pl.ds(c * TILES + j, 1), :] = seen[c : c + 1] + seen[c + 3 : c + 4]
        return carry

    lax.fori_loop(0, TILES, composite, 0, unroll=8)

    lane = iota((TILES, COLS), 1)
    in_tile = (lane >> 4) == tile_row
    for y in range(16):
        index = (lane & 15) + 16 * (y % 8)
        for c in range(3):
            half = 128 * (y // 8)
            source = tile_rad_ref[c * TILES : (c + 1) * TILES, half : half + 128]
            line = jnp.sum(jnp.where(in_tile, lane_gather(source, index), 0.0), axis=0, keepdims=True)
            strips_ref[1, c, y : y + 1, :] = line

    @pl.when(me < n - 1)
    def _():
        strip_copy(after, 0).start()

    @pl.when(me > 0)
    def _():
        strip_copy(before, 1).start()

    @pl.when(me == 0)
    def _():
        edge_ref[0] = jnp.zeros((CHANNELS, ROWS, COLS), F32)
        strips_ref[0] = jnp.zeros((3, ROWS, COLS), F32)

    @pl.when(me == n - 1)
    def _():
        edge_ref[1] = jnp.zeros((CHANNELS, ROWS, COLS), F32)
        strips_ref[2] = jnp.zeros((3, ROWS, COLS), F32)

    @pl.when(me > 0)
    def _():
        target_copy(before, 0).wait_recv()

    @pl.when(me < n - 1)
    def _():
        target_copy(after, 1).wait_recv()

    for strip in range(3):
        for ch in range(16):
            if ch == CHANNELS:
                value = jnp.zeros((ROWS, COLS), F32)
            elif strip == 1:
                value = target_ref[0, ch]
            else:
                value = edge_ref[strip // 2, ch]
            t_ref[pl.ds(strip * 256 + ch, ROWS, stride=16), :] = value

    band = band_factors()

    def square_target(row, carry):
        rows = pl.ds(pl.multiple_of(row * 16, 16), 16)
        tt_ref[rows, :] = t_ref[rows, :] * t_ref[rows, :]
        return carry

    lax.fori_loop(FIRST - 5, FIRST + MAPS + 5, square_target, 0, unroll=4)

    def target_maps(i, carry):
        rows = pl.ds(pl.multiple_of(i * 16, 16), 16)
        second = pl.ds(pl.multiple_of((MAPS + i) * 16, 16), 16)
        split_three(along_rows(t_ref, FIRST + i), split_ref, rows)
        split_three(along_rows(tt_ref, FIRST + i), split_ref, second)
        return carry

    lax.fori_loop(0, MAPS, target_maps, 0, unroll=MAPS)
    count = MAPS * 16
    for k, maps in enumerate((mt_ref, btt_ref)):
        both = dot(split_ref[k * count : (k + 1) * count, :], band)
        maps[...] = both[:, 0:COLS] + both[:, COLS:]

    rad_ref[0] = strips_ref[1]

    channel = iota((16, COLS), 0)
    of_colour = [lax.rem(channel, 3) == c for c in range(3)]
    bracket = channel // 3
    exposure = jnp.zeros((16, COLS), F32)
    for b in range(5):
        exposure = jnp.where(bracket == b, expo_ref[0:1, b : b + 1], exposure)

    def tone(row, carry):
        strip = row // ROWS
        y = lax.rem(row, ROWS)
        lines = [strips_ref[strip, c, pl.ds(y, 1), :] for c in range(3)]
        scaled = exposure * jnp.where(
            of_colour[0], lines[0], jnp.where(of_colour[1], lines[1], lines[2])
        )
        mapped = scaled / (1.0 + scaled)
        rows = pl.ds(pl.multiple_of(row * 16, 16), 16)
        p_ref[rows, :] = mapped
        pp_ref[rows, :] = mapped * mapped
        pt_ref[rows, :] = mapped * t_ref[rows, :]
        return carry

    lax.fori_loop(ROWS, 2 * ROWS, tone, 0, unroll=ROWS)

    @pl.when(me > 0)
    def _():
        strip_copy(before, 0).wait_recv()

    @pl.when(me < n - 1)
    def _():
        strip_copy(after, 1).wait_recv()

    lax.fori_loop(FIRST - 5, ROWS, tone, 0, unroll=10)
    lax.fori_loop(2 * ROWS, FIRST + MAPS + 5, tone, 0, unroll=10)

    def filter_rows(i, carry):
        rows = pl.ds(pl.multiple_of(i * 16, 16), 16)
        second = pl.ds(pl.multiple_of((MAPS + i) * 16, 16), 16)
        third = pl.ds(pl.multiple_of((2 * MAPS + i) * 16, 16), 16)
        split_three(along_rows(p_ref, FIRST + i), split_ref, rows)
        split_three(along_rows(pp_ref, FIRST + i), split_ref, second)
        split_three(along_rows(pt_ref, FIRST + i), split_ref, third)
        return carry

    lax.fori_loop(0, MAPS, filter_rows, 0, unroll=MAPS)
    for k, maps in enumerate((gm_ref, gpp_ref, gpt_ref)):
        both = dot(split_ref[k * count : (k + 1) * count, :], band)
        maps[...] = both[:, 0:COLS] + both[:, COLS:]

    def similarity_row(i, carry):
        row = FIRST + i
        rows = pl.ds(pl.multiple_of(i * 16, 16), 16)
        mean_p = gm_ref[rows, :]
        square_p = gpp_ref[rows, :]
        cross = gpt_ref[rows, :]
        mean_t = mt_ref[rows, :]
        both = mean_p * mean_t
        n1 = 2.0 * both + FLOOR_MEAN
        n2 = 2.0 * (cross - both) + FLOOR_VAR
        d1 = mean_p * mean_p + mean_t * mean_t + FLOOR_MEAN
        d2 = (square_p - mean_p * mean_p) + (btt_ref[rows, :] - mean_t * mean_t) + FLOOR_VAR
        inside = ((row >= ROWS) | (me > 0)) & ((row < 2 * ROWS) | (me < n - 1))
        share = jnp.where(inside, 1.0, 0.0) / (d1 * d2)
        similar = n1 * n2 * share
        gpt_ref[rows, :] = -2.0 * n1 * share
        by_d2 = similar / d2
        gpp_ref[rows, :] = by_d2
        gm_ref[rows, :] = 2.0 * (
            mean_t * (n1 - n2) * share + mean_p * (similar / d1 - by_d2)
        )
        return carry

    lax.fori_loop(0, MAPS, similarity_row, 0, unroll=26)

    def filter_back(y, carry):
        for k, source in enumerate((gm_ref, gpp_ref, gpt_ref)):
            rows = pl.ds(pl.multiple_of((k * ROWS + y) * 16, 16), 16)
            split_three(along_rows(source, y + 5), split_ref, rows)
        return carry

    lax.fori_loop(0, ROWS, filter_back, 0, unroll=ROWS)
    for k, maps in enumerate((bm_ref, bpp_ref, bpt_ref)):
        both = dot(split_ref[k * ROWS * 16 : (k + 1) * ROWS * 16, :], band)
        maps[...] = both[:, 0:COLS] + both[:, COLS:]

    def radiance_row(y, carry):
        own = pl.ds(pl.multiple_of((y + ROWS) * 16, 16), 16)
        mapped = p_ref[own, :]
        wanted = t_ref[own, :]
        rows = pl.ds(pl.multiple_of(y * 16, 16), 16)
        slope = bm_ref[rows, :] + 2.0 * mapped * bpp_ref[rows, :] + wanted * bpt_ref[rows, :]
        slope = slope + 1.6 * (mapped - wanted)
        rest = 1.0 - mapped
        slope = slope * exposure * (rest * rest)
        for c in range(3):
            line = jnp.sum(jnp.where(of_colour[c], slope, 0.0), axis=0, keepdims=True)
            gimg_ref[pl.ds(c * ROWS + y, 1), :] = line
        return carry

    lax.fori_loop(0, ROWS, radiance_row, 0, unroll=16)

    spread_index = 16 * tile_row + (lane & 15)
    for c in range(3):
        for half in range(2):
            total = jnp.zeros((TILES, COLS), F32)
            for y in range(8):
                row = c * ROWS + half * 8 + y
                source = jnp.broadcast_to(gimg_ref[row : row + 1, :], (TILES, COLS))
                total = jnp.where((lane >> 4) == y, lane_gather(source, spread_index), total)
            gtile_ref[c * TILES : (c + 1) * TILES, 128 * half : 128 * half + 128] = total

    def composite_back(j, carry):
        ox, oy, a, b, c_ = [splat_row(f, j) for f in range(5)]
        colours = jnp.concatenate([splat_row(6 + c, j) for c in range(3)], axis=0)
        colour_top = colours.astype(BF16).astype(F32)
        slopes = jnp.concatenate(
            [gtile_ref[pl.ds(c * TILES + j, 1), :] for c in range(3)], axis=0
        )
        slope_top = slopes.astype(BF16).astype(F32)
        left = jnp.concatenate(
            [slope_top, slopes - slope_top, slope_top, jnp.zeros((7, LIST), F32)], axis=0
        )
        right = jnp.concatenate(
            [colour_top, colour_top, colours - colour_top, jnp.zeros((7, LIST), F32)], axis=0
        )
        deriv_ref[...] = dot(left.T.astype(BF16), right.astype(BF16))
        for y in range(16):
            rows = pixel_rows(j, y)
            value = deriv_ref[y * 16 : y * 16 + 16, :] * weight_ref[rows, :]
            weight_ref[rows, :] = value
            top, low = parts(value)
            pair_ref[y * 16 : y * 16 + 16, 0:LIST] = top
            pair_ref[y * 16 : y * 16 + 16, LIST : 2 * LIST] = low
        deriv_ref[...] = dot(pair_ref[...], later)
        dx = column_x - ox
        dxx = dx * dx
        zero = jnp.zeros((ROWS, LIST), F32)
        m0, mx, mxx = zero, zero, zero
        my, mxy, myy = zero, zero, zero
        for y in range(16):
            rows = pixel_rows(j, y)
            dy = (y + 0.5 - 8.0) - oy
            q = weight_ref[rows, :] - deriv_ref[y * 16 : y * 16 + 16, :] * cover_ref[rows, :]
            qx = q * dx
            qy = q * dy
            m0 = m0 + q
            mx = mx + qx
            my = my + qy
            mxx = mxx + q * dxx
            mxy = mxy + qx * dy
            myy = myy + qy * dy
        m0, mx, my, mxx, mxy, myy = [
            jnp.sum(m, axis=0, keepdims=True) for m in (m0, mx, my, mxx, mxy, myy)
        ]
        tile_rows = pl.ds(pl.multiple_of(j * 256, 256), 256)
        packed = left.astype(BF16)
        by_colour = dot(packed, top_ref[tile_rows, :]) + dot(packed, low_ref[tile_rows, :])
        rows = [
            a * mx + b * my,
            b * mx + c_ * my,
            -0.5 * mxx,
            -mxy,
            -0.5 * myy,
            m0 / splat_row(5, j),
        ] + [by_colour[c : c + 1] + by_colour[c + 3 : c + 4] for c in range(3)]
        lanes = pl.ds(pl.multiple_of(j * LIST, LIST), LIST)
        mask = slot_mask_ref[:, lanes]
        for f in range(SPLAT):
            top = rows[f].astype(BF16).astype(F32)
            for k, part in enumerate((top, rows[f] - top)):
                at = (k * SPLAT + f) * halves
                slot_left_ref[at : at + halves, :] = (
                    jnp.broadcast_to(part, (halves, LIST)).astype(BF16) * mask
                )
        update = dot_nt(slot_left_ref[...], slot_one_ref[:, lanes])

        @pl.when(j == 0)
        def _():
            slot_sum_ref[...] = update

        @pl.when(j > 0)
        def _():
            slot_sum_ref[...] = slot_sum_ref[...] + update

        return carry

    lax.fori_loop(0, TILES, composite_back, 0, unroll=8)

    count = SPLAT * halves
    for side in range(2):
        lanes = slice(side * COLS, side * COLS + COLS)
        sgrad_ref[side * count : (side + 1) * count, :] = (
            slot_sum_ref[0:count, lanes] + slot_sum_ref[count : 2 * count, lanes]
        )

    def send_back(step, carry):
        block = lax.rem(my_group + shift_of(step), groups)
        for i in range(group):
            peer = block * group + i
            first = (i % 2) * count + block * (group // 2) + i // 2
            back_ref[peer] = sgrad_ref[pl.ds(first, SPLAT, stride=halves), :]
        for i in range(group):
            peer = block * group + lax.rem(me + i, group)

            @pl.when(peer != me)
            def _():
                back_copy(peer, me).start()

        return carry

    lax.fori_loop(0, groups, send_back, 0)
    ret_ref[me] = back_ref[me]

    for i in range(1, nv):
        peer = lax.rem(mv + i, nv)
        camera_copy(peer, peer).wait_recv()
    for v in range(nv):
        angles = [jnp.broadcast_to(cams_ref[v, i : i + 1, :], (8, COLS)) for i in range(5)]
        turn = camera_rotation(angles)
        shift = [0.15 * angles[3], 0.15 * angles[4], 6.0]
        flat = [jnp.broadcast_to(turn[i][k], (8, COLS)) for i in range(3) for k in range(3)]
        flat += [sum((turn[i][k] * shift[i] for i in range(3))) for k in range(3)]
        for k in range(12):
            turn_ref[v, 8 * k : 8 * k + 8, :] = flat[k]

    def chunk_rows(f, i):
        return pl.ds(pl.multiple_of(f * HIGH + i * 8, 8), 8)

    def turn_of(v):
        flat = [turn_ref[v, 8 * k : 8 * k + 8, :] for k in range(12)]
        return [flat[0:3], flat[3:6], flat[6:9]], flat[9:12]

    def prepare(i, carry):
        position = [wide_ref[chunk_rows(f, i), :] for f in range(3)]
        stretch = [jnp.exp(wide_ref[chunk_rows(3 + k, i), :]) for k in range(3)]
        orient = quaternion_matrix(*[wide_ref[chunk_rows(6 + k, i), :] for k in range(4)])
        for v in range(nv):
            turn, away = turn_of(v)
            shift = [
                0.15 * jnp.broadcast_to(cams_ref[v, 3:4, :], (8, COLS)),
                0.15 * jnp.broadcast_to(cams_ref[v, 4:5, :], (8, COLS)),
                6.0,
            ]
            viewed = [
                sum((turn[r][k] * position[k] for k in range(3))) + shift[r] for r in range(3)
            ]
            inverse_z = 1.0 / viewed[2]
            slant_x = viewed[0] * inverse_z
            slant_y = viewed[1] * inverse_z
            focal_z = FOCAL * inverse_z
            row_x = [focal_z * (turn[0][k] - slant_x * turn[2][k]) for k in range(3)]
            row_y = [focal_z * (turn[1][k] - slant_y * turn[2][k]) for k in range(3)]
            image_x = [
                sum((row_x[r] * orient[r][k] for r in range(3))) * stretch[k] for k in range(3)
            ]
            image_y = [
                sum((row_y[r] * orient[r][k] for r in range(3))) * stretch[k] for k in range(3)
            ]
            cov_xx = sum((e * e for e in image_x)) + DILATE
            cov_yy = sum((e * e for e in image_y)) + DILATE
            cov_xy = sum((image_x[k] * image_y[k] for k in range(3)))
            share = 1.0 / (cov_xx * cov_yy - cov_xy * cov_xy)
            toward = [position[k] + away[k] for k in range(3)]
            closeness = 1.0 / jnp.sqrt(sum((e * e for e in toward)))
            direction = [e * closeness for e in toward]
            harmonic, pull = jax.vjp(harmonics, *direction)
            colours, moves = [], []
            for c in range(3):
                factors = [wide_ref[chunk_rows(11 + 3 * l + c, i), :] for l in range(16)]
                colour = jnp.exp(sum((harmonic[l] * factors[l] for l in range(16))))
                slope = pull(factors)
                along = sum((direction[k] * slope[k] for k in range(3)))
                reach = closeness * colour
                colours.append(colour)
                moves += [(slope[k] - direction[k] * along) * reach for k in range(3)]
            kept = (
                harmonic[1:]
                + colours
                + moves
                + [cov_yy * share, -cov_xy * share, cov_xx * share]
                + image_x
                + image_y
                + row_x
                + row_y
                + [inverse_z, slant_x, slant_y]
            )
            for k in range(JAC):
                jac_ref[v, chunk_rows(k, i), :] = kept[k]
        return carry

    lax.fori_loop(0, HIGH // 8, prepare, 0)

    own_sum_ref[...] = jnp.zeros_like(own_sum_ref)

    def add_group(step, carry):
        block = lax.rem(my_group + groups - shift_of(step), groups)
        for i in range(group):
            sender = block * group + i

            @pl.when(sender != me)
            def _():
                back_copy(sender, sender).wait_recv()

        for i in range(group):
            sender = block * group + i
            mask = own_mask_ref[:, pl.ds(pl.multiple_of(sender * COLS, COLS), COLS)]
            message = ret_ref[sender]
            top = message.astype(BF16).astype(F32)
            for k, part in enumerate((top, message - top)):
                for f in range(SPLAT):
                    at = (k * SPLAT + f) * 16
                    own_left_ref[at : at + 16, i * COLS : (i + 1) * COLS] = (
                        jnp.broadcast_to(part[f : f + 1], (16, COLS)).astype(BF16) * mask
                    )
        lanes = pl.ds(pl.multiple_of(block * group * COLS, COLS), group * COLS)
        own_sum_ref[...] = own_sum_ref[...] + dot_nt(own_left_ref[...], own_one_ref[:, lanes])
        return carry

    lax.fori_loop(0, groups, add_group, 0)
    for f in range(SPLAT):
        for side in range(2):
            lanes = slice(side * COLS, side * COLS + COLS)
            low = (SPLAT + f) * 16
            gall_ref[mv, pl.ds(f * HIGH + side, 16, stride=2), :] = (
                own_sum_ref[f * 16 : f * 16 + 16, lanes] + own_sum_ref[low : low + 16, lanes]
            )

    up = lax.rem(mv + 1, nv)
    down = lax.rem(mv + nv - 1, nv)
    half = SPLAT * HIGH // 2
    lower, upper = pl.ds(0, half), pl.ds(half, half)

    def view_copy(slot, rows, peer, k):
        return pltpu.make_async_remote_copy(
            src_ref=gall_ref.at[slot, rows],
            dst_ref=gall_ref.at[slot, rows],
            send_sem=v_send.at[k],
            recv_sem=v_recv.at[k],
            device_id={"view": peer},
            device_id_type=MESH,
        )

    sent = [view_copy(mv, lower, up, 0), view_copy(mv, upper, down, 1)]
    if nv > 2:
        sent += [view_copy(mv, upper, up, 2), view_copy(mv, lower, down, 3)]
    for copy in sent:
        copy.start()
    def drain(i, carry):
        peer = lax.rem(me + i, n)
        forward_copy(peer, me).wait_send()
        back_copy(peer, me).wait_send()
        return carry

    lax.fori_loop(1, n, drain, 0)

    @pl.when(me < n - 1)
    def _():
        target_copy(after, 0).wait_send()
        strip_copy(after, 0).wait_send()

    @pl.when(me > 0)
    def _():
        target_copy(before, 1).wait_send()
        strip_copy(before, 1).wait_send()

    if nv > 2:
        view_copy(down, lower, up, 0).wait_recv()
        sent.append(view_copy(down, lower, up, 4))
        sent[-1].start()
        view_copy(up, upper, down, 1).wait_recv()
        sent.append(view_copy(up, upper, down, 5))
        sent[-1].start()
        view_copy(down, upper, up, 2).wait_recv()
        view_copy(up, lower, down, 3).wait_recv()
        far = lax.rem(mv + 2, nv)
        view_copy(far, lower, up, 4).wait_recv()
        view_copy(far, upper, down, 5).wait_recv()
    else:
        view_copy(down, lower, up, 0).wait_recv()
        view_copy(up, upper, down, 1).wait_recv()

    def pull_back(i, carry):
        stretch = [jnp.exp(wide_ref[chunk_rows(3 + k, i), :]) for k in range(3)]
        quaternion = [wide_ref[chunk_rows(6 + k, i), :] for k in range(4)]
        orient, pull = jax.vjp(quaternion_matrix, *quaternion)
        opacity = 1.0 / (1.0 + jnp.exp(-wide_ref[chunk_rows(10, i), :]))
        by_position, by_scale, by_orient, by_opacity = [0.0] * 3, [0.0] * 3, [[0.0] * 3] * 3, 0.0
        by_colour = []
        for v in range(nv):
            slope = [gall_ref[v, chunk_rows(f, i), :] for f in range(SPLAT)]

            def kept(k):
                return jac_ref[v, chunk_rows(k, i), :]

            turn, _ = turn_of(v)
            a, b, c = [kept(27 + k) for k in range(3)]
            image_x = [kept(30 + k) for k in range(3)]
            image_y = [kept(33 + k) for k in range(3)]
            row_x = [kept(36 + k) for k in range(3)]
            row_y = [kept(39 + k) for k in range(3)]
            inverse_z, slant_x, slant_y = [kept(42 + k) for k in range(3)]
            ab, bb, bc = a * b, b * b, b * c
            by_xx = -(a * a * slope[2] + ab * slope[3] + bb * slope[4])
            by_yy = -(bb * slope[2] + bc * slope[3] + c * c * slope[4])
            by_xy = -(2 * ab * slope[2] + (bb + a * c) * slope[3] + 2 * bc * slope[4])
            by_x = [2 * by_xx * image_x[k] + by_xy * image_y[k] for k in range(3)]
            by_y = [2 * by_yy * image_y[k] + by_xy * image_x[k] for k in range(3)]
            by_scale = [
                by_scale[k] + by_x[k] * image_x[k] + by_y[k] * image_y[k] for k in range(3)
            ]
            by_x = [by_x[k] * stretch[k] for k in range(3)]
            by_y = [by_y[k] * stretch[k] for k in range(3)]
            by_orient = [
                [by_orient[r][k] + row_x[r] * by_x[k] + row_y[r] * by_y[k] for k in range(3)]
                for r in range(3)
            ]
            by_row_x = [sum((orient[r][k] * by_x[k] for k in range(3))) for r in range(3)]
            by_row_y = [sum((orient[r][k] * by_y[k] for k in range(3))) for r in range(3)]
            pulled = sum((by_row_x[r] * row_x[r] + by_row_y[r] * row_y[r] for r in range(3)))
            depth_x = sum((by_row_x[r] * turn[2][r] for r in range(3)))
            depth_y = sum((by_row_y[r] * turn[2][r] for r in range(3)))
            by_slant_x = FOCAL * (slope[0] - inverse_z * depth_x)
            by_slant_y = FOCAL * (slope[1] - inverse_z * depth_y)
            by_viewed = [
                by_slant_x * inverse_z,
                by_slant_y * inverse_z,
                -inverse_z * (pulled + by_slant_x * slant_x + by_slant_y * slant_y),
            ]
            by_position = [
                by_position[k]
                + sum((turn[r][k] * by_viewed[r] for r in range(3)))
                + sum((slope[6 + c_] * kept(18 + 3 * c_ + k) for c_ in range(3)))
                for k in range(3)
            ]
            by_opacity = by_opacity + slope[5]
            by_colour.append([slope[6 + c_] * kept(15 + c_) for c_ in range(3)])
        by_quaternion = pull(by_orient)
        grads = (
            by_position + by_scale + list(by_quaternion) + [by_opacity * opacity * (1.0 - opacity)]
        )
        for f in range(11):
            wide_grad_ref[chunk_rows(f, i), :] = grads[f]
        for l in range(16):
            for c_ in range(3):
                if l == 0:
                    total = SH_C0 * sum((by_colour[v][c_] for v in range(nv)))
                else:
                    total = sum(
                        (by_colour[v][c_] * jac_ref[v, chunk_rows(l - 1, i), :] for v in range(nv))
                    )
                wide_grad_ref[chunk_rows(11 + 3 * l + c_, i), :] = total
        return carry

    lax.fori_loop(0, HIGH // 8, pull_back, 0)

    for copy in sent:
        copy.wait_send()
    for i in range(1, nv):
        camera_copy(lax.rem(mv + i, nv), mv).wait_send()


def row_order_kernel(wide_hbm, rad_hbm, grad_hbm, radiance_hbm, grad_ref, wide_ref, sems, out_sems):
    groups = [(first, min(8, FEAT - first)) for first in range(0, FEAT, 8)]
    loads = [pltpu.make_async_copy(rad_hbm, radiance_hbm, sems.at[len(groups)])]
    stores = []
    for g, (first, size) in enumerate(groups):
        rows = pl.ds(first * HIGH, size * HIGH)
        loads.append(pltpu.make_async_copy(wide_hbm.at[rows], wide_ref.at[rows], sems.at[g]))
    for load in loads:
        load.start()
    for g, (first, size) in enumerate(groups):
        loads[g + 1].wait()
        for h in range(HIGH):
            grad_ref[first : first + size, h * COLS : (h + 1) * COLS] = wide_ref[
                pl.ds(first * HIGH + h, size, stride=HIGH), :
            ]
        rows = pl.ds(first, size)
        stores.append(pltpu.make_async_copy(grad_ref.at[rows], grad_hbm.at[rows], out_sems.at[g]))
        stores[-1].start()
    for copy in stores + loads[:1]:
        copy.wait()


def shards(n, nv, gaussians, send_index, tile_list, tile_length, camera, exposure, target):
    vmem = pl.BlockSpec(memory_space=pltpu.VMEM)
    halves = max(16, n // 2)
    group = min(8, n)

    def scratch(shape, dtype=F32):
        return pltpu.VMEM(shape, dtype)

    pixels = TILES * 256
    scratches = [
        scratch((FEAT, HIGH * COLS)),
        scratch((1, n, COLS), I32),
        scratch((1, TILES, LIST), I32),
        scratch((1, TILES), I32),
        scratch((1, 5)),
        scratch((1, 5)),
        scratch((1, CHANNELS, ROWS, COLS)),
        scratch((64 * HIGH, COLS)),
        scratch((SPLAT * HIGH, COLS)),
        scratch((SPLAT * group, COLS)),
        scratch((n, SPLAT, COLS)),
        scratch((n, SPLAT, COLS)),
        scratch(((SPLAT + 1) * TILES, LIST)),
        scratch((pixels, LIST)),
        scratch((pixels, LIST)),
        scratch((pixels, LIST), BF16),
        scratch((pixels, LIST), BF16),
        scratch((LIST, 2 * LIST), BF16),
        scratch((LIST, LIST)),
        scratch((3 * TILES, LIST)),
        scratch((3, 3, ROWS, COLS)),
        scratch((2, CHANNELS, ROWS, COLS)),
        scratch((48 * 16, COLS)),
        scratch((48 * 16, COLS)),
        scratch((48 * 16, COLS)),
        scratch((48 * 16, COLS)),
        scratch((48 * 16, COLS)),
        scratch((MAPS * 16, COLS)),
        scratch((MAPS * 16, COLS)),
        scratch((MAPS * 16, COLS)),
        scratch((MAPS * 16, COLS)),
        scratch((MAPS * 16, COLS)),
        scratch((ROWS * 16, COLS)),
        scratch((ROWS * 16, COLS)),
        scratch((ROWS * 16, COLS)),
        scratch((3 * MAPS * 16, 4 * COLS), BF16),
        scratch((3 * ROWS, COLS)),
        scratch((3 * TILES, LIST)),
        scratch((2 * SPLAT * halves, COLS)),
        scratch((256, TILES * LIST), BF16),
        scratch((halves, TILES * LIST), BF16),
        scratch((256, n * COLS), BF16),
        scratch((16, n * COLS), BF16),
        scratch((2 * SPLAT * halves, LIST), BF16),
        scratch((2 * SPLAT * halves, 256)),
        scratch((n, SPLAT, COLS)),
        scratch((n, SPLAT, COLS)),
        scratch((2 * SPLAT * 16, group * COLS), BF16),
        scratch((2 * SPLAT * 16, 256)),
        scratch((nv, SPLAT * HIGH, COLS)),
        scratch((nv, 8, COLS)),
        scratch((nv, 12 * 8, COLS)),
        scratch((nv, JAC * HIGH, COLS)),
    ]
    sems = [pltpu.SemaphoreType.DMA((k,)) for k in (n, n, n, n, 2, 2, 2, 2, 6, 6, nv, nv, 7)]
    wide_grad, strip = pl.pallas_call(
        functools.partial(step_kernel, n, nv),
        out_shape=(
            jax.ShapeDtypeStruct((FEAT * HIGH, COLS), F32),
            jax.ShapeDtypeStruct((1, 3, ROWS, COLS), F32),
        ),
        in_specs=[pl.BlockSpec(memory_space=pl.ANY)] * 7,
        out_specs=(vmem, vmem),
        scratch_shapes=scratches + sems,
        compiler_params=pltpu.CompilerParams(
            collective_id=0, has_side_effects=True, vmem_limit_bytes=56 * 2**20
        ),
        name="splat_step",
    )(gaussians, send_index, tile_list, tile_length, camera, exposure, target)
    return pl.pallas_call(
        row_order_kernel,
        out_shape=(
            jax.ShapeDtypeStruct((FEAT, HIGH * COLS), F32),
            jax.ShapeDtypeStruct((1, 3, ROWS, COLS), F32),
        ),
        in_specs=[pl.BlockSpec(memory_space=pl.ANY)] * 2,
        out_specs=(pl.BlockSpec(memory_space=pl.ANY),) * 2,
        scratch_shapes=[
            scratch((FEAT, HIGH * COLS)),
            scratch((FEAT * HIGH, COLS)),
            pltpu.SemaphoreType.DMA((9,)),
            pltpu.SemaphoreType.DMA((8,)),
        ],
        name="row_order",
    )(wide_grad, strip)


def solution(mesh):
    placed = (
        P(None, "gs"),
        P("view", "gs", None),
        P("view", "gs", None),
        P("view", "gs"),
        P("view", None),
        P("view", None),
        P("view", None, "gs", None),
    )
    return jax.shard_map(
        functools.partial(shards, mesh.shape["gs"], mesh.shape["view"]),
        mesh=mesh,
        in_specs=placed,
        out_specs=(P(None, "gs"), P("view", None, "gs", None)),
        check_vma=False,
    )
```
